32 devices in a mesh: dp: 16 (over z, x, core), seq: 2 (over y).
Axes of the slice: x: 2, y: 2, z: 4, core: 2. Of those that a mesh axis runs over, the one named last changes fastest.
Arguments:
- tokens: float32 [32, 1024, 256], P('dp', 'seq'), may hold values from -6 to 6
- masked: int32 [32, 1024], P('dp', 'seq'), may hold values from 0 to 1
- lengths: int32 [32], P('dp'), may hold values from 256 to 1024, as said below
- cotangent: float32 [32, 1024, 256], P('dp', 'seq'), may hold values from -6 to 6
- mask_embed: float32 [256], replicated, may hold values from -4 to 4
- query_weight: float32 [256, 256], replicated, may hold values from -0.5 to 0.5
- query_bias: float32 [256], replicated, may hold values from -1.2 to 1.2
- key_weight: float32 [256, 256], replicated, may hold values from -0.5 to 0.5
- value_weight: float32 [256, 256], replicated, may hold values from -0.375 to 0.375
- value_bias: float32 [256], replicated, may hold values from -1.2 to 1.2
- out_weight: float32 [256, 256], replicated, may hold values from -1 to 1
- out_bias: float32 [256], replicated, may hold values from -3 to 3
- gain_one: float32 [256], replicated, may hold values from 0.1 to 1.9
- shift_one: float32 [256], replicated, may hold values from -3 to 3
- expand_weight: float32 [256, 512], replicated, may hold values from -0.375 to 0.375
- expand_bias: float32 [512], replicated, may hold values from -1.2 to 1.2
- reduce_weight: float32 [512, 256], replicated, may hold values from -0.25 to 0.25
- reduce_bias: float32 [256], replicated, may hold values from -3 to 3
- gain_two: float32 [256], replicated, may hold values from 0.1 to 1.9
- shift_two: float32 [256], replicated, may hold values from -3 to 3
Outputs:
- result: float32 [32, 1024, 256], P('dp', 'seq')
- tokens_grad: float32 [32, 1024, 256], P('dp', 'seq')
- mask_embed_grad: float32 [256], replicated
- query_weight_grad: float32 [256, 256], replicated
- query_bias_grad: float32 [256], replicated
- key_weight_grad: float32 [256, 256], replicated
- value_weight_grad: float32 [256, 256], replicated
- value_bias_grad: float32 [256], replicated
- out_weight_grad: float32 [256, 256], replicated
- out_bias_grad: float32 [256], replicated
- gain_one_grad: float32 [256], replicated
- shift_one_grad: float32 [256], replicated
- expand_weight_grad: float32 [256, 512], replicated
- expand_bias_grad: float32 [512], replicated
- reduce_weight_grad: float32 [512, 256], replicated
- reduce_bias_grad: float32 [256], replicated
- gain_two_grad: float32 [256], replicated
- shift_two_grad: float32 [256], replicated
- root_means: float32 [3], replicated
The draws below stay inside these ranges and needn't reach their ends.
Inputs may be any that keep to these rules, and one draw needn't show every extreme that they name: `lengths`: in each group of 2 consecutive cells one cell is valid over all 1024 positions.
All inputs are finite; a program needn't handle non-finite values.
Results may differ from the reference program's by a relative error of at most 0.014.
The reference program's roundings to bfloat16 on the way count: a program that leaves them out, or rounds other values in their place, can miss the bound.
Values may be sent and summed in bfloat16 or wider, within the bound.
No kernel may reach another device: no remote copies, remote signals or barrier semaphores. Data moves between devices by JAX's collectives and lax.ppermute only.
A program may use at most 192 MiB of HBM per device.

```python
import jax
import jax.numpy as jnp
from jax import lax

D = 256
HEADS = 4
HEAD_DIM = 64
FF = 512
CELLS_DEV = 2
LENGTH = 1024
CELLS = 32


def draw_lengths(key, part):
    key = jax.random.fold_in(key, 11)
    length_key, pick_key = jax.random.split(key)
    drawn_lengths = jax.random.randint(length_key, (CELLS,), LENGTH // 4, LENGTH + 1)
    groups = CELLS // CELLS_DEV
    chosen = jax.random.randint(pick_key, (groups,), 0, CELLS_DEV)
    within = jnp.arange(CELLS, dtype=jnp.int32) % CELLS_DEV
    is_full = within == jnp.repeat(chosen, CELLS_DEV)
    return jnp.where(is_full, LENGTH, drawn_lengths).astype(jnp.int32)


def draw_masked(key, part):
    key = jax.random.fold_in(key, 23)
    rate_key, roll_key = jax.random.split(key)
    percent = jax.random.randint(rate_key, (CELLS, 1), 5, 26)
    rolled = jax.random.randint(roll_key, (CELLS, LENGTH), 0, 100)
    return (rolled < percent).astype(jnp.int32)


def level_of(own_key, extent, cuts, smallest, largest):
    loudness = 1.0
    for dim, blocks in cuts:
        draws = jax.random.uniform(jax.random.fold_in(jax.random.fold_in(own_key, 6), dim), (blocks,), jnp.float32, smallest / len(cuts), largest / len(cuts))
        loudness = loudness * jnp.repeat(jnp.exp(draws), extent[dim] // blocks).reshape((-1,) + (1,) * (len(extent) - 1 - dim))
    return loudness


def noise(rng, extent, spread, most, shards=(), kind=jnp.bfloat16):
    array = jax.random.normal(rng, extent, jnp.float32) * spread
    if len(shards) > 0:
        array = level_of(rng, extent, shards, -0.22, 0.18) * array
    return jnp.clip(array, min=-most, max=most).astype(kind)


def setup_inputs(seed: int = 0) -> dict:
    splits = jax.random.split(jax.random.key(seed), 21)
    return {
        "tokens": noise(splits[0], (CELLS, LENGTH, D), 1.0, 6.0, ((0, 16), (1, 2)), jnp.float32),
        "masked": draw_masked(jax.random.fold_in(splits[20], 71), 0),
        "lengths": draw_lengths(jax.random.fold_in(splits[20], 71), 0),
        "cotangent": noise(splits[3], (CELLS, LENGTH, D), 1.0, 6.0, ((0, 16), (1, 2)), jnp.float32),
        "mask_embed": noise(splits[4], (D,), 1.0, 4.0, (), jnp.float32),
        "query_weight": noise(splits[5], (D, D), (D // 2) ** -0.5, 0.5, (), jnp.float32),
        "query_bias": noise(splits[6], (D,), 0.2, 1.2, (), jnp.float32),
        "key_weight": noise(splits[7], (D, D), (D // 2) ** -0.5, 0.5, (), jnp.float32),
        "value_weight": noise(splits[8], (D, D), D ** -0.5, 0.375, (), jnp.float32),
        "value_bias": noise(splits[9], (D,), 0.2, 1.2, (), jnp.float32),
        "out_weight": noise(splits[10], (D, D), (D // 8) ** -0.5, 1.0, (), jnp.float32),
        "out_bias": noise(splits[11], (D,), 0.5, 3.0, (), jnp.float32),
        "gain_one": jnp.clip(1.0 + 0.18 * jax.random.normal(splits[12], (D,), jnp.float32), 0.1, 1.9),
        "shift_one": noise(splits[13], (D,), 0.5, 3.0, (), jnp.float32),
        "expand_weight": noise(splits[14], (D, FF), D ** -0.5, 0.375, (), jnp.float32),
        "expand_bias": noise(splits[15], (FF,), 0.2, 1.2, (), jnp.float32),
        "reduce_weight": noise(splits[16], (FF, D), FF ** -0.5, 0.25, (), jnp.float32),
        "reduce_bias": noise(splits[17], (D,), 0.5, 3.0, (), jnp.float32),
        "gain_two": jnp.clip(1.0 + 0.18 * jax.random.normal(splits[18], (D,), jnp.float32), 0.1, 1.9),
        "shift_two": noise(splits[19], (D,), 0.5, 3.0, (), jnp.float32),
    }


HIGH = lax.Precision.HIGHEST
EPSILON = 1e-05
NEGATIVE = -1e+30

@jax.custom_vjp
def low(v):
    return lax.optimization_barrier(v.astype(jnp.bfloat16)).astype(jnp.float32)

@jax.custom_vjp
def low_back(v):
    return v

def low_keep(v):
    return (low(v), None)

def low_pass(kept, grad):
    return (grad,)

def back_keep(v):
    return (v, None)

def back_low(kept, grad):
    return (low(grad),)
low.defvjp(low_keep, low_pass)
low_back.defvjp(back_keep, back_low)

def layer_norm(matrix, gain_vec, offset_vec):
    row_mean = lax.optimization_barrier(jnp.mean(matrix, axis=-1, keepdims=True))
    centred = matrix - row_mean
    row_var = lax.optimization_barrier(jnp.mean(centred * centred, axis=-1, keepdims=True))
    return centred * lax.rsqrt(row_var + EPSILON) * gain_vec + offset_vec

def gelu_fn(matrix):
    return 0.5 * matrix * (1.0 + lax.erf(matrix * 0.7071067811865476))

def product(left, right):
    return jnp.dot(left, right, precision=HIGH)

def attend(queries, keys, values, usable):
    scores = jnp.einsum('qhe,khe->hqk', queries, keys, precision=HIGH) * HEAD_DIM ** (-0.5)
    scores = low_back(jnp.where(usable[None, None, :], scores, NEGATIVE))
    row_peak = lax.optimization_barrier(jnp.max(scores, axis=-1, keepdims=True))
    log_total = row_peak + jnp.log(lax.optimization_barrier(jnp.sum(jnp.exp(scores - row_peak), axis=-1, keepdims=True)))
    attn_weights = jnp.exp(scores - log_total)
    return jnp.einsum('hqk,khe->qhe', attn_weights, values, precision=HIGH)

def cell_forward(params, cell_tokens, cell_masked, cell_length):
    mask_embed, query_weight, query_bias, key_weight, value_weight, value_bias, out_weight, out_bias, gain_one, shift_one, expand_weight, expand_bias, reduce_weight, reduce_bias, gain_two, shift_two = params
    places = jnp.arange(LENGTH, dtype=jnp.int32)
    usable = places < cell_length
    stream = jnp.where(cell_masked[:, None] == 1, mask_embed[None, :], cell_tokens)
    residual_reduced = low(stream)
    queries = low(low_back(product(residual_reduced, query_weight) + query_bias)).reshape(LENGTH, HEADS, HEAD_DIM)
    keys = low(low_back(product(residual_reduced, key_weight))).reshape(LENGTH, HEADS, HEAD_DIM)
    values = low(low_back(product(residual_reduced, value_weight) + value_bias)).reshape(LENGTH, HEADS, HEAD_DIM)
    attended = jax.checkpoint(attend)(queries, keys, values, usable).reshape(LENGTH, HEADS * HEAD_DIM)
    attn_out = low_back(product(low(low_back(attended)), out_weight) + out_bias)
    normed_one = layer_norm(stream + attn_out, gain_one, shift_one)
    hidden_pre = low_back(product(low(normed_one), expand_weight) + expand_bias)
    branch = low_back(product(low(gelu_fn(hidden_pre)), reduce_weight) + reduce_bias)
    result = layer_norm(normed_one + branch, gain_two, shift_two)
    valid_rows = usable.astype(jnp.float32)[:, None]
    squares = jnp.stack([jnp.sum(stream * stream * valid_rows), jnp.sum(attn_out * attn_out * valid_rows), jnp.sum(branch * branch * valid_rows)])
    return (result, squares)

def forward(tokens, params, masked, lengths):
    rounded = tuple((low(item) if place in (1, 3, 4, 6, 10, 12) else item for place, item in enumerate(params)))

    def per_cell(carried, inputs):
        cell_tokens, cell_masked, cell_length = inputs
        result, squares = cell_forward(rounded, cell_tokens, cell_masked, cell_length)
        return (carried, (result, squares))
    carried, outputs = lax.scan(per_cell, jnp.zeros((), jnp.float32), (tokens, masked, lengths))
    return (outputs[0], lax.optimization_barrier(jnp.sum(outputs[1], axis=0)))

def reference(tokens, masked, lengths, cotangent, mask_embed, query_weight, query_bias, key_weight, value_weight, value_bias, out_weight, out_bias, gain_one, shift_one, expand_weight, expand_bias, reduce_weight, reduce_bias, gain_two, shift_two):
    params = (mask_embed, query_weight, query_bias, key_weight, value_weight, value_bias, out_weight, out_bias, gain_one, shift_one, expand_weight, expand_bias, reduce_weight, reduce_bias, gain_two, shift_two)

    def wrapped(tokens_in, params_in):
        return forward(tokens_in, params_in, masked, lengths)
    result, pullback, square_sums = jax.vjp(wrapped, tokens, params, has_aux=True)
    usable = (jnp.arange(LENGTH, dtype=jnp.int32)[None, :] < lengths[:, None]).astype(jnp.float32)
    tokens_grad, grads = pullback(cotangent * usable[:, :, None])
    count = jnp.sum(lengths.astype(jnp.float32))
    root_means = jnp.sqrt(square_sums / (count * D))
    return (result, tokens_grad, grads[0], grads[1], grads[2], grads[3], grads[4], grads[5], grads[6], grads[7], grads[8], grads[9], grads[10], grads[11], grads[12], grads[13], grads[14], grads[15], root_means)
```

```python
import functools

import jax
import jax.numpy as jnp
from jax import lax
from jax.experimental import pallas as pl
from jax.experimental.pallas import tpu as pltpu
from jax.sharding import PartitionSpec as P

HEADS = 4
HEAD_DIM = 64
SLOT = 128
WIDE = HEADS * SLOT

EPSILON = 1e-05
NEGATIVE = -1e30
INV_ROOT_TWO_PI = 0.3989422804014327
BF = jnp.bfloat16
F32 = jnp.float32
VMEM_LIMIT = 16 * 1024 * 1024
MASK_ROWS = 16


def nn(left, right):
    return lax.dot_general(left, right, (((1,), (0,)), ((), ())), preferred_element_type=F32)


def nt(left, right):
    return lax.dot_general(left, right, (((1,), (1,)), ((), ())), preferred_element_type=F32)


def tn(left, right):
    return lax.dot_general(left, right, (((0,), (0,)), ((), ())), preferred_element_type=F32)


def lane_of(shape):
    return lax.broadcasted_iota(jnp.int32, shape, len(shape) - 1)


def row_of(shape):
    return lax.broadcasted_iota(jnp.int32, shape, len(shape) - 2)


def spread(matrix):
    pieces = []
    for pair in range(HEADS // 2):
        both = matrix[:, pair * SLOT : (pair + 1) * SLOT]
        first = lane_of(both.shape) < HEAD_DIM
        pieces.append(jnp.where(first, both, 0.0))
        pieces.append(jnp.where(first, pltpu.roll(both, HEAD_DIM, 1), 0.0))
    return jnp.concatenate(pieces, axis=1)


def joined(wide):
    pieces = []
    for pair in range(HEADS // 2):
        even = wide[:, 2 * pair * SLOT : (2 * pair + 1) * SLOT]
        odd = wide[:, (2 * pair + 1) * SLOT : (2 * pair + 2) * SLOT]
        pieces.append(jnp.where(lane_of(even.shape) < HEAD_DIM, even, pltpu.roll(odd, HEAD_DIM, 1)))
    return jnp.concatenate(pieces, axis=1)


def spread_rows(matrix):
    gap = jnp.zeros((SLOT - HEAD_DIM, matrix.shape[1]), matrix.dtype)
    pieces = []
    for head in range(HEADS):
        pieces += [matrix[head * HEAD_DIM : (head + 1) * HEAD_DIM], gap]
    return jnp.concatenate(pieces, axis=0)


def head_cols(head):
    return slice(head * SLOT, (head + 1) * SLOT)


def project_keys(x, w_all, bias_v, first_place, length, k_out, v_out):
    raw = nn(x, w_all[:, WIDE : 2 * WIDE])
    shut = lane_of(raw.shape) % SLOT == HEAD_DIM + 2
    shut &= row_of(raw.shape) + first_place >= length
    k_out[...] = jnp.where(shut, NEGATIVE, raw).astype(BF)
    one_row = lane_of((1, WIDE)) % SLOT
    ones_row = jnp.where((one_row == HEAD_DIM) | (one_row == HEAD_DIM + 1), 1.0, 0.0)
    v_out[...] = (nn(x, w_all[:, 2 * WIDE :]) + (spread(bias_v) + ones_row)).astype(BF)


def attend(queries, keys, values, kept):
    scores = nt(queries, keys)
    peak = jnp.max(scores, axis=1, keepdims=True)
    kept[...] = jnp.exp(scores - peak).astype(BF)
    return nn(kept[...], values), jnp.broadcast_to(peak, (peak.shape[0], SLOT))


def kept_rows(head, rows):
    return slice(head * rows, (head + 1) * rows)


def owner_of(distance, ring):
    return lax.rem(lax.axis_index("seq") - distance + ring, ring)


def mask_of(carrier, cell):
    rows = carrier.shape[0] - MASK_ROWS
    count = rows // carrier.shape[1]
    under = carrier[rows:, :].astype(F32)
    first = cell * count
    return jnp.concatenate([under[first + at : first + at + 1] for at in range(count)], axis=1)


def first_kernel(cells, lengths, *refs):
    xs, refs = refs[:cells], refs[cells:]
    wq, wk, wv, bias_q, bias_v, wo, w1, w2 = refs[:8]
    outs, (w_all, w_kv, wo_out, w1_out, w2_out) = refs[8:-5], refs[-5:]
    w_all[:, :WIDE] = spread(wq[...] * HEAD_DIM ** (-0.5)).astype(BF)
    w_all[:, WIDE : 2 * WIDE] = spread(wk[...]).astype(BF)
    w_all[:, 2 * WIDE :] = spread(wv[...]).astype(BF)
    rows = outs[0].shape[0]
    first_place = lax.axis_index("seq") * rows
    one_row = lane_of((1, WIDE)) % SLOT
    bias = spread(bias_q[...]) * HEAD_DIM ** (-0.5) + jnp.where(one_row == HEAD_DIM + 2, 1.0, 0.0)
    for cell in range(cells):
        x = xs[cell].at[:rows]
        q_out, k_out, v_out, kept_out, state_out, peak_out = outs[6 * cell : 6 * cell + 6]
        q_out[...] = (nn(x[...], w_all[:, :WIDE]) + bias).astype(BF)
        project_keys(x[...], w_all, bias_v[...], first_place, lengths[cell], k_out, v_out)
        for head in range(HEADS):
            cols = head_cols(head)
            state_out[:, cols], peak_out[:, cols] = attend(
                q_out[:, cols], k_out[:, cols], v_out[:, cols], kept_out.at[kept_rows(head, rows)]
            )
    width = wk.shape[1]
    w_kv[:, :width] = wk[...].astype(BF)
    w_kv[:, width:] = wv[...].astype(BF)
    wo_out[...] = spread_rows(wo[...].astype(BF))
    w1_out[...] = w1[...].astype(BF)
    w2_out[...] = w2[...].astype(BF)


def more_kernel(
    cell, distance, ring,
    lengths, x, q, state, peak, w_all, bias_v,
    k_out, v_out, kept_out, own_out, state_out, peak_out,
):
    rows = q.shape[0]
    first_place = owner_of(distance, ring) * rows
    project_keys(x[:rows, :], w_all, bias_v[...], first_place, lengths[cell], k_out, v_out)
    for head in range(HEADS):
        cols = head_cols(head)
        total, own = attend(
            q[:, cols], k_out[:, cols], v_out[:, cols], kept_out.at[kept_rows(head, rows)]
        )
        top = jnp.maximum(peak[:, cols], own)
        own_out[:, cols] = own
        peak_out[:, cols] = top
        state_out[:, cols] = state[:, cols] * jnp.exp(peak[:, cols] - top)
        state_out[:, cols] += total * jnp.exp(own - top)


def norm_parts(matrix):
    row_mean = jnp.mean(matrix, axis=1, keepdims=True)
    centred = matrix - row_mean
    row_var = jnp.mean(centred * centred, axis=1, keepdims=True)
    inverse = lax.rsqrt(row_var + EPSILON)
    return centred * inverse, inverse


def norm_back(grad, unit, inverse):
    shift = jnp.mean(grad, axis=1, keepdims=True)
    scale = jnp.mean(grad * unit, axis=1, keepdims=True)
    return (grad - shift - unit * scale) * inverse


def eight_sum(matrix):
    return jnp.sum(matrix.reshape(-1, 8, matrix.shape[1]), axis=0)


def inverse_of(value):
    guess = pl.reciprocal(value, approx=True)
    return guess * (2.0 - value * guess)


def gelu_parts(pre):
    bell = jnp.exp(pre * pre * (-0.5))
    t = inverse_of(1.0 + (0.3275911 * 0.7071067811865476) * jnp.abs(pre))
    poly = 0.5 * 1.061405429
    for factor in (-1.453152027, 1.421413741, -0.284496736, 0.254829592):
        poly = poly * t + 0.5 * factor
    tail = poly * t * bell
    half = jnp.where(pre >= 0.0, 1.0 - tail, tail)
    return pre * half, half + pre * bell * INV_ROOT_TWO_PI


def halve(pack, keep_out, give_out):
    half = keep_out.shape[0]
    core = lax.axis_index("core")
    keep_out[...] = pack[pl.ds(pl.multiple_of(core * half, half), half), :]
    give_out[...] = pack[pl.ds(pl.multiple_of((1 - core) * half, half), half), :]


def my_plane(ring):
    return lax.axis_index("x") * ring + lax.axis_index("seq")


def halve(pack, keep_out, give_out):
    half = keep_out.shape[0]
    core = lax.axis_index("core")
    keep_out[...] = pack[pl.ds(pl.multiple_of(core * half, half), half), :]
    give_out[...] = pack[pl.ds(pl.multiple_of((1 - core) * half, half), half), :]


def near_bits(ring, core):
    bits = [("seq", 1 << i) for i in range(ring.bit_length() - 1)]
    return bits + [("x", 1)] if core else [("x", 1)] + bits


def my_side(ring, step):
    sides = []
    for core in range(2):
        axis, bit = near_bits(ring, core)[step]
        sides.append(lax.rem(lax.axis_index(axis) // bit, 2))
    return jnp.where(lax.axis_index("core") == 0, sides[0], sides[1])


def halve_kernel(ring, step, keep, received, keep_out, give_out):
    half = keep_out.shape[0]
    side = my_side(ring, step)
    for out, place in ((keep_out, side), (give_out, 1 - side)):
        at = pl.ds(pl.multiple_of(place * half, half), half)
        out[...] = (keep[at, :].astype(F32) + received[at, :].astype(F32)).astype(BF)


def join_kernel(ring, step, mine, other, out):
    rows = mine.shape[0]
    side = my_side(ring, step)
    out[pl.ds(pl.multiple_of(side * rows, rows), rows), :] = mine[...]
    out[pl.ds(pl.multiple_of((1 - side) * rows, rows), rows), :] = other[...]


def divide_kernel(ring, keep, received, own_out, *give_outs):
    piece = own_out.shape[0]
    plane = my_plane(ring)
    for step, out in enumerate((own_out,) + give_outs):
        at = pl.ds(pl.multiple_of((plane ^ step) * piece, piece), piece)
        out[...] = (keep[at, :].astype(F32) + received[at, :].astype(F32)).astype(BF)


def place_pieces(ring, mine, other, pack_one, pack_two):
    plane, core = my_plane(ring), lax.axis_index("core")
    for step in range(2 * ring):
        start = 0
        for pack in (pack_one, pack_two):
            piece = pack.shape[0] // (4 * ring)
            for half, sources in ((core, mine), (1 - core, other)):
                at = pl.multiple_of((half * 2 * ring + (plane ^ step)) * piece, piece)
                pack[pl.ds(at, piece), :] = sources[step][start : start + piece, :]
            start += piece


def middle_kernel(
    cell, ring, carry, finish,
    lengths, x, q, state, peak, stream, cotangent, w_all, bias_v, wo, bias_o, gain_one, shift_one,
    w1, bias_1, w2, bias_2, gain_two, shift_two, *refs,
):
    count = ring - 1 if ring > 2 else 0
    before, refs = refs[:count], refs[count:]
    if carry:
        dwo_in, dw1_in, dw2_in, vec_in = refs[:4]
        refs = refs[4:]
    do_outs, refs = refs[:ring], refs[ring:]
    result_out, k_out, v_out, kept_out, first_out, vec_out = refs[:6]
    refs = refs[6:]
    if finish:
        keep_out, give_out = refs[:2]
        refs = refs[2:]
    else:
        dwo_out, dw1_out, dw2_out = refs[:3]
        refs = refs[3:]
    scales, refs = refs[:ring], refs[ring:]
    (
        attended_wide, attended_low, normed_low, active_low, hidden_low, branch_low, attn_low,
        unit_one, inverse_one, narrow_b, wide_b, acc, acc_wide, *pack_ref,
    ) = refs
    rows, width = stream.shape
    hidden = w1.shape[1]
    length = lengths[cell]
    first_place = owner_of(ring - 1, ring) * rows
    project_keys(x[:rows, :], w_all, bias_v[...], first_place, length, k_out, v_out)
    for head in range(HEADS):
        cols = head_cols(head)
        total, own = attend(
            q[:, cols], k_out[:, cols], v_out[:, cols], kept_out.at[kept_rows(head, rows)]
        )
        top = jnp.maximum(peak[:, cols], own)
        old_scale, own_scale = jnp.exp(peak[:, cols] - top), jnp.exp(own - top)
        both = state[:, cols] * old_scale + total * own_scale
        inverse = inverse_of(both[:, HEAD_DIM : HEAD_DIM + 1])
        attended = jnp.where(lane_of(both.shape) < HEAD_DIM, both * inverse, 0.0)
        attended_wide[:, cols] = attended
        attended_low[:, cols] = attended.astype(BF)
        scales[ring - 1][:, cols] = own_scale * inverse
        if ring == 2:
            scales[0][:, cols] = old_scale * inverse
        else:
            for block in range(ring - 1):
                scales[block][:, cols] = jnp.exp(before[block][:, cols] - top) * inverse

    my_place = lax.axis_index("seq") * rows

    valid = jnp.where(row_of((rows, width)) + my_place < length, 1.0, 0.0)

    def add(slot, matrix):
        acc[slot] = eight_sum(matrix)

    attn_out = nn(attended_low[...], wo[...]) + bias_o[...]
    unit, inverse = norm_parts(stream[...] + attn_out)
    unit_one[...] = unit
    inverse_one[...] = jnp.broadcast_to(inverse, (rows, SLOT))
    normed = unit * gain_one[...] + shift_one[...]
    narrow_b[...] = normed
    normed_low[...] = normed.astype(BF)
    add(8, stream[...] * stream[...] * valid)
    add(9, attn_out * attn_out * valid)

    active, slope = gelu_parts(nn(normed_low[...], w1[...]) + bias_1[...])
    active_low[...] = active.astype(BF)
    wide_b[...] = slope

    branch = nn(active_low[...], w2[...]) + bias_2[...]
    unit, inverse = norm_parts(narrow_b[...] + branch)
    result_out[...] = unit * gain_two[...] + shift_two[...]
    grad_result = cotangent[...] * valid
    grad_second = norm_back(grad_result * gain_two[...], unit, inverse)
    narrow_b[...] = grad_second
    branch_bf = grad_second.astype(BF)
    branch_low[...] = branch_bf
    add(0, grad_result * unit)
    add(1, grad_result)
    add(2, branch_bf.astype(F32))
    add(10, branch * branch * valid)
    add(11, valid)

    hidden_bf = (nt(branch_low[...], w2[...]) * wide_b[...]).astype(BF)
    hidden_low[...] = hidden_bf
    acc_wide[...] = eight_sum(hidden_bf.astype(F32))

    grad_normed = narrow_b[...] + nt(hidden_low[...], w1[...])
    unit = unit_one[...]
    grad_first = norm_back(grad_normed * gain_one[...], unit, inverse_one[:, :1])
    first_out[...] = grad_first
    attn_bf = grad_first.astype(BF)
    attn_low[...] = attn_bf
    add(5, grad_normed * unit)
    add(6, grad_normed)
    add(7, attn_bf.astype(F32))

    do_wide = nt(attn_low[...], wo[...]).astype(BF).astype(F32)
    for head in range(HEADS):
        cols = head_cols(head)
        do_head = do_wide[:, cols]
        row_dot = jnp.sum(do_head * attended_wide[:, cols], axis=1, keepdims=True)
        lane = lane_of(do_head.shape)
        for scale, do_out in zip(scales, do_outs):
            factor = scale[:, cols]
            dot = -row_dot * factor
            rest = dot - dot.astype(BF).astype(F32)
            scaled = jnp.where(lane == HEAD_DIM, dot, do_head * factor)
            do_out[:, cols] = jnp.where(lane == HEAD_DIM + 1, rest, scaled).astype(BF)

    hidden_sum = jnp.sum(acc_wide[...], axis=0, keepdims=True)
    sums = [
        hidden_sum[:, (slot - 3) * width : (slot - 2) * width]
        if slot in (3, 4)
        else jnp.sum(acc[slot], axis=0, keepdims=True)
        for slot in range(12)
    ]
    vec = jnp.concatenate(sums + [jnp.zeros((4, width), F32)], axis=0)
    vec_out[...] = vec + vec_in[...] if carry else vec

    dwo = tn(attn_low[...], attended_low[...])
    dw1 = tn(normed_low[...], hidden_low[...])
    dw2 = tn(branch_low[...], active_low[...])
    if carry:
        dwo += dwo_in[...]
        dw1 += dw1_in[...]
        dw2 += dw2_in[...]
    if not finish:
        dwo_out[...] = dwo
        dw1_out[...] = dw1
        dw2_out[...] = dw2
        return
    (pack,) = pack_ref
    pack[:width, :] = joined(dwo).astype(BF)
    pack[width : 2 * width, :] = dw1[:, :width].astype(BF)
    pack[2 * width : 3 * width, :] = dw1[:, width:].astype(BF)
    for at in range(0, hidden, width):
        pack[3 * width + at : 4 * width + at, :] = dw2[:, at : at + width].astype(BF)
    used = 3 * width + hidden
    if pack.shape[0] > used:
        pack[used:, :] = jnp.zeros((pack.shape[0] - used, width), BF)
    halve(pack, keep_out, give_out)


def head_grads(q, k, v, do, kept):
    score_grad = (kept.astype(F32) * nt(do, v)).astype(BF)
    return (
        nn(score_grad, k),
        tn(q[:, :HEAD_DIM], score_grad),
        tn(do[:, :HEAD_DIM], kept),
    )


def all_heads(q, k, v, do, kept, low, put_query):
    rows = q.shape[0]
    for head in range(HEADS):
        cols = head_cols(head)
        dq, dk, dv = head_grads(
            q[:, cols], k[:, cols], v[:, cols], do[:, cols], kept[kept_rows(head, rows), :]
        )
        put_query(cols, dq)
        low[head * HEAD_DIM : (head + 1) * HEAD_DIM, :] = dk.astype(BF)
        at = (HEADS + head) * HEAD_DIM
        low[at : at + HEAD_DIM, :] = dv.astype(BF)


def masked_sum(carrier, cell, grad_bf):
    mask = mask_of(carrier, cell)
    picked = jnp.broadcast_to(mask, (8, mask.shape[1])).astype(BF)
    return nn(picked, grad_bf)[0:1]


def value_sums(low):
    half = low.shape[0] // 2
    sums = jnp.sum(low[half:, :].astype(F32), axis=1, keepdims=True)
    return jnp.broadcast_to(sums, (half, SLOT))


def block_kernel(cell, carry_dq, carry, sent, carrier, q, do, k, v, kept, w_kv, *refs):
    if carry_dq:
        dq_in, refs = refs[0], refs[1:]
    if carry:
        (dw_in, sum_in, vec_in), refs = refs[:3], refs[3:]
    dq_out, dx_out, dw_out, sum_out, vec_out, low = refs

    def put_query(cols, dq):
        dq_out[:, cols] = dq + dq_in[:, cols] if carry_dq else dq

    all_heads(q, k, v, do, kept, low, put_query)
    x = sent[: q.shape[0], :]
    dx_bf = jnp.transpose(nn(w_kv[...], low[...])).astype(BF)
    dx_out[...] = dx_bf
    dw = nn(low[...], x)
    dw_out[...] = dw + dw_in[...] if carry else dw
    sums = value_sums(low)
    sum_out[...] = sums + sum_in[...] if carry else sums
    vec_out[...] = vec_in[...] if carry else jnp.zeros_like(vec_out)
    vec_out[0:1, : x.shape[1]] += masked_sum(carrier[...], cell, dx_bf)


def last_kernel(
    cell, carry, finish,
    sent, carrier, q, do, k, v, kept, w_all, w_kv, first, dq_in, dw_in, sum_in, vec_in, *refs
):
    if carry:
        dwq_in, refs = refs[0], refs[1:]
    if finish:
        vec_mid, dx_out, keep_out, give_out, low_q, low, pack = refs
    else:
        dx_out, dw_out, sum_out, vec_out, dwq_out, low_q, low = refs

    def put_query(cols, dq):
        low_q[:, cols] = ((dq + dq_in[:, cols]) * HEAD_DIM ** (-0.5)).astype(BF)

    all_heads(q, k, v, do, kept, low, put_query)
    grads = first[...] + nt(low_q[...], w_all[:, :WIDE]) * HEAD_DIM**0.5
    grads += jnp.transpose(nn(w_kv[...], low[...]))
    dx_out[...] = grads
    width = grads.shape[1]
    x = sent[: q.shape[0], :]
    dwq = tn(x, low_q[...])
    dw = nn(low[...], x) + dw_in[...]
    sum_q = jnp.sum(low_q[...].astype(F32), axis=0, keepdims=True) + vec_in[1:2, :]
    sum_v = value_sums(low) + sum_in[...]
    sum_mask = masked_sum(carrier[...], cell, grads.astype(BF)) + vec_in[0:1, :width]
    if carry:
        dwq += dwq_in[...]
    if not finish:
        dwq_out[...] = dwq
        dw_out[...] = dw
        sum_out[...] = sum_v
        vec_out[...] = jnp.zeros_like(vec_out)
        vec_out[0:1, :width] = sum_mask
        vec_out[1:2, :] = sum_q
        return
    pack[:width, :] = joined(dwq).astype(BF)
    pack[width : 3 * width, :] = dw.astype(BF)
    rows = jnp.concatenate(
        [
            vec_mid[:12, :],
            joined(sum_q),
            jnp.transpose(sum_v)[0:1, :],
            sum_mask,
            jnp.zeros((1, width), F32),
        ],
        axis=0,
    )
    high = rows.astype(BF)
    pack[3 * width : 3 * width + 16, :] = high
    pack[3 * width + 16 : 3 * width + 32, :] = (rows - high.astype(F32)).astype(BF)
    used = 3 * width + 32
    if pack.shape[0] > used:
        pack[used:, :] = jnp.zeros((pack.shape[0] - used, width), BF)
    halve(pack, keep_out, give_out)


def unpack_kernel(ring, *refs):
    mine, other, refs = refs[: 2 * ring], refs[2 * ring : 4 * ring], refs[4 * ring :]
    dwo_out, dw1_out, dw2_out, dwq_out, dwk_out, dwv_out = refs[:6]
    outs, pack_one, pack = refs[6:-2], refs[-2], refs[-1]
    place_pieces(ring, mine, other, pack_one, pack)
    width = pack.shape[1]
    dwo_out[...] = jnp.transpose(pack_one[:width, :].astype(F32))
    dw1_out[:, :width] = pack_one[width : 2 * width, :].astype(F32)
    dw1_out[:, width:] = pack_one[2 * width : 3 * width, :].astype(F32)
    for at in range(0, dw2_out.shape[0], width):
        dw2_out[at : at + width, :] = jnp.transpose(
            pack_one[3 * width + at : 4 * width + at, :].astype(F32)
        )
    dwq_out[...] = pack[:width, :].astype(F32)
    dwk_out[...] = jnp.transpose(pack[width : 2 * width, :].astype(F32))
    dwv_out[...] = jnp.transpose(pack[2 * width : 3 * width, :].astype(F32))
    vec = pack[3 * width : 3 * width + 16, :].astype(F32)
    vec += pack[3 * width + 16 : 3 * width + 32, :].astype(F32)
    for out, row in zip(outs, (0, 1, 2, (3, 4), 5, 6, 7, 12, 13, 14)):
        if isinstance(row, tuple):
            out[:, :width] = vec[row[0] : row[0] + 1]
            out[:, width:] = vec[row[1] : row[1] + 1]
        else:
            out[...] = vec[row : row + 1]
    squares = jnp.sum(vec[8:16], axis=1, keepdims=True)
    count = vec[11:12, 0:1]
    means = jnp.sqrt(squares / (count * width))
    lane = lane_of((1, 3))
    outs[10][...] = jnp.where(
        lane == 0, means[0:1], jnp.where(lane == 1, means[1:2], means[2:3])
    )


def finish_kernel(cells, carrier, *refs):
    local, received, out = refs[:cells], refs[cells:-1], refs[-1]
    rows, count = local[0].shape[0], len(received) // cells
    for cell in range(cells):
        grads = local[cell][...]
        for piece in received[cell * count : (cell + 1) * count]:
            grads += piece[...].astype(F32)
        mask = jnp.broadcast_to(mask_of(carrier[...], cell), (8, rows))
        out[cell] = jnp.where(jnp.transpose(mask)[:, :1] == 1.0, 0.0, grads)


def call(kernel, ins, outs, scratch=(), flops=0):
    moved = sum(a.size * a.dtype.itemsize for a in ins) + sum(
        s.size * s.dtype.itemsize for s in outs
    )
    vmem = pl.BlockSpec(memory_space=pltpu.VMEM)
    smem = pl.BlockSpec(memory_space=pltpu.SMEM)
    return pl.pallas_call(
        kernel,
        in_specs=[smem if a.ndim == 1 else vmem for a in ins],
        out_specs=[vmem] * len(outs),
        out_shape=outs,
        scratch_shapes=list(scratch),
        compiler_params=pltpu.CompilerParams(vmem_limit_bytes=VMEM_LIMIT),
        cost_estimate=pl.CostEstimate(
            flops=flops, bytes_accessed=moved if flops != 1 else 1, transcendentals=0
        ),
    )(*ins)


def send(block, distance, ring):
    route = [(i, (i + distance) % ring) for i in range(ring)]
    return lax.ppermute(block, "seq", route)


NEAR = ("x", "core", "seq")
PLANE = ("x", "seq")


def swap(block, axes, step):
    return lax.ppermute(block, axes, [(i, i ^ step) for i in range(lax.axis_size(axes))])


def tree_sum(blocks):
    blocks = [block.astype(F32) for block in blocks]
    while len(blocks) > 1:
        blocks = [a + b for a, b in zip(blocks[::2], blocks[1::2])]
    return blocks[0].astype(BF)


def swaps(blocks, axes):
    return {step: swap(blocks[step], axes, step) for step in sorted(blocks, reverse=True)}


def sum_steps(own, got):
    return tree_sum([own] + [got[step] for step in sorted(got)])


def divide(keep, received, ring):
    half, width = keep.shape
    piece = jax.ShapeDtypeStruct((half // (2 * ring), width), BF)
    own, *pieces = call(
        functools.partial(divide_kernel, ring), [keep, received], [piece] * (2 * ring)
    )
    return own, dict(enumerate(pieces, 1))


def to_all(block, axes):
    return swaps({step: block for step in range(1, lax.axis_size(axes))}, axes)


def padded(rows, pieces):
    piece = -(-rows // pieces)
    return -(-piece // 16) * 16 * pieces


def body(
    tokens, masked, lengths, cotangent, mask_embed, query_weight, query_bias, key_weight,
    value_weight, value_bias, out_weight, out_bias, gain_one, shift_one, expand_weight,
    expand_bias, reduce_weight, reduce_bias, gain_two, shift_two,
):
    cells, rows, width = tokens.shape
    hidden = expand_weight.shape[1]
    ring = lax.axis_size("seq")

    def row(vector):
        return vector.reshape(1, -1)

    shape = jax.ShapeDtypeStruct
    low_wide, full_wide = shape((rows, WIDE), BF), shape((rows, WIDE), F32)
    low_narrow, full_narrow = shape((rows, width), BF), shape((rows, width), F32)
    weights = shape((HEADS * rows, rows), BF)
    score_flops = 2 * rows * rows * HEADS * 256

    stream = [
        jnp.where(masked[cell][:, None] == 1, mask_embed, tokens[cell]) for cell in range(cells)
    ]
    x_low = [part.astype(BF) for part in stream]
    x_moved = [[part] for part in x_low]
    x_moved[0] += [send(x_low[0], t, ring) for t in range(1, ring)]
    under = masked.astype(BF).reshape(-1, width)
    under = jnp.pad(under, ((0, MASK_ROWS - under.shape[0]), (0, 0)))
    x_moved[-1] = [jnp.concatenate([x_low[-1], under], axis=0)]

    made = call(
        functools.partial(first_kernel, cells),
        [lengths]
        + x_low
        + [query_weight, key_weight, value_weight, row(query_bias), row(value_bias)]
        + [out_weight, expand_weight, reduce_weight],
        [low_wide, low_wide, low_wide, weights, full_wide, full_wide] * cells
        + [
            shape((width, 3 * WIDE), BF),
            shape((width, 2 * width), BF),
            shape((WIDE, width), BF),
            shape((width, hidden), BF),
            shape((hidden, width), BF),
        ],
        flops=2 * cells * score_flops,
    )
    w_all, w_kv, wo, w1, w2 = made[-5:]
    bias_v = row(value_bias)
    for cell in range(1, cells):
        sent, w_all = lax.optimization_barrier((x_moved[cell][0], w_all))
        x_moved[cell] += [send(sent, t, ring) for t in range(1, ring)]
    keys, values, kept, queries, states, peaks = [], [], [], [], [], []
    for cell in range(cells):
        q, k, v, p, state, peak = made[6 * cell : 6 * cell + 6]
        queries.append(q)
        keys.append([k])
        values.append([v])
        kept.append([p])
        own_peaks = [peak]
        for t in range(1, ring - 1):
            k, v, p, own, state, peak = call(
                functools.partial(more_kernel, cell, t, ring),
                [lengths, x_moved[cell][t], q, state, peak, w_all, bias_v],
                [low_wide, low_wide, weights, full_wide, full_wide, full_wide],
                flops=2 * score_flops,
            )
            keys[cell].append(k)
            values[cell].append(v)
            kept[cell].append(p)
            own_peaks.append(own)
        states.append([state, peak])
        peaks.append(own_peaks if ring > 2 else [])

    one_rows = padded(3 * width + hidden, lax.axis_size(NEAR))
    results, firsts, grads_out = [], [], []
    carried, carried_back, received = [], [], []
    dq = [None] * cells

    def backward_of_blocks(cell):
        nonlocal carried_back
        partial = []
        for t in range(1, ring):
            ins = [
                x_moved[cell][t], x_moved[-1][t], queries[cell], grads_out[cell][t],
                keys[cell][t], values[cell][t], kept[cell][t], w_kv,
            ]
            ins += ([dq[cell]] if t > 1 else []) + carried_back
            dq[cell], dx, *carried_back = call(
                functools.partial(block_kernel, cell, t > 1, bool(carried_back)),
                ins,
                [
                    full_wide,
                    low_narrow,
                    shape((2 * width, width), F32),
                    shape((width, SLOT), F32),
                    shape((8, WIDE), F32),
                ],
                [pltpu.VMEM((2 * width, rows), BF)],
                flops=5 * score_flops,
            )
            partial.append(dx)
        return partial

    def returned(partial):
        return [send(dx, -t, ring) for t, dx in enumerate(partial, 1)]

    for cell in range(cells):
        finish = cell == cells - 1
        if cell > 0:
            partial = backward_of_blocks(cell - 1)
            states[cell], partial = lax.optimization_barrier((states[cell], partial))
            received.append(returned(partial))
        outs = [low_wide] * ring
        outs += [full_narrow, low_wide, low_wide, weights, full_narrow]
        outs += [shape((16, width), F32)]
        if finish:
            outs += [shape((one_rows // 2, width), BF)] * 2
        else:
            outs += [shape((width, WIDE), F32)] + [shape((width, hidden), F32)] * 2
        scratch = [pltpu.VMEM((rows, WIDE), F32)] * ring + [
            pltpu.VMEM((rows, WIDE), F32),
            pltpu.VMEM((rows, WIDE), BF),
            pltpu.VMEM((rows, width), BF),
            pltpu.VMEM((rows, hidden), BF),
            pltpu.VMEM((rows, hidden), BF),
            pltpu.VMEM((rows, width), BF),
            pltpu.VMEM((rows, width), BF),
            pltpu.VMEM((rows, width), F32),
            pltpu.VMEM((rows, SLOT), F32),
            pltpu.VMEM((rows, width), F32),
            pltpu.VMEM((rows, hidden), F32),
            pltpu.VMEM((12, 8, width), F32),
            pltpu.VMEM((8, hidden), F32),
        ]
        if finish:
            scratch.append(pltpu.VMEM((one_rows, width), BF))
        made = call(
            functools.partial(middle_kernel, cell, ring, bool(carried), finish),
            [
                lengths, x_moved[cell][ring - 1], queries[cell], *states[cell], stream[cell],
                cotangent[cell], w_all, bias_v, wo, row(out_bias), row(gain_one), row(shift_one),
                w1, row(expand_bias), w2, row(reduce_bias), row(gain_two), row(shift_two),
            ]
            + peaks[cell]
            + carried,
            outs,
            scratch,
            flops=7 * score_flops,
        )
        grads_out.append(made[:ring])
        result, k, v, p, first, vec_mid = made[ring : ring + 6]
        results.append(result)
        keys[cell].append(k)
        values[cell].append(v)
        kept[cell].append(p)
        firsts.append(first)
        carried = list(made[ring + 6 :]) + [vec_mid]
    keep, give = made[ring + 6 :]
    received_one = swap(give, "core", 1)
    queries[-1], received = lax.optimization_barrier((queries[-1], received))
    partial = backward_of_blocks(cells - 1)
    own_one, pieces = divide(keep, received_one, ring)
    carried, partial, own_one, pieces = lax.optimization_barrier(
        (carried_back, partial, own_one, pieces)
    )
    got_one = swaps(pieces, PLANE)

    two_rows = padded(3 * width + 32, lax.axis_size(NEAR))
    local = []
    depth_steps = [1 << i for i in range(lax.axis_size("z").bit_length() - 1)]
    for cell in range(cells):
        finish = cell == cells - 1
        if finish:
            carried, got_one, partial = lax.optimization_barrier((carried, got_one, partial))
            own_one = sum_steps(own_one, got_one)
            got_one = swap(own_one, "z", depth_steps[0])
            received.append(returned(partial))
        ins = [
            x_moved[cell][0], x_moved[-1][0], queries[cell], grads_out[cell][0], keys[cell][0],
            values[cell][0], kept[cell][0], w_all, w_kv, firsts[cell], dq[cell],
        ]
        outs = [full_narrow]
        scratch = [pltpu.VMEM((rows, WIDE), BF), pltpu.VMEM((2 * width, rows), BF)]
        if finish:
            outs += [shape((two_rows // 2, width), BF)] * 2
            scratch += [pltpu.VMEM((two_rows, width), BF)]
        else:
            outs += [shape((2 * width, width), F32), shape((width, SLOT), F32)]
            outs += [shape((8, WIDE), F32), shape((width, WIDE), F32)]
        made = call(
            functools.partial(last_kernel, cell, cell > 0, finish),
            ins + carried + ([vec_mid] if finish else []),
            outs,
            scratch,
            flops=1,
        )
        local.append(made[0])
        carried = list(made[1:])
    keep, give = carried
    give, got_one = lax.optimization_barrier((give, got_one))
    other = swap(give, "core", 1)
    for step in depth_steps[1:]:
        own_one = tree_sum([own_one, got_one])
        got_one = swap(own_one, "z", step)
    other, received = lax.optimization_barrier((other, received))
    own, pieces = divide(keep, other, ring)
    got, got_one = lax.optimization_barrier((swaps(pieces, PLANE), got_one))
    own = sum_steps(own, got)
    own = sum_steps(own, to_all(own, "z"))
    own_one = tree_sum([own_one, got_one])
    own = jnp.concatenate([own_one, own], axis=0)
    tokens_grad = call(
        functools.partial(finish_kernel, cells),
        [x_moved[-1][0]] + local + sum(received, []),
        [shape((cells, rows, width), F32)],
    )[0]
    got = to_all(own, PLANE)
    result = jnp.stack(results)
    got[1], tokens_grad, result = lax.optimization_barrier((got[1], tokens_grad, result))
    mine = [own] + [got[step] for step in sorted(got)]
    other = [swap(piece, "core", 1) for piece in mine]

    vector = shape((1, width), F32)
    made = call(
        functools.partial(unpack_kernel, ring),
        mine + other,
        [shape((width, width), F32), shape((width, hidden), F32), shape((hidden, width), F32)]
        + [shape((width, width), F32)] * 3
        + [vector] * 3
        + [shape((1, hidden), F32)]
        + [vector] * 6
        + [shape((1, 3), F32)],
        [pltpu.VMEM((one_rows, width), BF), pltpu.VMEM((two_rows, width), BF)],
    )
    dwo, dw1, dw2, dwq, dwk, dwv = made[:6]
    (
        gain_two_grad, shift_two_grad, bias_2_grad, bias_1_grad, gain_one_grad, shift_one_grad,
        bias_o_grad, bias_q_grad, bias_v_grad, mask_embed_grad, root_means,
    ) = [a.reshape(-1) for a in made[6:]]

    return (
        result,
        tokens_grad,
        mask_embed_grad,
        dwq,
        bias_q_grad,
        dwk,
        dwv,
        bias_v_grad,
        dwo,
        bias_o_grad,
        gain_one_grad,
        shift_one_grad,
        dw1,
        bias_1_grad,
        dw2,
        bias_2_grad,
        gain_two_grad,
        shift_two_grad,
        root_means,
    )


def solution(mesh):
    dp, seq = mesh.shape["dp"], mesh.shape["seq"]
    cut = jax.sharding.Mesh(mesh.devices.reshape(dp // 4, 2, 2, seq), ("z",) + NEAR)
    dp = ("z", "x", "core")
    split = P(dp, "seq", None)
    return jax.shard_map(
        body,
        mesh=cut,
        in_specs=(split, P(dp, "seq"), P(dp), split) + (P(),) * 16,
        out_specs=(split, split) + (P(),) * 17,
        check_vma=False,
    )
```

```python
import functools

import jax
import jax.numpy as jnp
from jax import lax
from jax.experimental import pallas as pl
from jax.experimental.pallas import tpu as pltpu
from jax.sharding import PartitionSpec as P

HEADS = 4
HEAD_DIM = 64
SLOT = 128
WIDE = HEADS * SLOT

EPSILON = 1e-05
NEGATIVE = -1e30
INV_ROOT_TWO_PI = 0.3989422804014327
BF = jnp.bfloat16
F32 = jnp.float32
VMEM_LIMIT = 16 * 1024 * 1024
MASK_ROWS = 16


def nn(left, right):
    return lax.dot_general(left, right, (((1,), (0,)), ((), ())), preferred_element_type=F32)


def nt(left, right):
    return lax.dot_general(left, right, (((1,), (1,)), ((), ())), preferred_element_type=F32)


def tn(left, right):
    return lax.dot_general(left, right, (((0,), (0,)), ((), ())), preferred_element_type=F32)


def lane_of(shape):
    return lax.broadcasted_iota(jnp.int32, shape, len(shape) - 1)


def row_of(shape):
    return lax.broadcasted_iota(jnp.int32, shape, len(shape) - 2)


def spread(matrix):
    pieces = []
    for pair in range(HEADS // 2):
        both = matrix[:, pair * SLOT : (pair + 1) * SLOT]
        first = lane_of(both.shape) < HEAD_DIM
        pieces.append(jnp.where(first, both, 0.0))
        pieces.append(jnp.where(first, pltpu.roll(both, HEAD_DIM, 1), 0.0))
    return jnp.concatenate(pieces, axis=1)


def joined(wide):
    pieces = []
    for pair in range(HEADS // 2):
        even = wide[:, 2 * pair * SLOT : (2 * pair + 1) * SLOT]
        odd = wide[:, (2 * pair + 1) * SLOT : (2 * pair + 2) * SLOT]
        pieces.append(jnp.where(lane_of(even.shape) < HEAD_DIM, even, pltpu.roll(odd, HEAD_DIM, 1)))
    return jnp.concatenate(pieces, axis=1)


def spread_rows(matrix):
    gap = jnp.zeros((SLOT - HEAD_DIM, matrix.shape[1]), matrix.dtype)
    pieces = []
    for head in range(HEADS):
        pieces += [matrix[head * HEAD_DIM : (head + 1) * HEAD_DIM], gap]
    return jnp.concatenate(pieces, axis=0)


def head_cols(head):
    return slice(head * SLOT, (head + 1) * SLOT)


def project_keys(x, w_all, bias_v, first_place, length, k_out, v_out):
    raw = nn(x, w_all[:, WIDE : 2 * WIDE])
    shut = lane_of(raw.shape) % SLOT == HEAD_DIM + 2
    shut &= row_of(raw.shape) + first_place >= length
    k_out[...] = jnp.where(shut, NEGATIVE, raw).astype(BF)
    one_row = lane_of((1, WIDE)) % SLOT
    ones_row = jnp.where((one_row == HEAD_DIM) | (one_row == HEAD_DIM + 1), 1.0, 0.0)
    v_out[...] = (nn(x, w_all[:, 2 * WIDE :]) + (spread(bias_v) + ones_row)).astype(BF)


def attend(queries, keys, values, kept):
    scores = nt(queries, keys)
    peak = jnp.max(scores, axis=1, keepdims=True)
    kept[...] = jnp.exp(scores - peak).astype(BF)
    return nn(kept[...], values), jnp.broadcast_to(peak, (peak.shape[0], SLOT))


def kept_rows(head, rows):
    return slice(head * rows, (head + 1) * rows)


def owner_of(distance, ring):
    return lax.rem(lax.axis_index("seq") - distance + ring, ring)


def select_kernel(
    cell, carry, tokens, masks, embed, stream_out, low_out, *refs
):
    held, mask_held, embed_held, arrived = refs[-4:]
    copies = [
        pltpu.make_async_copy(source, target, arrived.at[which])
        for which, (source, target) in enumerate(
            ((tokens.at[cell], held), (masks, mask_held), (embed, embed_held))
        )
    ]
    for copy in copies:
        copy.start()
    for copy in copies[1:]:
        copy.wait()
    rows, width = held.shape
    mask = mask_held[cell : cell + 1, :].astype(F32)
    column = jnp.transpose(jnp.broadcast_to(mask, (8, rows)))[:, :1]
    copies[0].wait()
    stream = jnp.where(column == 1.0, embed_held[...], held[...])
    stream_out[...] = stream
    low_out[...] = stream.astype(BF)
    if not carry:
        return
    carrier_out = refs[0]
    pieces = [
        mask_held[which : which + 1, at : at + width]
        for which in range(masks.shape[0])
        for at in range(0, rows, width)
    ]
    pieces.append(jnp.zeros((MASK_ROWS - len(pieces), width), masks.dtype))
    carrier_out[:rows, :] = stream.astype(BF)
    carrier_out[rows:, :] = jnp.concatenate(pieces, axis=0).astype(F32).astype(BF)


def mask_of(carrier, cell):
    rows = carrier.shape[0] - MASK_ROWS
    count = rows // carrier.shape[1]
    under = carrier[rows:, :].astype(F32)
    first = cell * count
    return jnp.concatenate([under[first + at : first + at + 1] for at in range(count)], axis=1)


def first_kernel(cells, lengths, *refs):
    xs, refs = refs[:cells], refs[cells:]
    wq, wk, wv, bias_q, bias_v = refs[:5]
    outs, (w_all, w_kv) = refs[5:-2], refs[-2:]
    w_all[:, :WIDE] = spread(wq[...] * HEAD_DIM ** (-0.5)).astype(BF)
    w_all[:, WIDE : 2 * WIDE] = spread(wk[...]).astype(BF)
    w_all[:, 2 * WIDE :] = spread(wv[...]).astype(BF)
    rows = outs[0].shape[0]
    first_place = lax.axis_index("seq") * rows
    one_row = lane_of((1, WIDE)) % SLOT
    bias = spread(bias_q[...]) * HEAD_DIM ** (-0.5) + jnp.where(one_row == HEAD_DIM + 2, 1.0, 0.0)
    for cell in range(cells):
        x = xs[cell].at[:rows]
        q_out, k_out, v_out, kept_out, state_out, peak_out = outs[6 * cell : 6 * cell + 6]
        q_out[...] = (nn(x[...], w_all[:, :WIDE]) + bias).astype(BF)
        project_keys(x[...], w_all, bias_v[...], first_place, lengths[cell], k_out, v_out)
        for head in range(HEADS):
            cols = head_cols(head)
            state_out[:, cols], peak_out[:, cols] = attend(
                q_out[:, cols], k_out[:, cols], v_out[:, cols], kept_out.at[kept_rows(head, rows)]
            )
    width = wk.shape[1]
    w_kv[:, :width] = wk[...].astype(BF)
    w_kv[:, width:] = wv[...].astype(BF)


def more_kernel(
    cell, distance, ring,
    lengths, x, q, state, peak, w_all, bias_v,
    k_out, v_out, kept_out, own_out, state_out, peak_out,
):
    rows = q.shape[0]
    first_place = owner_of(distance, ring) * rows
    project_keys(x[:rows, :], w_all, bias_v[...], first_place, lengths[cell], k_out, v_out)
    for head in range(HEADS):
        cols = head_cols(head)
        total, own = attend(
            q[:, cols], k_out[:, cols], v_out[:, cols], kept_out.at[kept_rows(head, rows)]
        )
        top = jnp.maximum(peak[:, cols], own)
        own_out[:, cols] = own
        peak_out[:, cols] = top
        state_out[:, cols] = state[:, cols] * jnp.exp(peak[:, cols] - top)
        state_out[:, cols] += total * jnp.exp(own - top)


def norm_parts(matrix):
    row_mean = jnp.mean(matrix, axis=1, keepdims=True)
    centred = matrix - row_mean
    row_var = jnp.mean(centred * centred, axis=1, keepdims=True)
    inverse = lax.rsqrt(row_var + EPSILON)
    return centred * inverse, inverse


def norm_back(grad, unit, inverse):
    shift = jnp.mean(grad, axis=1, keepdims=True)
    scale = jnp.mean(grad * unit, axis=1, keepdims=True)
    return (grad - shift - unit * scale) * inverse


def eight_sum(matrix):
    return jnp.sum(matrix.reshape(-1, 8, matrix.shape[1]), axis=0)


def inverse_of(value):
    guess = pl.reciprocal(value, approx=True)
    return guess * (2.0 - value * guess)


def gelu_parts(pre):
    bell = jnp.exp(pre * pre * (-0.5))
    t = inverse_of(1.0 + (0.3275911 * 0.7071067811865476) * jnp.abs(pre))
    poly = 0.5 * 1.061405429
    for factor in (-1.453152027, 1.421413741, -0.284496736, 0.254829592):
        poly = poly * t + 0.5 * factor
    tail = poly * t * bell
    half = jnp.where(pre >= 0.0, 1.0 - tail, tail)
    return pre * half, half + pre * bell * INV_ROOT_TWO_PI


def halve(pack, keep_out, give_out):
    half = keep_out.shape[0]
    core = lax.axis_index("core")
    keep_out[...] = pack[pl.ds(pl.multiple_of(core * half, half), half), :]
    give_out[...] = pack[pl.ds(pl.multiple_of((1 - core) * half, half), half), :]


def my_plane(ring):
    return lax.axis_index("x") * ring + lax.axis_index("seq")


def halve(pack, keep_out, give_out):
    half = keep_out.shape[0]
    core = lax.axis_index("core")
    keep_out[...] = pack[pl.ds(pl.multiple_of(core * half, half), half), :]
    give_out[...] = pack[pl.ds(pl.multiple_of((1 - core) * half, half), half), :]


def near_bits(ring, core):
    bits = [("seq", 1 << i) for i in range(ring.bit_length() - 1)]
    return bits + [("x", 1)] if core else [("x", 1)] + bits


def my_side(ring, step):
    sides = []
    for core in range(2):
        axis, bit = near_bits(ring, core)[step]
        sides.append(lax.rem(lax.axis_index(axis) // bit, 2))
    return jnp.where(lax.axis_index("core") == 0, sides[0], sides[1])


def halve_kernel(ring, step, keep, received, keep_out, give_out):
    half = keep_out.shape[0]
    side = my_side(ring, step)
    for out, place in ((keep_out, side), (give_out, 1 - side)):
        at = pl.ds(pl.multiple_of(place * half, half), half)
        out[...] = (keep[at, :].astype(F32) + received[at, :].astype(F32)).astype(BF)


def join_kernel(ring, step, mine, other, out):
    rows = mine.shape[0]
    side = my_side(ring, step)
    out[pl.ds(pl.multiple_of(side * rows, rows), rows), :] = mine[...]
    out[pl.ds(pl.multiple_of((1 - side) * rows, rows), rows), :] = other[...]


def divide_kernel(ring, keep, received, own_out, *give_outs):
    piece = own_out.shape[0]
    plane = my_plane(ring)
    for step, out in enumerate((own_out,) + give_outs):
        at = pl.ds(pl.multiple_of((plane ^ step) * piece, piece), piece)
        out[...] = (keep[at, :].astype(F32) + received[at, :].astype(F32)).astype(BF)


def place_pieces(ring, mine, other, pack_one, pack_two):
    plane, core = my_plane(ring), lax.axis_index("core")
    for step in range(2 * ring):
        start = 0
        for pack in (pack_one, pack_two):
            piece = pack.shape[0] // (4 * ring)
            for half, sources in ((core, mine), (1 - core, other)):
                at = pl.multiple_of((half * 2 * ring + (plane ^ step)) * piece, piece)
                pack[pl.ds(at, piece), :] = sources[step][start : start + piece, :]
            start += piece


def middle_kernel(
    cell, ring, carry, finish,
    lengths, x, q, state, peak, stream, cotangent, w_all, bias_v, wo_in, bias_o, gain_one,
    shift_one, w1_in, bias_1, w2_in, bias_2, gain_two, shift_two, *refs,
):
    count = ring - 1 if ring > 2 else 0
    before, refs = refs[:count], refs[count:]
    if carry:
        dwo_in, dw1_in, dw2_in, vec_in = refs[:4]
        refs = refs[4:]
    do_outs, refs = refs[:ring], refs[ring:]
    result_out, k_out, v_out, kept_out, x_out, first_out, vec_out = refs[:7]
    refs = refs[7:]
    if carry:
        wo, w1, w2 = wo_in, w1_in, w2_in
    else:
        wo, w1, w2 = refs[:3]
        refs = refs[3:]
        wo[...] = spread_rows(wo_in[...].astype(BF))
        w1[...] = w1_in[...].astype(BF)
        w2[...] = w2_in[...].astype(BF)
    if finish:
        keep_out, give_out = refs[:2]
        refs = refs[2:]
    else:
        dwo_out, dw1_out, dw2_out = refs[:3]
        refs = refs[3:]
    scales, refs = refs[:ring], refs[ring:]
    (
        attended_wide, attended_low, normed_low, active_low, hidden_low, branch_low, attn_low,
        unit_one, inverse_one, narrow_b, wide_b, acc, *pack_ref,
    ) = refs
    rows, width = stream.shape
    x_out[...] = x[:rows, :]
    hidden = w1.shape[1]
    length = lengths[cell]
    first_place = owner_of(ring - 1, ring) * rows
    project_keys(x[:rows, :], w_all, bias_v[...], first_place, length, k_out, v_out)
    for head in range(HEADS):
        cols = head_cols(head)
        total, own = attend(
            q[:, cols], k_out[:, cols], v_out[:, cols], kept_out.at[kept_rows(head, rows)]
        )
        top = jnp.maximum(peak[:, cols], own)
        old_scale, own_scale = jnp.exp(peak[:, cols] - top), jnp.exp(own - top)
        both = state[:, cols] * old_scale + total * own_scale
        inverse = inverse_of(both[:, HEAD_DIM : HEAD_DIM + 1])
        attended = both * inverse
        attended_wide[:, cols] = attended
        attended_low[:, cols] = attended.astype(BF)
        scales[ring - 1][:, cols] = own_scale * inverse
        if ring == 2:
            scales[0][:, cols] = old_scale * inverse
        else:
            for block in range(ring - 1):
                scales[block][:, cols] = jnp.exp(before[block][:, cols] - top) * inverse

    my_place = lax.axis_index("seq") * rows

    valid = jnp.where(row_of((rows, width)) + my_place < length, 1.0, 0.0)

    def add(slot, matrix):
        acc[slot] = eight_sum(matrix)

    attn_out = nn(attended_low[...], wo[...]) + bias_o[...]
    unit, inverse = norm_parts(stream[...] + attn_out)
    unit_one[...] = unit
    inverse_one[...] = jnp.broadcast_to(inverse, (rows, SLOT))
    normed = unit * gain_one[...] + shift_one[...]
    narrow_b[...] = normed
    normed_low[...] = normed.astype(BF)
    add(8, stream[...] * stream[...] * valid)
    add(9, attn_out * attn_out * valid)

    active, slope = gelu_parts(nn(normed_low[...], w1[...]) + bias_1[...])
    active_low[...] = active.astype(BF)
    wide_b[...] = slope

    branch = nn(active_low[...], w2[...]) + bias_2[...]
    unit, inverse = norm_parts(narrow_b[...] + branch)
    result_out[...] = unit * gain_two[...] + shift_two[...]
    grad_result = cotangent[...] * valid
    grad_second = norm_back(grad_result * gain_two[...], unit, inverse)
    narrow_b[...] = grad_second
    branch_bf = grad_second.astype(BF)
    branch_low[...] = branch_bf
    add(0, grad_result * unit)
    add(1, grad_result)
    add(10, branch * branch * valid)

    hidden_bf = (nt(branch_low[...], w2[...]) * wide_b[...]).astype(BF)
    hidden_low[...] = hidden_bf

    grad_normed = narrow_b[...] + nt(hidden_low[...], w1[...])
    unit = unit_one[...]
    grad_first = norm_back(grad_normed * gain_one[...], unit, inverse_one[:, :1])
    first_out[...] = grad_first
    attn_bf = grad_first.astype(BF)
    attn_low[...] = attn_bf
    add(5, grad_normed * unit)
    add(6, grad_normed)

    do_wide = nt(attn_low[...], wo[...]).astype(BF).astype(F32)
    for head in range(HEADS):
        cols = head_cols(head)
        do_head = do_wide[:, cols]
        row_dot = jnp.sum(do_head * attended_wide[:, cols], axis=1, keepdims=True)
        lane = lane_of(do_head.shape)
        for scale, do_out in zip(scales, do_outs):
            factor = scale[:, cols]
            dot = -row_dot * factor
            rest = dot - dot.astype(BF).astype(F32)
            scaled = jnp.where(lane == HEAD_DIM, dot, do_head * factor)
            do_out[:, cols] = jnp.where(lane == HEAD_DIM + 1, rest, scaled).astype(BF)

    ones = jnp.ones((8, rows), BF)
    hidden_sum = nn(ones, hidden_low[...])[0:1]
    known = {
        2: nn(ones, branch_low[...])[0:1],
        3: hidden_sum[:, :width],
        4: hidden_sum[:, width:],
        7: nn(ones, attn_low[...])[0:1],
        11: jnp.full((1, width), jnp.clip(length - my_place, 0, rows).astype(F32)),
    }
    sums = [
        known[slot] if slot in known else jnp.sum(acc[slot], axis=0, keepdims=True)
        for slot in range(12)
    ]
    vec = jnp.concatenate(sums + [jnp.zeros((4, width), F32)], axis=0)
    vec_out[...] = vec + vec_in[...] if carry else vec

    dwo = tn(attn_low[...], attended_low[...])
    dw1 = tn(normed_low[...], hidden_low[...])
    dw2 = tn(branch_low[...], active_low[...])
    if carry:
        dwo += dwo_in[...]
        dw1 += dw1_in[...]
        dw2 += dw2_in[...]
    if not finish:
        dwo_out[...] = dwo
        dw1_out[...] = dw1
        dw2_out[...] = dw2
        return
    (pack,) = pack_ref
    pack[:width, :] = joined(dwo).astype(BF)
    pack[width : 2 * width, :] = dw1[:, :width].astype(BF)
    pack[2 * width : 3 * width, :] = dw1[:, width:].astype(BF)
    for at in range(0, hidden, width):
        pack[3 * width + at : 4 * width + at, :] = dw2[:, at : at + width].astype(BF)
    used = 3 * width + hidden
    if pack.shape[0] > used:
        pack[used:, :] = jnp.zeros((pack.shape[0] - used, width), BF)
    halve(pack, keep_out, give_out)


def head_grads(q, k, v, do, kept):
    score_grad = (kept.astype(F32) * nt(do, v)).astype(BF)
    return (
        nn(score_grad, k),
        tn(q[:, :HEAD_DIM], score_grad),
        tn(do[:, :HEAD_DIM], kept),
    )


def all_heads(q, k, v, do, kept, low, put_query):
    rows = q.shape[0]
    for head in range(HEADS):
        cols = head_cols(head)
        dq, dk, dv = head_grads(
            q[:, cols], k[:, cols], v[:, cols], do[:, cols], kept[kept_rows(head, rows), :]
        )
        put_query(cols, dq)
        low[head * HEAD_DIM : (head + 1) * HEAD_DIM, :] = dk.astype(BF)
        at = (HEADS + head) * HEAD_DIM
        low[at : at + HEAD_DIM, :] = dv.astype(BF)


def masked_sum(carrier, cell, grad_bf):
    mask = mask_of(carrier, cell)
    picked = jnp.broadcast_to(mask, (8, mask.shape[1])).astype(BF)
    return nn(picked, grad_bf)[0:1]


def value_sums(low):
    half = low.shape[0] // 2
    sums = jnp.sum(low[half:, :].astype(F32), axis=1, keepdims=True)
    return jnp.broadcast_to(sums, (half, SLOT))


def block_kernel(cell, carry_dq, carry, sent, carrier, q, do, k, v, kept, w_kv, *refs):
    if carry_dq:
        dq_in, refs = refs[0], refs[1:]
    if carry:
        (dw_in, sum_in, vec_in), refs = refs[:3], refs[3:]
    dq_out, dx_out, dw_out, sum_out, vec_out, low = refs

    def put_query(cols, dq):
        dq_out[:, cols] = dq + dq_in[:, cols] if carry_dq else dq

    all_heads(q, k, v, do, kept, low, put_query)
    x = sent[: q.shape[0], :]
    dx_bf = jnp.transpose(nn(w_kv[...], low[...])).astype(BF)
    dx_out[...] = dx_bf
    dw = nn(low[...], x)
    dw_out[...] = dw + dw_in[...] if carry else dw
    sums = value_sums(low)
    sum_out[...] = sums + sum_in[...] if carry else sums
    vec_out[...] = vec_in[...] if carry else jnp.zeros_like(vec_out)
    vec_out[0:1, : x.shape[1]] += masked_sum(carrier[...], cell, dx_bf)


def last_kernel(
    cell, carry, finish,
    sent, carrier, q, do, k, v, kept, w_all, w_kv, first, dq_in, dw_in, sum_in, vec_in, *refs
):
    if carry:
        dwq_in, refs = refs[0], refs[1:]
    if finish:
        vec_mid, dx_out, keep_out, give_out, low_q, low, pack = refs
    else:
        dx_out, dw_out, sum_out, vec_out, dwq_out, low_q, low = refs

    def put_query(cols, dq):
        low_q[:, cols] = ((dq + dq_in[:, cols]) * HEAD_DIM ** (-0.5)).astype(BF)

    all_heads(q, k, v, do, kept, low, put_query)
    grads = first[...] + nt(low_q[...], w_all[:, :WIDE]) * HEAD_DIM**0.5
    grads += jnp.transpose(nn(w_kv[...], low[...]))
    dx_out[...] = grads
    width = grads.shape[1]
    x = sent[: q.shape[0], :]
    dwq = tn(x, low_q[...])
    dw = nn(low[...], x) + dw_in[...]
    sum_q = jnp.sum(low_q[...].astype(F32), axis=0, keepdims=True) + vec_in[1:2, :]
    sum_v = value_sums(low) + sum_in[...]
    sum_mask = masked_sum(carrier[...], cell, grads.astype(BF)) + vec_in[0:1, :width]
    if carry:
        dwq += dwq_in[...]
    if not finish:
        dwq_out[...] = dwq
        dw_out[...] = dw
        sum_out[...] = sum_v
        vec_out[...] = jnp.zeros_like(vec_out)
        vec_out[0:1, :width] = sum_mask
        vec_out[1:2, :] = sum_q
        return
    pack[:width, :] = joined(dwq).astype(BF)
    pack[width : 3 * width, :] = dw.astype(BF)
    rows = jnp.concatenate(
        [
            vec_mid[:12, :],
            joined(sum_q),
            jnp.transpose(sum_v)[0:1, :],
            sum_mask,
            jnp.zeros((1, width), F32),
        ],
        axis=0,
    )
    high = rows.astype(BF)
    pack[3 * width : 3 * width + 16, :] = high
    pack[3 * width + 16 : 3 * width + 32, :] = (rows - high.astype(F32)).astype(BF)
    used = 3 * width + 32
    if pack.shape[0] > used:
        pack[used:, :] = jnp.zeros((pack.shape[0] - used, width), BF)
    halve(pack, keep_out, give_out)


def unpack_kernel(ring, *refs):
    mine, other, refs = refs[: 2 * ring], refs[2 * ring : 4 * ring], refs[4 * ring :]
    dwo_out, dw1_out, dw2_out, dwq_out, dwk_out, dwv_out = refs[:6]
    outs, pack_one, pack = refs[6:-2], refs[-2], refs[-1]
    place_pieces(ring, mine, other, pack_one, pack)
    width = pack.shape[1]
    dwo_out[...] = jnp.transpose(pack_one[:width, :].astype(F32))
    dw1_out[:, :width] = pack_one[width : 2 * width, :].astype(F32)
    dw1_out[:, width:] = pack_one[2 * width : 3 * width, :].astype(F32)
    for at in range(0, dw2_out.shape[0], width):
        dw2_out[at : at + width, :] = jnp.transpose(
            pack_one[3 * width + at : 4 * width + at, :].astype(F32)
        )
    dwq_out[...] = pack[:width, :].astype(F32)
    dwk_out[...] = jnp.transpose(pack[width : 2 * width, :].astype(F32))
    dwv_out[...] = jnp.transpose(pack[2 * width : 3 * width, :].astype(F32))
    vec = pack[3 * width : 3 * width + 16, :].astype(F32)
    vec += pack[3 * width + 16 : 3 * width + 32, :].astype(F32)
    for out, row in zip(outs, (0, 1, 2, (3, 4), 5, 6, 7, 12, 13, 14)):
        if isinstance(row, tuple):
            out[:, :width] = vec[row[0] : row[0] + 1]
            out[:, width:] = vec[row[1] : row[1] + 1]
        else:
            out[...] = vec[row : row + 1]
    squares = jnp.sum(vec[8:16], axis=1, keepdims=True)
    count = vec[11:12, 0:1]
    means = jnp.sqrt(squares / (count * width))
    lane = lane_of((1, 3))
    outs[10][...] = jnp.where(
        lane == 0, means[0:1], jnp.where(lane == 1, means[1:2], means[2:3])
    )


def finish_kernel(cells, carrier, *refs):
    local, received, out = refs[:cells], refs[cells:-1], refs[-1]
    rows, count = local[0].shape[0], len(received) // cells
    for cell in range(cells):
        grads = local[cell][...]
        for piece in received[cell * count : (cell + 1) * count]:
            grads += piece[...].astype(F32)
        mask = jnp.broadcast_to(mask_of(carrier[...], cell), (8, rows))
        out[cell] = jnp.where(jnp.transpose(mask)[:, :1] == 1.0, 0.0, grads)


def call(kernel, ins, outs, scratch=(), flops=0):
    moved = sum(a.size * a.dtype.itemsize for a in ins) + sum(
        s.size * s.dtype.itemsize for s in outs
    )
    vmem = pl.BlockSpec(memory_space=pltpu.VMEM)
    smem = pl.BlockSpec(memory_space=pltpu.SMEM)
    return pl.pallas_call(
        kernel,
        in_specs=[smem if a.ndim == 1 else vmem for a in ins],
        out_specs=[vmem] * len(outs),
        out_shape=outs,
        scratch_shapes=list(scratch),
        compiler_params=pltpu.CompilerParams(vmem_limit_bytes=VMEM_LIMIT),
        cost_estimate=pl.CostEstimate(
            flops=flops, bytes_accessed=moved if flops != 1 else 1, transcendentals=0
        ),
    )(*ins)


def send(block, distance, ring):
    route = [(i, (i + distance) % ring) for i in range(ring)]
    return lax.ppermute(block, "seq", route)


NEAR = ("x", "core", "seq")
PLANE = ("x", "seq")


def swap(block, axes, step):
    return lax.ppermute(block, axes, [(i, i ^ step) for i in range(lax.axis_size(axes))])


def tree_sum(blocks):
    blocks = [block.astype(F32) for block in blocks]
    while len(blocks) > 1:
        blocks = [a + b for a, b in zip(blocks[::2], blocks[1::2])]
    return blocks[0].astype(BF)


def swaps(blocks, axes):
    return {step: swap(blocks[step], axes, step) for step in sorted(blocks, reverse=True)}


def sum_steps(own, got):
    return tree_sum([own] + [got[step] for step in sorted(got)])


def divide(keep, received, ring):
    half, width = keep.shape
    piece = jax.ShapeDtypeStruct((half // (2 * ring), width), BF)
    own, *pieces = call(
        functools.partial(divide_kernel, ring), [keep, received], [piece] * (2 * ring)
    )
    return own, dict(enumerate(pieces, 1))


def to_all(block, axes):
    return swaps({step: block for step in range(1, lax.axis_size(axes))}, axes)


def padded(rows, pieces):
    piece = -(-rows // pieces)
    return -(-piece // 16) * 16 * pieces


def body(
    tokens, masked, lengths, cotangent, mask_embed, query_weight, query_bias, key_weight,
    value_weight, value_bias, out_weight, out_bias, gain_one, shift_one, expand_weight,
    expand_bias, reduce_weight, reduce_bias, gain_two, shift_two,
):
    cells, rows, width = tokens.shape
    hidden = expand_weight.shape[1]
    ring = lax.axis_size("seq")

    def row(vector):
        return vector.reshape(1, -1)

    shape = jax.ShapeDtypeStruct
    low_wide, full_wide = shape((rows, WIDE), BF), shape((rows, WIDE), F32)
    low_narrow, full_narrow = shape((rows, width), BF), shape((rows, width), F32)
    weights = shape((HEADS * rows, rows), BF)
    score_flops = 2 * rows * rows * HEADS * 256

    stream, x_moved, x_low = [], [], []
    vmem = pl.BlockSpec(memory_space=pltpu.VMEM)
    masks = masked
    for cell in range(cells):
        carry = cell == cells - 1
        outs = [full_narrow, low_narrow] + [shape((rows + MASK_ROWS, width), BF)] * carry
        made = pl.pallas_call(
            functools.partial(select_kernel, cell, carry),
            in_specs=[pl.BlockSpec(memory_space=pltpu.HBM)] * 3,
            out_specs=[vmem] * len(outs),
            out_shape=outs,
            scratch_shapes=[
                pltpu.VMEM((rows, width), F32),
                pltpu.VMEM((cells, rows), jnp.int32),
                pltpu.VMEM((1, width), F32),
                pltpu.SemaphoreType.DMA((3,)),
            ],
            compiler_params=pltpu.CompilerParams(vmem_limit_bytes=VMEM_LIMIT),
        )(
            *[
                pltpu.with_memory_space_constraint(a, pltpu.HBM)
                for a in (tokens, masks, row(mask_embed))
            ]
        )
        stream.append(made[0])
        x_low.append(made[1])
        x_moved.append([made[-1]])
        if cell == 0:
            x_moved[0] += [send(x_moved[0][0], t, ring) for t in range(1, ring)]
        masks, x_low[cell] = lax.optimization_barrier((masks, x_low[cell]))

    made = call(
        functools.partial(first_kernel, cells),
        [lengths]
        + x_low
        + [query_weight, key_weight, value_weight, row(query_bias), row(value_bias)],
        [low_wide, low_wide, low_wide, weights, full_wide, full_wide] * cells
        + [
            shape((width, 3 * WIDE), BF),
            shape((width, 2 * width), BF),
        ],
        flops=2 * cells * score_flops,
    )
    w_all, w_kv = made[-2:]
    wo, w1, w2 = out_weight, expand_weight, reduce_weight
    low_weights = [
        shape((WIDE, width), BF), shape((width, hidden), BF), shape((hidden, width), BF)
    ]
    bias_v = row(value_bias)
    for cell in range(1, cells):
        sent, w_all = lax.optimization_barrier((x_moved[cell][0], w_all))
        x_moved[cell] += [send(sent, t, ring) for t in range(1, ring)]
    carriers = list(x_moved[-1])
    keys, values, kept, queries, states, peaks = [], [], [], [], [], []
    for cell in range(cells):
        q, k, v, p, state, peak = made[6 * cell : 6 * cell + 6]
        queries.append(q)
        keys.append([k])
        values.append([v])
        kept.append([p])
        own_peaks = [peak]
        for t in range(1, ring - 1):
            k, v, p, own, state, peak = call(
                functools.partial(more_kernel, cell, t, ring),
                [lengths, x_moved[cell][t], q, state, peak, w_all, bias_v],
                [low_wide, low_wide, weights, full_wide, full_wide, full_wide],
                flops=2 * score_flops,
            )
            keys[cell].append(k)
            values[cell].append(v)
            kept[cell].append(p)
            own_peaks.append(own)
        states.append([state, peak])
        peaks.append(own_peaks if ring > 2 else [])

    one_rows = padded(3 * width + hidden, lax.axis_size(NEAR))
    results, firsts, grads_out = [], [], []
    carried, carried_back, received = [], [], []
    dq = [None] * cells

    def backward_of_blocks(cell):
        nonlocal carried_back
        partial = []
        for t in range(1, ring):
            ins = [
                x_moved[cell][t], carriers[t], queries[cell], grads_out[cell][t],
                keys[cell][t], values[cell][t], kept[cell][t], w_kv,
            ]
            ins += ([dq[cell]] if t > 1 else []) + carried_back
            dq[cell], dx, *carried_back = call(
                functools.partial(block_kernel, cell, t > 1, bool(carried_back)),
                ins,
                [
                    full_wide,
                    low_narrow,
                    shape((2 * width, width), F32),
                    shape((width, SLOT), F32),
                    shape((8, WIDE), F32),
                ],
                [pltpu.VMEM((2 * width, rows), BF)],
                flops=5 * score_flops,
            )
            partial.append(dx)
        return partial

    def returned(partial):
        return [send(dx, -t, ring) for t, dx in enumerate(partial, 1)]

    for cell in range(cells):
        finish = cell == cells - 1
        if cell > 0:
            partial = backward_of_blocks(cell - 1)
            states[cell], partial = lax.optimization_barrier((states[cell], partial))
            received.append(returned(partial))
        outs = [low_wide] * ring
        outs += [full_narrow, low_wide, low_wide, weights, low_narrow, full_narrow]
        outs += [shape((16, width), F32)] + (low_weights if cell == 0 else [])
        if finish:
            outs += [shape((one_rows // 2, width), BF)] * 2
        else:
            outs += [shape((width, WIDE), F32)] + [shape((width, hidden), F32)] * 2
        scratch = [pltpu.VMEM((rows, WIDE), F32)] * ring + [
            pltpu.VMEM((rows, WIDE), F32),
            pltpu.VMEM((rows, WIDE), BF),
            pltpu.VMEM((rows, width), BF),
            pltpu.VMEM((rows, hidden), BF),
            pltpu.VMEM((rows, hidden), BF),
            pltpu.VMEM((rows, width), BF),
            pltpu.VMEM((rows, width), BF),
            pltpu.VMEM((rows, width), F32),
            pltpu.VMEM((rows, SLOT), F32),
            pltpu.VMEM((rows, width), F32),
            pltpu.VMEM((rows, hidden), F32),
            pltpu.VMEM((12, 8, width), F32),
        ]
        if finish:
            scratch.append(pltpu.VMEM((one_rows, width), BF))
        made = call(
            functools.partial(middle_kernel, cell, ring, bool(carried), finish),
            [
                lengths, x_moved[cell][ring - 1], queries[cell], *states[cell], stream[cell],
                cotangent[cell], w_all, bias_v, wo, row(out_bias), row(gain_one), row(shift_one),
                w1, row(expand_bias), w2, row(reduce_bias), row(gain_two), row(shift_two),
            ]
            + peaks[cell]
            + carried,
            outs,
            scratch,
            flops=7 * score_flops,
        )
        grads_out.append(made[:ring])
        result, k, v, p, x_moved[cell][ring - 1], first, vec_mid = made[ring : ring + 7]
        made = made[ring + 7 :]
        if cell == 0:
            wo, w1, w2 = made[:3]
            made = made[3:]
        results.append(result)
        keys[cell].append(k)
        values[cell].append(v)
        kept[cell].append(p)
        firsts.append(first)
        carried = list(made) + [vec_mid]
    keep, give = made
    received_one = swap(give, "core", 1)
    queries[-1], received = lax.optimization_barrier((queries[-1], received))
    partial = backward_of_blocks(cells - 1)
    own_one, pieces = divide(keep, received_one, ring)
    carried, partial, own_one, pieces = lax.optimization_barrier(
        (carried_back, partial, own_one, pieces)
    )
    got_one = swaps(pieces, PLANE)

    two_rows = padded(3 * width + 32, lax.axis_size(NEAR))
    local = []
    depth_steps = [1 << i for i in range(lax.axis_size("z").bit_length() - 1)]
    for cell in range(cells):
        finish = cell == cells - 1
        if finish:
            carried, got_one = lax.optimization_barrier((carried, got_one))
            own_one = sum_steps(own_one, got_one)
            got_one = swap(own_one, "z", depth_steps[0])
        ins = [
            x_moved[cell][0], carriers[0], queries[cell], grads_out[cell][0], keys[cell][0],
            values[cell][0], kept[cell][0], w_all, w_kv, firsts[cell], dq[cell],
        ]
        outs = [full_narrow]
        scratch = [pltpu.VMEM((rows, WIDE), BF), pltpu.VMEM((2 * width, rows), BF)]
        if finish:
            outs += [shape((two_rows // 2, width), BF)] * 2
            scratch += [pltpu.VMEM((two_rows, width), BF)]
        else:
            outs += [shape((2 * width, width), F32), shape((width, SLOT), F32)]
            outs += [shape((8, WIDE), F32), shape((width, WIDE), F32)]
        made = call(
            functools.partial(last_kernel, cell, cell > 0, finish),
            ins + carried + ([vec_mid] if finish else []),
            outs,
            scratch,
            flops=1,
        )
        local.append(made[0])
        carried = list(made[1:])
    keep, give = carried
    give, got_one = lax.optimization_barrier((give, got_one))
    other = swap(give, "core", 1)
    for step in depth_steps[1:]:
        own_one = tree_sum([own_one, got_one])
        got_one = swap(own_one, "z", step)
    own, pieces = divide(keep, other, ring)
    got, got_one = lax.optimization_barrier((swaps(pieces, PLANE), got_one))
    own = sum_steps(own, got)
    own, partial = lax.optimization_barrier((own, partial))
    received.append(returned(partial))
    got, received = lax.optimization_barrier((to_all(own, "z"), received))
    own = sum_steps(own, got)
    own_one = tree_sum([own_one, got_one])
    own = jnp.concatenate([own_one, own], axis=0)
    tokens_grad = call(
        functools.partial(finish_kernel, cells),
        [carriers[0]] + local + sum(received, []),
        [shape((cells, rows, width), F32)],
    )[0]
    got = to_all(own, PLANE)
    result = jnp.stack(results)
    got[1], tokens_grad, result = lax.optimization_barrier((got[1], tokens_grad, result))
    mine = [own] + [got[step] for step in sorted(got)]
    other = [swap(piece, "core", 1) for piece in mine]

    vector = shape((1, width), F32)
    made = call(
        functools.partial(unpack_kernel, ring),
        mine + other,
        [shape((width, width), F32), shape((width, hidden), F32), shape((hidden, width), F32)]
        + [shape((width, width), F32)] * 3
        + [vector] * 3
        + [shape((1, hidden), F32)]
        + [vector] * 6
        + [shape((1, 3), F32)],
        [pltpu.VMEM((one_rows, width), BF), pltpu.VMEM((two_rows, width), BF)],
    )
    dwo, dw1, dw2, dwq, dwk, dwv = made[:6]
    (
        gain_two_grad, shift_two_grad, bias_2_grad, bias_1_grad, gain_one_grad, shift_one_grad,
        bias_o_grad, bias_q_grad, bias_v_grad, mask_embed_grad, root_means,
    ) = [a.reshape(-1) for a in made[6:]]

    return (
        result,
        tokens_grad,
        mask_embed_grad,
        dwq,
        bias_q_grad,
        dwk,
        dwv,
        bias_v_grad,
        dwo,
        bias_o_grad,
        gain_one_grad,
        shift_one_grad,
        dw1,
        bias_1_grad,
        dw2,
        bias_2_grad,
        gain_two_grad,
        shift_two_grad,
        root_means,
    )


def solution(mesh):
    dp, seq = mesh.shape["dp"], mesh.shape["seq"]
    cut = jax.sharding.Mesh(mesh.devices.reshape(dp // 4, 2, 2, seq), ("z",) + NEAR)
    dp = ("z", "x", "core")
    split = P(dp, "seq", None)
    return jax.shard_map(
        body,
        mesh=cut,
        in_specs=(split, P(dp, "seq"), P(dp), split) + (P(),) * 16,
        out_specs=(split, split) + (P(),) * 17,
        check_vma=False,
    )
```

```python
import functools

import jax
import jax.numpy as jnp
from jax import lax
from jax.experimental import pallas as pl
from jax.experimental.pallas import tpu as pltpu
from jax.sharding import PartitionSpec as P

HEADS = 4
HEAD_DIM = 64
SLOT = 128
WIDE = HEADS * SLOT

EPSILON = 1e-05
NEGATIVE = -1e30
INV_ROOT_TWO_PI = 0.3989422804014327
BF = jnp.bfloat16
F32 = jnp.float32
VMEM_LIMIT = 16 * 1024 * 1024
MASK_ROWS = 16
PARTS = 2


def nn(left, right):
    return lax.dot_general(left, right, (((1,), (0,)), ((), ())), preferred_element_type=F32)


def nt(left, right):
    return lax.dot_general(left, right, (((1,), (1,)), ((), ())), preferred_element_type=F32)


def tn(left, right):
    return lax.dot_general(left, right, (((0,), (0,)), ((), ())), preferred_element_type=F32)


def lane_of(shape):
    return lax.broadcasted_iota(jnp.int32, shape, len(shape) - 1)


def row_of(shape):
    return lax.broadcasted_iota(jnp.int32, shape, len(shape) - 2)


def spread(matrix):
    pieces = []
    for pair in range(HEADS // 2):
        both = matrix[:, pair * SLOT : (pair + 1) * SLOT]
        first = lane_of(both.shape) < HEAD_DIM
        pieces.append(jnp.where(first, both, 0.0))
        pieces.append(jnp.where(first, pltpu.roll(both, HEAD_DIM, 1), 0.0))
    return jnp.concatenate(pieces, axis=1)


def joined(wide):
    pieces = []
    for pair in range(HEADS // 2):
        even = wide[:, 2 * pair * SLOT : (2 * pair + 1) * SLOT]
        odd = wide[:, (2 * pair + 1) * SLOT : (2 * pair + 2) * SLOT]
        pieces.append(jnp.where(lane_of(even.shape) < HEAD_DIM, even, pltpu.roll(odd, HEAD_DIM, 1)))
    return jnp.concatenate(pieces, axis=1)


def spread_rows(matrix):
    gap = jnp.zeros((SLOT - HEAD_DIM, matrix.shape[1]), matrix.dtype)
    pieces = []
    for head in range(HEADS):
        pieces += [matrix[head * HEAD_DIM : (head + 1) * HEAD_DIM], gap]
    return jnp.concatenate(pieces, axis=0)


def head_cols(head):
    return slice(head * SLOT, (head + 1) * SLOT)


def project_keys(x, w_all, bias_v, first_place, length, k_out, v_out):
    raw = nn(x, w_all[:, WIDE : 2 * WIDE])
    shut = lane_of(raw.shape) % SLOT == HEAD_DIM + 2
    shut &= row_of(raw.shape) + first_place >= length
    k_out[...] = jnp.where(shut, NEGATIVE, raw).astype(BF)
    one_row = lane_of((1, WIDE)) % SLOT
    ones_row = jnp.where((one_row == HEAD_DIM) | (one_row == HEAD_DIM + 1), 1.0, 0.0)
    v_out[...] = (nn(x, w_all[:, 2 * WIDE :]) + (spread(bias_v) + ones_row)).astype(BF)


def attend(queries, keys, values, kept):
    scores = nt(queries, keys)
    peak = jnp.max(scores, axis=1, keepdims=True)
    kept[...] = jnp.exp(scores - peak).astype(BF)
    return nn(kept[...], values), jnp.broadcast_to(peak, (peak.shape[0], SLOT))


def kept_rows(head, rows):
    return slice(head * rows, (head + 1) * rows)


def owner_of(distance, ring):
    return lax.rem(lax.axis_index("seq") - distance + ring, ring)


def select_kernel(
    cell, carry, tokens, masks, embed, stream_out, low_out, *refs
):
    held, mask_held, embed_held, arrived = refs[-4:]
    copies = [
        pltpu.make_async_copy(source, target, arrived.at[which])
        for which, (source, target) in enumerate(
            ((tokens.at[cell], held), (masks, mask_held), (embed, embed_held))
        )
    ]
    for copy in copies:
        copy.start()
    for copy in copies[1:]:
        copy.wait()
    rows, width = held.shape
    mask = mask_held[cell : cell + 1, :].astype(F32)
    column = jnp.transpose(jnp.broadcast_to(mask, (8, rows)))[:, :1]
    copies[0].wait()
    stream = jnp.where(column == 1.0, embed_held[...], held[...])
    stream_out[...] = stream
    low_out[...] = stream.astype(BF)
    if not carry:
        return
    carrier_out = refs[0]
    pieces = [
        mask_held[which : which + 1, at : at + width]
        for which in range(masks.shape[0])
        for at in range(0, rows, width)
    ]
    pieces.append(jnp.zeros((MASK_ROWS - len(pieces), width), masks.dtype))
    carrier_out[:rows, :] = stream.astype(BF)
    carrier_out[rows:, :] = jnp.concatenate(pieces, axis=0).astype(F32).astype(BF)


def mask_of(carrier, cell):
    rows = carrier.shape[0] - MASK_ROWS
    count = rows // carrier.shape[1]
    under = carrier[rows:, :].astype(F32)
    first = cell * count
    return jnp.concatenate([under[first + at : first + at + 1] for at in range(count)], axis=1)


def first_kernel(cells, lengths, *refs):
    xs, refs = refs[:cells], refs[cells:]
    wq, wk, wv, bias_q, bias_v = refs[:5]
    outs, (w_all, w_kv) = refs[5:-2], refs[-2:]
    w_all[:, :WIDE] = spread(wq[...] * HEAD_DIM ** (-0.5)).astype(BF)
    w_all[:, WIDE : 2 * WIDE] = spread(wk[...]).astype(BF)
    w_all[:, 2 * WIDE :] = spread(wv[...]).astype(BF)
    rows = outs[0].shape[0]
    first_place = lax.axis_index("seq") * rows
    one_row = lane_of((1, WIDE)) % SLOT
    bias = spread(bias_q[...]) * HEAD_DIM ** (-0.5) + jnp.where(one_row == HEAD_DIM + 2, 1.0, 0.0)
    for cell in range(cells):
        x = xs[cell].at[:rows]
        q_out, k_out, v_out, kept_out, state_out, peak_out = outs[6 * cell : 6 * cell + 6]
        q_out[...] = (nn(x[...], w_all[:, :WIDE]) + bias).astype(BF)
        project_keys(x[...], w_all, bias_v[...], first_place, lengths[cell], k_out, v_out)
        for head in range(HEADS):
            cols = head_cols(head)
            state_out[:, cols], peak_out[:, cols] = attend(
                q_out[:, cols], k_out[:, cols], v_out[:, cols], kept_out.at[kept_rows(head, rows)]
            )
    width = wk.shape[1]
    w_kv[:, :width] = wk[...].astype(BF)
    w_kv[:, width:] = wv[...].astype(BF)


def more_kernel(
    cell, distance, ring,
    lengths, x, q, state, peak, w_all, bias_v,
    k_out, v_out, kept_out, own_out, state_out, peak_out,
):
    rows = q.shape[0]
    first_place = owner_of(distance, ring) * rows
    project_keys(x[:rows, :], w_all, bias_v[...], first_place, lengths[cell], k_out, v_out)
    for head in range(HEADS):
        cols = head_cols(head)
        total, own = attend(
            q[:, cols], k_out[:, cols], v_out[:, cols], kept_out.at[kept_rows(head, rows)]
        )
        top = jnp.maximum(peak[:, cols], own)
        own_out[:, cols] = own
        peak_out[:, cols] = top
        state_out[:, cols] = state[:, cols] * jnp.exp(peak[:, cols] - top)
        state_out[:, cols] += total * jnp.exp(own - top)


def norm_parts(matrix):
    row_mean = jnp.mean(matrix, axis=1, keepdims=True)
    centred = matrix - row_mean
    row_var = jnp.mean(centred * centred, axis=1, keepdims=True)
    inverse = lax.rsqrt(row_var + EPSILON)
    return centred * inverse, inverse


def norm_back(grad, unit, inverse):
    shift = jnp.mean(grad, axis=1, keepdims=True)
    scale = jnp.mean(grad * unit, axis=1, keepdims=True)
    return (grad - shift - unit * scale) * inverse


def eight_sum(matrix):
    return jnp.sum(matrix.reshape(-1, 8, matrix.shape[1]), axis=0)


def inverse_of(value):
    guess = pl.reciprocal(value, approx=True)
    return guess * (2.0 - value * guess)


def gelu_parts(pre):
    bell = jnp.exp(pre * pre * (-0.5))
    t = inverse_of(1.0 + (0.3275911 * 0.7071067811865476) * jnp.abs(pre))
    poly = 0.5 * 1.061405429
    for factor in (-1.453152027, 1.421413741, -0.284496736, 0.254829592):
        poly = poly * t + 0.5 * factor
    tail = poly * t * bell
    half = jnp.where(pre >= 0.0, 1.0 - tail, tail)
    return pre * half, half + pre * bell * INV_ROOT_TWO_PI


def halve(pack, keep_out, give_out):
    half = keep_out.shape[0]
    core = lax.axis_index("core")
    keep_out[...] = pack[pl.ds(pl.multiple_of(core * half, half), half), :]
    give_out[...] = pack[pl.ds(pl.multiple_of((1 - core) * half, half), half), :]


def my_plane(ring):
    return lax.axis_index("x") * ring + lax.axis_index("seq")


def halve(pack, keep_out, give_out):
    half = keep_out.shape[0]
    core = lax.axis_index("core")
    keep_out[...] = pack[pl.ds(pl.multiple_of(core * half, half), half), :]
    give_out[...] = pack[pl.ds(pl.multiple_of((1 - core) * half, half), half), :]


def near_bits(ring, core):
    bits = [("seq", 1 << i) for i in range(ring.bit_length() - 1)]
    return bits + [("x", 1)] if core else [("x", 1)] + bits


def my_side(ring, step):
    sides = []
    for core in range(2):
        axis, bit = near_bits(ring, core)[step]
        sides.append(lax.rem(lax.axis_index(axis) // bit, 2))
    return jnp.where(lax.axis_index("core") == 0, sides[0], sides[1])


def halve_kernel(ring, step, keep, received, keep_out, give_out):
    half = keep_out.shape[0]
    side = my_side(ring, step)
    for out, place in ((keep_out, side), (give_out, 1 - side)):
        at = pl.ds(pl.multiple_of(place * half, half), half)
        out[...] = (keep[at, :].astype(F32) + received[at, :].astype(F32)).astype(BF)


def join_kernel(ring, step, mine, other, out):
    rows = mine.shape[0]
    side = my_side(ring, step)
    out[pl.ds(pl.multiple_of(side * rows, rows), rows), :] = mine[...]
    out[pl.ds(pl.multiple_of((1 - side) * rows, rows), rows), :] = other[...]


def divide_kernel(ring, keep, received, own_out, *give_outs):
    piece = own_out.shape[0]
    plane = my_plane(ring)
    for step, out in enumerate((own_out,) + give_outs):
        at = pl.ds(pl.multiple_of((plane ^ step) * piece, piece), piece)
        out[...] = (keep[at, :].astype(F32) + received[at, :].astype(F32)).astype(BF)


def place_pieces(ring, mine, other, pack_one, pack_two):
    plane, core = my_plane(ring), lax.axis_index("core")
    for step in range(2 * ring):
        start = 0
        for pack in (pack_one, pack_two):
            piece = pack.shape[0] // (4 * ring)
            for half, sources in ((core, mine), (1 - core, other)):
                at = pl.multiple_of((half * 2 * ring + (plane ^ step)) * piece, piece)
                pack[pl.ds(at, piece), :] = sources[step][start : start + piece, :]
            start += piece


def middle_kernel(
    cell, ring, carry, finish,
    lengths, x, q, state, peak, stream, cotangent, w_all, bias_v, wo_in, bias_o, gain_one,
    shift_one, w1_in, bias_1, w2_in, bias_2, gain_two, shift_two, *refs,
):
    count = ring - 1 if ring > 2 else 0
    before, refs = refs[:count], refs[count:]
    if carry:
        dwo_in, dw1_in, dw2_in, vec_in = refs[:4]
        refs = refs[4:]
    do_outs, refs = refs[:ring], refs[ring:]
    result_out, k_out, v_out, kept_out, x_out, first_out, vec_out = refs[:7]
    refs = refs[7:]
    if carry:
        wo, w1, w2 = wo_in, w1_in, w2_in
    else:
        wo, w1, w2 = refs[:3]
        refs = refs[3:]
        wo[...] = spread_rows(wo_in[...].astype(BF))
        w1[...] = w1_in[...].astype(BF)
        w2[...] = w2_in[...].astype(BF)
    if finish:
        keep_out, give_out = refs[:2]
        refs = refs[2:]
    else:
        dwo_out, dw1_out, dw2_out = refs[:3]
        refs = refs[3:]
    scales, refs = refs[:ring], refs[ring:]
    (
        attended_wide, attended_low, normed_low, active_low, hidden_low, branch_low, attn_low,
        unit_one, inverse_one, narrow_b, wide_b, acc, *pack_ref,
    ) = refs
    rows, width = stream.shape
    x_out[...] = x[:rows, :]
    hidden = w1.shape[1]
    length = lengths[cell]
    first_place = owner_of(ring - 1, ring) * rows
    project_keys(x[:rows, :], w_all, bias_v[...], first_place, length, k_out, v_out)
    for head in range(HEADS):
        cols = head_cols(head)
        total, own = attend(
            q[:, cols], k_out[:, cols], v_out[:, cols], kept_out.at[kept_rows(head, rows)]
        )
        top = jnp.maximum(peak[:, cols], own)
        old_scale, own_scale = jnp.exp(peak[:, cols] - top), jnp.exp(own - top)
        both = state[:, cols] * old_scale + total * own_scale
        inverse = inverse_of(both[:, HEAD_DIM : HEAD_DIM + 1])
        attended = both * inverse
        attended_wide[:, cols] = attended
        attended_low[:, cols] = attended.astype(BF)
        scales[ring - 1][:, cols] = own_scale * inverse
        if ring == 2:
            scales[0][:, cols] = old_scale * inverse
        else:
            for block in range(ring - 1):
                scales[block][:, cols] = jnp.exp(before[block][:, cols] - top) * inverse

    my_place = lax.axis_index("seq") * rows

    def part_steps(part):
        count = rows // PARTS
        span = slice(part * count, (part + 1) * count)
        place = row_of((count, width)) + (my_place + part * count)
        valid = jnp.where(place < length, 1.0, 0.0)

        def add(slot, matrix):
            sums = eight_sum(matrix)
            acc[slot] = acc[slot] + sums if part else sums

        attn_out = nn(attended_low[span, :], wo[...]) + bias_o[...]
        unit, inverse = norm_parts(stream[span, :] + attn_out)
        unit_one[span, :] = unit
        inverse_one[span, :] = jnp.broadcast_to(inverse, (count, SLOT))
        normed = unit * gain_one[...] + shift_one[...]
        narrow_b[span, :] = normed
        normed_low[span, :] = normed.astype(BF)
        add(8, stream[span, :] * stream[span, :] * valid)
        add(9, attn_out * attn_out * valid)
        yield
        active, slope = gelu_parts(nn(normed_low[span, :], w1[...]) + bias_1[...])
        active_low[span, :] = active.astype(BF)
        wide_b[span, :] = slope
        yield
        branch = nn(active_low[span, :], w2[...]) + bias_2[...]
        unit, inverse = norm_parts(narrow_b[span, :] + branch)
        result_out[span, :] = unit * gain_two[...] + shift_two[...]
        grad_result = cotangent[span, :] * valid
        grad_second = norm_back(grad_result * gain_two[...], unit, inverse)
        narrow_b[span, :] = grad_second
        branch_low[span, :] = grad_second.astype(BF)
        add(0, grad_result * unit)
        add(1, grad_result)
        add(10, branch * branch * valid)
        yield
        hidden_low[span, :] = (nt(branch_low[span, :], w2[...]) * wide_b[span, :]).astype(BF)
        yield
        grad_normed = narrow_b[span, :] + nt(hidden_low[span, :], w1[...])
        unit = unit_one[span, :]
        grad_first = norm_back(grad_normed * gain_one[...], unit, inverse_one[span, :1])
        first_out[span, :] = grad_first
        attn_low[span, :] = grad_first.astype(BF)
        add(5, grad_normed * unit)
        add(6, grad_normed)
        yield
        do_wide = nt(attn_low[span, :], wo[...]).astype(BF).astype(F32)
        for head in range(HEADS):
            cols = head_cols(head)
            do_head = do_wide[:, cols]
            row_dot = jnp.sum(do_head * attended_wide[span, cols], axis=1, keepdims=True)
            lane = lane_of(do_head.shape)
            for scale, do_out in zip(scales, do_outs):
                factor = scale[span, cols]
                dot = -row_dot * factor
                rest = dot - dot.astype(BF).astype(F32)
                scaled = jnp.where(lane == HEAD_DIM, dot, do_head * factor)
                do_out[span, cols] = jnp.where(lane == HEAD_DIM + 1, rest, scaled).astype(BF)
        yield

    parts = [part_steps(part) for part in range(PARTS)]
    for _ in range(6):
        for part in parts:
            next(part)

    ones = jnp.ones((8, rows), BF)
    hidden_sum = nn(ones, hidden_low[...])[0:1]
    known = {
        2: nn(ones, branch_low[...])[0:1],
        3: hidden_sum[:, :width],
        4: hidden_sum[:, width:],
        7: nn(ones, attn_low[...])[0:1],
        11: jnp.full((1, width), jnp.clip(length - my_place, 0, rows).astype(F32)),
    }
    sums = [
        known[slot] if slot in known else jnp.sum(acc[slot], axis=0, keepdims=True)
        for slot in range(12)
    ]
    vec = jnp.concatenate(sums + [jnp.zeros((4, width), F32)], axis=0)
    vec_out[...] = vec + vec_in[...] if carry else vec

    dwo = tn(attn_low[...], attended_low[...])
    dw1 = tn(normed_low[...], hidden_low[...])
    dw2 = tn(branch_low[...], active_low[...])
    if carry:
        dwo += dwo_in[...]
        dw1 += dw1_in[...]
        dw2 += dw2_in[...]
    if not finish:
        dwo_out[...] = dwo
        dw1_out[...] = dw1
        dw2_out[...] = dw2
        return
    (pack,) = pack_ref
    pack[:width, :] = joined(dwo).astype(BF)
    pack[width : 2 * width, :] = dw1[:, :width].astype(BF)
    pack[2 * width : 3 * width, :] = dw1[:, width:].astype(BF)
    for at in range(0, hidden, width):
        pack[3 * width + at : 4 * width + at, :] = dw2[:, at : at + width].astype(BF)
    used = 3 * width + hidden
    if pack.shape[0] > used:
        pack[used:, :] = jnp.zeros((pack.shape[0] - used, width), BF)
    halve(pack, keep_out, give_out)


def head_grads(q, k, v, do, kept):
    score_grad = (kept.astype(F32) * nt(do, v)).astype(BF)
    return (
        nn(score_grad, k),
        tn(q[:, :HEAD_DIM], score_grad),
        tn(do[:, :HEAD_DIM], kept),
    )


def all_heads(q, k, v, do, kept, low, put_query):
    rows = q.shape[0]
    for head in range(HEADS):
        cols = head_cols(head)
        dq, dk, dv = head_grads(
            q[:, cols], k[:, cols], v[:, cols], do[:, cols], kept[kept_rows(head, rows), :]
        )
        put_query(cols, dq)
        low[head * HEAD_DIM : (head + 1) * HEAD_DIM, :] = dk.astype(BF)
        at = (HEADS + head) * HEAD_DIM
        low[at : at + HEAD_DIM, :] = dv.astype(BF)


def masked_sum(carrier, cell, grad_bf):
    mask = mask_of(carrier, cell)
    picked = jnp.broadcast_to(mask, (8, mask.shape[1])).astype(BF)
    return nn(picked, grad_bf)[0:1]


def value_sums(low):
    half = low.shape[0] // 2
    sums = jnp.sum(low[half:, :].astype(F32), axis=1, keepdims=True)
    return jnp.broadcast_to(sums, (half, SLOT))


def block_kernel(cell, carry_dq, carry, sent, carrier, q, do, k, v, kept, w_kv, *refs):
    if carry_dq:
        dq_in, refs = refs[0], refs[1:]
    if carry:
        (dw_in, sum_in, vec_in), refs = refs[:3], refs[3:]
    dq_out, dx_out, dw_out, sum_out, vec_out, low = refs

    def put_query(cols, dq):
        dq_out[:, cols] = dq + dq_in[:, cols] if carry_dq else dq

    all_heads(q, k, v, do, kept, low, put_query)
    x = sent[: q.shape[0], :]
    dx_bf = jnp.transpose(nn(w_kv[...], low[...])).astype(BF)
    dx_out[...] = dx_bf
    dw = nn(low[...], x)
    dw_out[...] = dw + dw_in[...] if carry else dw
    sums = value_sums(low)
    sum_out[...] = sums + sum_in[...] if carry else sums
    vec_out[...] = vec_in[...] if carry else jnp.zeros_like(vec_out)
    vec_out[0:1, : x.shape[1]] += masked_sum(carrier[...], cell, dx_bf)


def last_kernel(
    cell, carry, finish,
    sent, carrier, q, do, k, v, kept, w_all, w_kv, first, dq_in, dw_in, sum_in, vec_in, *refs
):
    if carry:
        dwq_in, refs = refs[0], refs[1:]
    if finish:
        vec_mid, dx_out, keep_out, give_out, low_q, low, pack = refs
    else:
        dx_out, dw_out, sum_out, vec_out, dwq_out, low_q, low = refs

    def put_query(cols, dq):
        low_q[:, cols] = ((dq + dq_in[:, cols]) * HEAD_DIM ** (-0.5)).astype(BF)

    all_heads(q, k, v, do, kept, low, put_query)
    grads = first[...] + nt(low_q[...], w_all[:, :WIDE]) * HEAD_DIM**0.5
    grads += jnp.transpose(nn(w_kv[...], low[...]))
    dx_out[...] = grads
    width = grads.shape[1]
    x = sent[: q.shape[0], :]
    dwq = tn(x, low_q[...])
    dw = nn(low[...], x) + dw_in[...]
    sum_q = jnp.sum(low_q[...].astype(F32), axis=0, keepdims=True) + vec_in[1:2, :]
    sum_v = value_sums(low) + sum_in[...]
    sum_mask = masked_sum(carrier[...], cell, grads.astype(BF)) + vec_in[0:1, :width]
    if carry:
        dwq += dwq_in[...]
    if not finish:
        dwq_out[...] = dwq
        dw_out[...] = dw
        sum_out[...] = sum_v
        vec_out[...] = jnp.zeros_like(vec_out)
        vec_out[0:1, :width] = sum_mask
        vec_out[1:2, :] = sum_q
        return
    pack[:width, :] = joined(dwq).astype(BF)
    pack[width : 3 * width, :] = dw.astype(BF)
    rows = jnp.concatenate(
        [
            vec_mid[:12, :],
            joined(sum_q),
            jnp.transpose(sum_v)[0:1, :],
            sum_mask,
            jnp.zeros((1, width), F32),
        ],
        axis=0,
    )
    high = rows.astype(BF)
    pack[3 * width : 3 * width + 16, :] = high
    pack[3 * width + 16 : 3 * width + 32, :] = (rows - high.astype(F32)).astype(BF)
    used = 3 * width + 32
    if pack.shape[0] > used:
        pack[used:, :] = jnp.zeros((pack.shape[0] - used, width), BF)
    halve(pack, keep_out, give_out)


def unpack_kernel(ring, *refs):
    mine, other, refs = refs[: 2 * ring], refs[2 * ring : 4 * ring], refs[4 * ring :]
    dwo_out, dw1_out, dw2_out, dwq_out, dwk_out, dwv_out = refs[:6]
    outs, pack_one, pack = refs[6:-2], refs[-2], refs[-1]
    place_pieces(ring, mine, other, pack_one, pack)
    width = pack.shape[1]
    dwo_out[...] = jnp.transpose(pack_one[:width, :].astype(F32))
    dw1_out[:, :width] = pack_one[width : 2 * width, :].astype(F32)
    dw1_out[:, width:] = pack_one[2 * width : 3 * width, :].astype(F32)
    for at in range(0, dw2_out.shape[0], width):
        dw2_out[at : at + width, :] = jnp.transpose(
            pack_one[3 * width + at : 4 * width + at, :].astype(F32)
        )
    dwq_out[...] = pack[:width, :].astype(F32)
    dwk_out[...] = jnp.transpose(pack[width : 2 * width, :].astype(F32))
    dwv_out[...] = jnp.transpose(pack[2 * width : 3 * width, :].astype(F32))
    vec = pack[3 * width : 3 * width + 16, :].astype(F32)
    vec += pack[3 * width + 16 : 3 * width + 32, :].astype(F32)
    for out, row in zip(outs, (0, 1, 2, (3, 4), 5, 6, 7, 12, 13, 14)):
        if isinstance(row, tuple):
            out[:, :width] = vec[row[0] : row[0] + 1]
            out[:, width:] = vec[row[1] : row[1] + 1]
        else:
            out[...] = vec[row : row + 1]
    squares = jnp.sum(vec[8:16], axis=1, keepdims=True)
    count = vec[11:12, 0:1]
    means = jnp.sqrt(squares / (count * width))
    lane = lane_of((1, 3))
    outs[10][...] = jnp.where(
        lane == 0, means[0:1], jnp.where(lane == 1, means[1:2], means[2:3])
    )


def finish_kernel(cells, carrier, *refs):
    local, received, out = refs[:cells], refs[cells:-1], refs[-1]
    rows, count = local[0].shape[0], len(received) // cells
    for cell in range(cells):
        grads = local[cell][...]
        for piece in received[cell * count : (cell + 1) * count]:
            grads += piece[...].astype(F32)
        mask = jnp.broadcast_to(mask_of(carrier[...], cell), (8, rows))
        out[cell] = jnp.where(jnp.transpose(mask)[:, :1] == 1.0, 0.0, grads)


def call(kernel, ins, outs, scratch=(), flops=0):
    moved = sum(a.size * a.dtype.itemsize for a in ins) + sum(
        s.size * s.dtype.itemsize for s in outs
    )
    vmem = pl.BlockSpec(memory_space=pltpu.VMEM)
    smem = pl.BlockSpec(memory_space=pltpu.SMEM)
    return pl.pallas_call(
        kernel,
        in_specs=[smem if a.ndim == 1 else vmem for a in ins],
        out_specs=[vmem] * len(outs),
        out_shape=outs,
        scratch_shapes=list(scratch),
        compiler_params=pltpu.CompilerParams(vmem_limit_bytes=VMEM_LIMIT),
        cost_estimate=pl.CostEstimate(
            flops=flops, bytes_accessed=moved if flops != 1 else 1, transcendentals=0
        ),
    )(*ins)


def send(block, distance, ring):
    route = [(i, (i + distance) % ring) for i in range(ring)]
    return lax.ppermute(block, "seq", route)


NEAR = ("x", "core", "seq")
PLANE = ("x", "seq")


def swap(block, axes, step):
    return lax.ppermute(block, axes, [(i, i ^ step) for i in range(lax.axis_size(axes))])


def tree_sum(blocks):
    blocks = [block.astype(F32) for block in blocks]
    while len(blocks) > 1:
        blocks = [a + b for a, b in zip(blocks[::2], blocks[1::2])]
    return blocks[0].astype(BF)


def swaps(blocks, axes):
    return {step: swap(blocks[step], axes, step) for step in sorted(blocks, reverse=True)}


def sum_steps(own, got):
    return tree_sum([own] + [got[step] for step in sorted(got)])


def divide(keep, received, ring):
    half, width = keep.shape
    piece = jax.ShapeDtypeStruct((half // (2 * ring), width), BF)
    own, *pieces = call(
        functools.partial(divide_kernel, ring), [keep, received], [piece] * (2 * ring)
    )
    return own, dict(enumerate(pieces, 1))


def to_all(block, axes):
    return swaps({step: block for step in range(1, lax.axis_size(axes))}, axes)


def padded(rows, pieces):
    piece = -(-rows // pieces)
    return -(-piece // 16) * 16 * pieces


def body(
    tokens, masked, lengths, cotangent, mask_embed, query_weight, query_bias, key_weight,
    value_weight, value_bias, out_weight, out_bias, gain_one, shift_one, expand_weight,
    expand_bias, reduce_weight, reduce_bias, gain_two, shift_two,
):
    cells, rows, width = tokens.shape
    hidden = expand_weight.shape[1]
    ring = lax.axis_size("seq")

    def row(vector):
        return vector.reshape(1, -1)

    shape = jax.ShapeDtypeStruct
    low_wide, full_wide = shape((rows, WIDE), BF), shape((rows, WIDE), F32)
    low_narrow, full_narrow = shape((rows, width), BF), shape((rows, width), F32)
    weights = shape((HEADS * rows, rows), BF)
    score_flops = 2 * rows * rows * HEADS * 256

    stream, x_moved, x_low = [], [], []
    vmem = pl.BlockSpec(memory_space=pltpu.VMEM)
    masks = masked
    for cell in range(cells):
        carry = cell == cells - 1
        outs = [full_narrow, low_narrow] + [shape((rows + MASK_ROWS, width), BF)] * carry
        made = pl.pallas_call(
            functools.partial(select_kernel, cell, carry),
            in_specs=[pl.BlockSpec(memory_space=pltpu.HBM)] * 3,
            out_specs=[vmem] * len(outs),
            out_shape=outs,
            scratch_shapes=[
                pltpu.VMEM((rows, width), F32),
                pltpu.VMEM((cells, rows), jnp.int32),
                pltpu.VMEM((1, width), F32),
                pltpu.SemaphoreType.DMA((3,)),
            ],
            compiler_params=pltpu.CompilerParams(vmem_limit_bytes=VMEM_LIMIT),
        )(
            *[
                pltpu.with_memory_space_constraint(a, pltpu.HBM)
                for a in (tokens, masks, row(mask_embed))
            ]
        )
        stream.append(made[0])
        x_low.append(made[1])
        x_moved.append([made[-1]])
        if cell == 0:
            x_moved[0] += [send(x_moved[0][0], t, ring) for t in range(1, ring)]
        masks, x_low[cell] = lax.optimization_barrier((masks, x_low[cell]))

    made = call(
        functools.partial(first_kernel, cells),
        [lengths]
        + x_low
        + [query_weight, key_weight, value_weight, row(query_bias), row(value_bias)],
        [low_wide, low_wide, low_wide, weights, full_wide, full_wide] * cells
        + [
            shape((width, 3 * WIDE), BF),
            shape((width, 2 * width), BF),
        ],
        flops=2 * cells * score_flops,
    )
    w_all, w_kv = made[-2:]
    wo, w1, w2 = out_weight, expand_weight, reduce_weight
    low_weights = [
        shape((WIDE, width), BF), shape((width, hidden), BF), shape((hidden, width), BF)
    ]
    bias_v = row(value_bias)
    for cell in range(1, cells):
        sent, w_all = lax.optimization_barrier((x_moved[cell][0], w_all))
        x_moved[cell] += [send(sent, t, ring) for t in range(1, ring)]
    carriers = list(x_moved[-1])
    keys, values, kept, queries, states, peaks = [], [], [], [], [], []
    for cell in range(cells):
        q, k, v, p, state, peak = made[6 * cell : 6 * cell + 6]
        queries.append(q)
        keys.append([k])
        values.append([v])
        kept.append([p])
        own_peaks = [peak]
        for t in range(1, ring - 1):
            k, v, p, own, state, peak = call(
                functools.partial(more_kernel, cell, t, ring),
                [lengths, x_moved[cell][t], q, state, peak, w_all, bias_v],
                [low_wide, low_wide, weights, full_wide, full_wide, full_wide],
                flops=2 * score_flops,
            )
            keys[cell].append(k)
            values[cell].append(v)
            kept[cell].append(p)
            own_peaks.append(own)
        states.append([state, peak])
        peaks.append(own_peaks if ring > 2 else [])

    one_rows = padded(3 * width + hidden, lax.axis_size(NEAR))
    results, firsts, grads_out = [], [], []
    carried, carried_back, received = [], [], []
    dq = [None] * cells

    def backward_of_blocks(cell):
        nonlocal carried_back
        partial = []
        for t in range(1, ring):
            ins = [
                x_moved[cell][t], carriers[t], queries[cell], grads_out[cell][t],
                keys[cell][t], values[cell][t], kept[cell][t], w_kv,
            ]
            ins += ([dq[cell]] if t > 1 else []) + carried_back
            dq[cell], dx, *carried_back = call(
                functools.partial(block_kernel, cell, t > 1, bool(carried_back)),
                ins,
                [
                    full_wide,
                    low_narrow,
                    shape((2 * width, width), F32),
                    shape((width, SLOT), F32),
                    shape((8, WIDE), F32),
                ],
                [pltpu.VMEM((2 * width, rows), BF)],
                flops=5 * score_flops,
            )
            partial.append(dx)
        return partial

    def returned(partial):
        return [send(dx, -t, ring) for t, dx in enumerate(partial, 1)]

    for cell in range(cells):
        finish = cell == cells - 1
        if cell > 0:
            partial = backward_of_blocks(cell - 1)
            states[cell], partial = lax.optimization_barrier((states[cell], partial))
            received.append(returned(partial))
        outs = [low_wide] * ring
        outs += [full_narrow, low_wide, low_wide, weights, low_narrow, full_narrow]
        outs += [shape((16, width), F32)] + (low_weights if cell == 0 else [])
        if finish:
            outs += [shape((one_rows // 2, width), BF)] * 2
        else:
            outs += [shape((width, WIDE), F32)] + [shape((width, hidden), F32)] * 2
        scratch = [pltpu.VMEM((rows, WIDE), F32)] * ring + [
            pltpu.VMEM((rows, WIDE), F32),
            pltpu.VMEM((rows, WIDE), BF),
            pltpu.VMEM((rows, width), BF),
            pltpu.VMEM((rows, hidden), BF),
            pltpu.VMEM((rows, hidden), BF),
            pltpu.VMEM((rows, width), BF),
            pltpu.VMEM((rows, width), BF),
            pltpu.VMEM((rows, width), F32),
            pltpu.VMEM((rows, SLOT), F32),
            pltpu.VMEM((rows, width), F32),
            pltpu.VMEM((rows, hidden), F32),
            pltpu.VMEM((12, 8, width), F32),
        ]
        if finish:
            scratch.append(pltpu.VMEM((one_rows, width), BF))
        made = call(
            functools.partial(middle_kernel, cell, ring, bool(carried), finish),
            [
                lengths, x_moved[cell][ring - 1], queries[cell], *states[cell], stream[cell],
                cotangent[cell], w_all, bias_v, wo, row(out_bias), row(gain_one), row(shift_one),
                w1, row(expand_bias), w2, row(reduce_bias), row(gain_two), row(shift_two),
            ]
            + peaks[cell]
            + carried,
            outs,
            scratch,
            flops=7 * score_flops,
        )
        grads_out.append(made[:ring])
        result, k, v, p, x_moved[cell][ring - 1], first, vec_mid = made[ring : ring + 7]
        made = made[ring + 7 :]
        if cell == 0:
            wo, w1, w2 = made[:3]
            made = made[3:]
        results.append(result)
        keys[cell].append(k)
        values[cell].append(v)
        kept[cell].append(p)
        firsts.append(first)
        carried = list(made) + [vec_mid]
    keep, give = made
    received_one = swap(give, "core", 1)
    queries[-1], received = lax.optimization_barrier((queries[-1], received))
    partial = backward_of_blocks(cells - 1)
    own_one, pieces = divide(keep, received_one, ring)
    carried, partial, own_one, pieces = lax.optimization_barrier(
        (carried_back, partial, own_one, pieces)
    )
    got_one = swaps(pieces, PLANE)

    two_rows = padded(3 * width + 32, lax.axis_size(NEAR))
    local = []
    depth_steps = [1 << i for i in range(lax.axis_size("z").bit_length() - 1)]
    for cell in range(cells):
        finish = cell == cells - 1
        if finish:
            carried, got_one = lax.optimization_barrier((carried, got_one))
            own_one = sum_steps(own_one, got_one)
            got_one = swap(own_one, "z", depth_steps[0])
        ins = [
            x_moved[cell][0], carriers[0], queries[cell], grads_out[cell][0], keys[cell][0],
            values[cell][0], kept[cell][0], w_all, w_kv, firsts[cell], dq[cell],
        ]
        outs = [full_narrow]
        scratch = [pltpu.VMEM((rows, WIDE), BF), pltpu.VMEM((2 * width, rows), BF)]
        if finish:
            outs += [shape((two_rows // 2, width), BF)] * 2
            scratch += [pltpu.VMEM((two_rows, width), BF)]
        else:
            outs += [shape((2 * width, width), F32), shape((width, SLOT), F32)]
            outs += [shape((8, WIDE), F32), shape((width, WIDE), F32)]
        made = call(
            functools.partial(last_kernel, cell, cell > 0, finish),
            ins + carried + ([vec_mid] if finish else []),
            outs,
            scratch,
            flops=1,
        )
        local.append(made[0])
        carried = list(made[1:])
    keep, give = carried
    give, got_one = lax.optimization_barrier((give, got_one))
    other = swap(give, "core", 1)
    for step in depth_steps[1:]:
        own_one = tree_sum([own_one, got_one])
        got_one = swap(own_one, "z", step)
    own, pieces = divide(keep, other, ring)
    got, got_one = lax.optimization_barrier((swaps(pieces, PLANE), got_one))
    own = sum_steps(own, got)
    own, partial = lax.optimization_barrier((own, partial))
    received.append(returned(partial))
    got, received = lax.optimization_barrier((to_all(own, "z"), received))
    own = sum_steps(own, got)
    own_one = tree_sum([own_one, got_one])
    own = jnp.concatenate([own_one, own], axis=0)
    tokens_grad = call(
        functools.partial(finish_kernel, cells),
        [carriers[0]] + local + sum(received, []),
        [shape((cells, rows, width), F32)],
    )[0]
    got = to_all(own, PLANE)
    result = jnp.stack(results)
    got[1], tokens_grad, result = lax.optimization_barrier((got[1], tokens_grad, result))
    mine = [own] + [got[step] for step in sorted(got)]
    other = [swap(piece, "core", 1) for piece in mine]

    vector = shape((1, width), F32)
    made = call(
        functools.partial(unpack_kernel, ring),
        mine + other,
        [shape((width, width), F32), shape((width, hidden), F32), shape((hidden, width), F32)]
        + [shape((width, width), F32)] * 3
        + [vector] * 3
        + [shape((1, hidden), F32)]
        + [vector] * 6
        + [shape((1, 3), F32)],
        [pltpu.VMEM((one_rows, width), BF), pltpu.VMEM((two_rows, width), BF)],
    )
    dwo, dw1, dw2, dwq, dwk, dwv = made[:6]
    (
        gain_two_grad, shift_two_grad, bias_2_grad, bias_1_grad, gain_one_grad, shift_one_grad,
        bias_o_grad, bias_q_grad, bias_v_grad, mask_embed_grad, root_means,
    ) = [a.reshape(-1) for a in made[6:]]

    return (
        result,
        tokens_grad,
        mask_embed_grad,
        dwq,
        bias_q_grad,
        dwk,
        dwv,
        bias_v_grad,
        dwo,
        bias_o_grad,
        gain_one_grad,
        shift_one_grad,
        dw1,
        bias_1_grad,
        dw2,
        bias_2_grad,
        gain_two_grad,
        shift_two_grad,
        root_means,
    )


def solution(mesh):
    dp, seq = mesh.shape["dp"], mesh.shape["seq"]
    cut = jax.sharding.Mesh(mesh.devices.reshape(dp // 4, 2, 2, seq), ("z",) + NEAR)
    dp = ("z", "x", "core")
    split = P(dp, "seq", None)
    return jax.shard_map(
        body,
        mesh=cut,
        in_specs=(split, P(dp, "seq"), P(dp), split) + (P(),) * 16,
        out_specs=(split, split) + (P(),) * 17,
        check_vma=False,
    )
```

```python
import functools

import jax
import jax.numpy as jnp
from jax import lax
from jax.experimental import pallas as pl
from jax.experimental.pallas import tpu as pltpu
from jax.sharding import PartitionSpec as P

HEADS = 4
HEAD_DIM = 64
SLOT = 128
WIDE = HEADS * SLOT

EPSILON = 1e-05
NEGATIVE = -1e30
INV_ROOT_TWO_PI = 0.3989422804014327
LOG2_E = 1.4426950408889634
BF = jnp.bfloat16
F32 = jnp.float32
VMEM_LIMIT = 16 * 1024 * 1024
MASK_ROWS = 16


def nn(left, right):
    return lax.dot_general(left, right, (((1,), (0,)), ((), ())), preferred_element_type=F32)


def nt(left, right):
    return lax.dot_general(left, right, (((1,), (1,)), ((), ())), preferred_element_type=F32)


def tn(left, right):
    return lax.dot_general(left, right, (((0,), (0,)), ((), ())), preferred_element_type=F32)


def lane_of(shape):
    return lax.broadcasted_iota(jnp.int32, shape, len(shape) - 1)


def row_of(shape):
    return lax.broadcasted_iota(jnp.int32, shape, len(shape) - 2)


def spread(matrix):
    pieces = []
    for pair in range(HEADS // 2):
        both = matrix[:, pair * SLOT : (pair + 1) * SLOT]
        first = lane_of(both.shape) < HEAD_DIM
        pieces.append(jnp.where(first, both, 0.0))
        pieces.append(jnp.where(first, pltpu.roll(both, HEAD_DIM, 1), 0.0))
    return jnp.concatenate(pieces, axis=1)


def joined(wide):
    pieces = []
    for pair in range(HEADS // 2):
        even = wide[:, 2 * pair * SLOT : (2 * pair + 1) * SLOT]
        odd = wide[:, (2 * pair + 1) * SLOT : (2 * pair + 2) * SLOT]
        pieces.append(jnp.where(lane_of(even.shape) < HEAD_DIM, even, pltpu.roll(odd, HEAD_DIM, 1)))
    return jnp.concatenate(pieces, axis=1)


def spread_rows(matrix):
    gap = jnp.zeros((SLOT - HEAD_DIM, matrix.shape[1]), matrix.dtype)
    pieces = []
    for head in range(HEADS):
        pieces += [matrix[head * HEAD_DIM : (head + 1) * HEAD_DIM], gap]
    return jnp.concatenate(pieces, axis=0)


def head_cols(head):
    return slice(head * SLOT, (head + 1) * SLOT)


def project_keys(x, w_all, bias_v, first_place, length, k_out, v_out):
    raw = nn(x, w_all[:, WIDE : 2 * WIDE])
    one_head = (raw.shape[0], SLOT)
    shut = jnp.where(row_of(one_head) + first_place >= length, NEGATIVE, 0.0)
    here = lane_of(one_head) == HEAD_DIM + 2
    for head in range(HEADS):
        cols = head_cols(head)
        k_out[:, cols] = jnp.where(here, shut, raw[:, cols]).astype(BF)
    ones_row = jnp.where(lane_of((1, WIDE)) % SLOT == HEAD_DIM, 1.0, 0.0)
    v_out[...] = (nn(x, w_all[:, 2 * WIDE :]) + (spread(bias_v) + ones_row)).astype(BF)


def attend(queries, keys, values, kept):
    scores = nt(queries, keys)
    peak = jnp.max(scores, axis=1, keepdims=True)
    kept[...] = jnp.exp(scores - peak).astype(BF)
    return nn(kept[...], values), jnp.broadcast_to(peak, (peak.shape[0], SLOT))


def kept_rows(head, rows):
    return slice(head * rows, (head + 1) * rows)


def owner_of(distance, ring):
    return lax.rem(lax.axis_index("seq") - distance + ring, ring)


def select_kernel(
    cell, carry, tokens, masks, embed, stream_out, low_out, *refs
):
    held, mask_held, embed_held, arrived = refs[-4:]
    copies = [
        pltpu.make_async_copy(source, target, arrived.at[which])
        for which, (source, target) in enumerate(
            ((tokens.at[cell], held), (masks, mask_held), (embed, embed_held))
        )
    ]
    for copy in copies:
        copy.start()
    for copy in copies[1:]:
        copy.wait()
    rows, width = held.shape
    mask = mask_held[cell : cell + 1, :].astype(F32)
    column = jnp.transpose(jnp.broadcast_to(mask, (8, rows)))[:, :1]
    copies[0].wait()
    stream = jnp.where(column == 1.0, embed_held[...], held[...])
    stream_out[...] = stream
    low_out[...] = stream.astype(BF)
    if not carry:
        return
    carrier_out = refs[0]
    pieces = [
        mask_held[which : which + 1, at : at + width]
        for which in range(masks.shape[0])
        for at in range(0, rows, width)
    ]
    pieces.append(jnp.zeros((MASK_ROWS - len(pieces), width), masks.dtype))
    carrier_out[:rows, :] = stream.astype(BF)
    carrier_out[rows:, :] = jnp.concatenate(pieces, axis=0).astype(F32).astype(BF)


def mask_of(carrier, cell):
    rows = carrier.shape[0] - MASK_ROWS
    count = rows // carrier.shape[1]
    under = carrier[rows:, :].astype(F32)
    first = cell * count
    return jnp.concatenate([under[first + at : first + at + 1] for at in range(count)], axis=1)


def first_kernel(cells, lengths, *refs):
    xs, refs = refs[:cells], refs[cells:]
    wq, wk, wv, bias_q, bias_v = refs[:5]
    outs, (w_all, w_kv) = refs[5:-2], refs[-2:]
    w_all[:, :WIDE] = spread(wq[...] * HEAD_DIM ** (-0.5)).astype(BF)
    w_all[:, WIDE : 2 * WIDE] = spread(wk[...]).astype(BF)
    w_all[:, 2 * WIDE :] = spread(wv[...]).astype(BF)
    rows = outs[0].shape[0]
    first_place = lax.axis_index("seq") * rows
    one_row = lane_of((1, WIDE)) % SLOT
    bias = spread(bias_q[...]) * HEAD_DIM ** (-0.5) + jnp.where(one_row == HEAD_DIM + 2, 1.0, 0.0)
    for cell in range(cells):
        x = xs[cell].at[:rows]
        q_out, k_out, v_out, kept_out, state_out, peak_out = outs[6 * cell : 6 * cell + 6]
        q_out[...] = (nn(x[...], w_all[:, :WIDE]) + bias).astype(BF)
        project_keys(x[...], w_all, bias_v[...], first_place, lengths[cell], k_out, v_out)
        for head in range(HEADS):
            cols = head_cols(head)
            state_out[:, cols], peak_out[:, cols] = attend(
                q_out[:, cols], k_out[:, cols], v_out[:, cols], kept_out.at[kept_rows(head, rows)]
            )
    width = wk.shape[1]
    w_kv[:, :width] = wk[...].astype(BF)
    w_kv[:, width:] = wv[...].astype(BF)


def more_kernel(
    cell, distance, ring,
    lengths, x, q, state, peak, w_all, bias_v,
    k_out, v_out, kept_out, own_out, state_out, peak_out,
):
    rows = q.shape[0]
    first_place = owner_of(distance, ring) * rows
    project_keys(x[:rows, :], w_all, bias_v[...], first_place, lengths[cell], k_out, v_out)
    for head in range(HEADS):
        cols = head_cols(head)
        total, own = attend(
            q[:, cols], k_out[:, cols], v_out[:, cols], kept_out.at[kept_rows(head, rows)]
        )
        top = jnp.maximum(peak[:, cols], own)
        own_out[:, cols] = own
        peak_out[:, cols] = top
        state_out[:, cols] = state[:, cols] * jnp.exp(peak[:, cols] - top)
        state_out[:, cols] += total * jnp.exp(own - top)


def norm_parts(matrix):
    row_mean = jnp.mean(matrix, axis=1, keepdims=True)
    centred = matrix - row_mean
    row_var = jnp.mean(centred * centred, axis=1, keepdims=True)
    inverse = lax.rsqrt(row_var + EPSILON)
    return centred * inverse, inverse


def norm_back(grad, gain, unit, inverse):
    product = grad * unit
    scaled = grad * gain
    shift = jnp.mean(scaled, axis=1, keepdims=True)
    scale = jnp.mean(product * gain, axis=1, keepdims=True)
    return (scaled - shift - unit * scale) * inverse, product


def eight_sum(matrix):
    return jnp.sum(matrix.reshape(-1, 8, matrix.shape[1]), axis=0)


def inverse_of(value):
    guess = pl.reciprocal(value, approx=True)
    return guess * (2.0 - value * guess)


def gelu_parts(pre):
    bell = jnp.exp2(pre * pre * (-0.5 * LOG2_E))
    t = inverse_of(1.0 + (0.3275911 * 0.7071067811865476) * jnp.abs(pre))
    poly = 0.5 * 1.061405429
    for factor in (-1.453152027, 1.421413741, -0.284496736, 0.254829592):
        poly = poly * t + 0.5 * factor
    tail = poly * t * bell
    half = jnp.where(pre >= 0.0, 1.0 - tail, tail)
    return pre * half, half + pre * bell * INV_ROOT_TWO_PI


def halve(pack, keep_out, give_out):
    half = keep_out.shape[0]
    core = lax.axis_index("core")
    keep_out[...] = pack[pl.ds(pl.multiple_of(core * half, half), half), :]
    give_out[...] = pack[pl.ds(pl.multiple_of((1 - core) * half, half), half), :]


def my_plane(ring):
    return lax.axis_index("x") * ring + lax.axis_index("seq")


def halve(pack, keep_out, give_out):
    half = keep_out.shape[0]
    core = lax.axis_index("core")
    keep_out[...] = pack[pl.ds(pl.multiple_of(core * half, half), half), :]
    give_out[...] = pack[pl.ds(pl.multiple_of((1 - core) * half, half), half), :]


def near_bits(ring, core):
    bits = [("seq", 1 << i) for i in range(ring.bit_length() - 1)]
    return bits + [("x", 1)] if core else [("x", 1)] + bits


def my_side(ring, step):
    sides = []
    for core in range(2):
        axis, bit = near_bits(ring, core)[step]
        sides.append(lax.rem(lax.axis_index(axis) // bit, 2))
    return jnp.where(lax.axis_index("core") == 0, sides[0], sides[1])


def halve_kernel(ring, step, keep, received, keep_out, give_out):
    half = keep_out.shape[0]
    side = my_side(ring, step)
    for out, place in ((keep_out, side), (give_out, 1 - side)):
        at = pl.ds(pl.multiple_of(place * half, half), half)
        out[...] = (keep[at, :].astype(F32) + received[at, :].astype(F32)).astype(BF)


def join_kernel(ring, step, mine, other, out):
    rows = mine.shape[0]
    side = my_side(ring, step)
    out[pl.ds(pl.multiple_of(side * rows, rows), rows), :] = mine[...]
    out[pl.ds(pl.multiple_of((1 - side) * rows, rows), rows), :] = other[...]


def divide_kernel(ring, keep, received, own_out, *give_outs):
    piece = own_out.shape[0]
    plane = my_plane(ring)
    for step, out in enumerate((own_out,) + give_outs):
        at = pl.ds(pl.multiple_of((plane ^ step) * piece, piece), piece)
        out[...] = (keep[at, :].astype(F32) + received[at, :].astype(F32)).astype(BF)


def place_pieces(ring, mine, other, pack_one, pack_two):
    plane, core = my_plane(ring), lax.axis_index("core")
    for step in range(2 * ring):
        start = 0
        for pack in (pack_one, pack_two):
            piece = pack.shape[0] // (4 * ring)
            for half, sources in ((core, mine), (1 - core, other)):
                at = pl.multiple_of((half * 2 * ring + (plane ^ step)) * piece, piece)
                pack[pl.ds(at, piece), :] = sources[step][start : start + piece, :]
            start += piece


def middle_kernel(
    cell, ring, carry, finish,
    lengths, x, q, state, peak, stream, cotangent, w_all, bias_v, wo_in, bias_o, gain_one,
    shift_one, w1_in, bias_1, w2_in, bias_2, gain_two, shift_two, *refs,
):
    count = ring - 1 if ring > 2 else 0
    before, refs = refs[:count], refs[count:]
    if carry:
        dwo_in, dw1_in, dw2_in, vec_in = refs[:4]
        refs = refs[4:]
    do_outs, dot_outs, refs = refs[:ring], refs[ring : 2 * ring], refs[2 * ring :]
    result_out, k_out, v_out, kept_out, x_out, first_out, vec_out = refs[:7]
    refs = refs[7:]
    if carry:
        wo, w1, w2 = wo_in, w1_in, w2_in
    else:
        wo, w1, w2 = refs[:3]
        refs = refs[3:]
        wo[...] = spread_rows(wo_in[...].astype(BF))
        w1[...] = w1_in[...].astype(BF)
        w2[...] = w2_in[...].astype(BF)
    if finish:
        keep_out, give_out = refs[:2]
        refs = refs[2:]
    else:
        dwo_out, dw1_out, dw2_out = refs[:3]
        refs = refs[3:]
    scales, refs = refs[:ring], refs[ring:]
    (
        attended_wide, attended_low, normed_low, active_low, hidden_low, branch_low, attn_low,
        unit_one, inverse_one, narrow_b, wide_b, acc, *pack_ref,
    ) = refs
    rows, width = stream.shape
    x_out[...] = x[:rows, :]
    hidden = w1.shape[1]
    length = lengths[cell]
    first_place = owner_of(ring - 1, ring) * rows
    project_keys(x[:rows, :], w_all, bias_v[...], first_place, length, k_out, v_out)
    for head in range(HEADS):
        cols = head_cols(head)
        total, own = attend(
            q[:, cols], k_out[:, cols], v_out[:, cols], kept_out.at[kept_rows(head, rows)]
        )
        top = jnp.maximum(peak[:, cols], own)
        old_scale, own_scale = jnp.exp(peak[:, cols] - top), jnp.exp(own - top)
        both = state[:, cols] * old_scale + total * own_scale
        inverse = inverse_of(both[:, HEAD_DIM : HEAD_DIM + 1])
        attended = both * inverse
        attended_wide[:, cols] = attended
        attended_low[:, cols] = attended.astype(BF)
        scales[ring - 1][:, cols] = own_scale * inverse
        if ring == 2:
            scales[0][:, cols] = old_scale * inverse
        else:
            for block in range(ring - 1):
                scales[block][:, cols] = jnp.exp(before[block][:, cols] - top) * inverse

    my_place = lax.axis_index("seq") * rows

    valid = jnp.where(row_of((rows, SLOT)) + my_place < length, 1.0, 0.0)
    valid = jnp.concatenate([valid] * (width // SLOT), axis=1)

    def add(slot, matrix):
        acc[slot] = eight_sum(matrix)

    attn_out = nn(attended_low[...], wo[...]) + bias_o[...]
    unit, inverse = norm_parts(stream[...] + attn_out)
    unit_one[...] = unit
    inverse_one[...] = jnp.broadcast_to(inverse, (rows, SLOT))
    normed = unit * gain_one[...] + shift_one[...]
    narrow_b[...] = normed
    normed_low[...] = normed.astype(BF)
    add(8, stream[...] * stream[...] * valid)
    add(9, attn_out * attn_out * valid)

    active, slope = gelu_parts(nn(normed_low[...], w1[...]) + bias_1[...])
    active_low[...] = active.astype(BF)
    wide_b[...] = slope

    branch = nn(active_low[...], w2[...]) + bias_2[...]
    unit, inverse = norm_parts(narrow_b[...] + branch)
    result_out[...] = unit * gain_two[...] + shift_two[...]
    grad_result = cotangent[...] * valid
    grad_second, product = norm_back(grad_result, gain_two[...], unit, inverse)
    narrow_b[...] = grad_second
    branch_bf = grad_second.astype(BF)
    branch_low[...] = branch_bf
    add(0, product)
    add(1, grad_result)
    add(10, branch * branch * valid)

    hidden_bf = (nt(branch_low[...], w2[...]) * wide_b[...]).astype(BF)
    hidden_low[...] = hidden_bf

    grad_normed = narrow_b[...] + nt(hidden_low[...], w1[...])
    unit = unit_one[...]
    grad_first, product = norm_back(grad_normed, gain_one[...], unit, inverse_one[:, :1])
    first_out[...] = grad_first
    attn_bf = grad_first.astype(BF)
    attn_low[...] = attn_bf
    add(5, product)
    add(6, grad_normed)

    do_wide = nt(attn_low[...], wo[...]).astype(BF).astype(F32)
    for head in range(HEADS):
        cols = head_cols(head)
        do_head = do_wide[:, cols]
        row_dot = jnp.sum(do_head * attended_wide[:, cols], axis=1, keepdims=True)
        for scale, do_out, dot_out in zip(scales, do_outs, dot_outs):
            factor = scale[:, cols]
            do_out[:, cols] = (do_head * factor).astype(BF)
            dot_out[:, cols] = row_dot * factor

    ones = jnp.ones((8, rows), BF)
    hidden_sum = nn(ones, hidden_low[...])[0:1]
    known = {
        2: nn(ones, branch_low[...])[0:1],
        3: hidden_sum[:, :width],
        4: hidden_sum[:, width:],
        7: nn(ones, attn_low[...])[0:1],
        11: jnp.full((1, width), jnp.clip(length - my_place, 0, rows).astype(F32)),
    }
    sums = [
        known[slot] if slot in known else jnp.sum(acc[slot], axis=0, keepdims=True)
        for slot in range(12)
    ]
    vec = jnp.concatenate(sums + [jnp.zeros((4, width), F32)], axis=0)
    vec_out[...] = vec + vec_in[...] if carry else vec

    dwo = tn(attn_low[...], attended_low[...])
    dw1 = tn(normed_low[...], hidden_low[...])
    dw2 = tn(branch_low[...], active_low[...])
    if carry:
        dwo += dwo_in[...]
        dw1 += dw1_in[...]
        dw2 += dw2_in[...]
    if not finish:
        dwo_out[...] = dwo
        dw1_out[...] = dw1
        dw2_out[...] = dw2
        return
    (pack,) = pack_ref
    pack[:width, :] = joined(dwo).astype(BF)
    pack[width : 2 * width, :] = dw1[:, :width].astype(BF)
    pack[2 * width : 3 * width, :] = dw1[:, width:].astype(BF)
    for at in range(0, hidden, width):
        pack[3 * width + at : 4 * width + at, :] = dw2[:, at : at + width].astype(BF)
    used = 3 * width + hidden
    if pack.shape[0] > used:
        pack[used:, :] = jnp.zeros((pack.shape[0] - used, width), BF)
    halve(pack, keep_out, give_out)


def head_grads(q, k, v, do, dot, kept):
    dots = jnp.concatenate([dot] * (kept.shape[1] // SLOT), axis=1)
    score_grad = (kept.astype(F32) * (nt(do, v) - dots)).astype(BF)
    return (
        nn(score_grad, k),
        tn(q[:, :HEAD_DIM], score_grad),
        tn(do[:, :HEAD_DIM], kept),
    )


def all_heads(q, k, v, do, dot, kept, low, put_query):
    rows = q.shape[0]
    for head in range(HEADS):
        cols = head_cols(head)
        dq, dk, dv = head_grads(
            q[:, cols], k[:, cols], v[:, cols], do[:, cols], dot[:, cols],
            kept[kept_rows(head, rows), :],
        )
        put_query(cols, dq)
        low[head * HEAD_DIM : (head + 1) * HEAD_DIM, :] = dk.astype(BF)
        at = (HEADS + head) * HEAD_DIM
        low[at : at + HEAD_DIM, :] = dv.astype(BF)


def masked_sum(carrier, cell, grad_bf):
    mask = mask_of(carrier, cell)
    picked = jnp.broadcast_to(mask, (8, mask.shape[1])).astype(BF)
    return nn(picked, grad_bf)[0:1]


def value_sums(low):
    half = low.shape[0] // 2
    sums = jnp.sum(low[half:, :].astype(F32), axis=1, keepdims=True)
    return jnp.broadcast_to(sums, (half, SLOT))


def block_kernel(cell, carry_dq, carry, sent, carrier, q, do, dot, k, v, kept, w_kv, *refs):
    if carry_dq:
        dq_in, refs = refs[0], refs[1:]
    if carry:
        (dw_in, sum_in, vec_in), refs = refs[:3], refs[3:]
    dq_out, dx_out, dw_out, sum_out, vec_out, low = refs

    def put_query(cols, dq):
        dq_out[:, cols] = dq + dq_in[:, cols] if carry_dq else dq

    all_heads(q, k, v, do, dot, kept, low, put_query)
    x = sent[: q.shape[0], :]
    dx_bf = jnp.transpose(nn(w_kv[...], low[...])).astype(BF)
    dx_out[...] = dx_bf
    dw = nn(low[...], x)
    dw_out[...] = dw + dw_in[...] if carry else dw
    sums = value_sums(low)
    sum_out[...] = sums + sum_in[...] if carry else sums
    vec_out[...] = vec_in[...] if carry else jnp.zeros_like(vec_out)
    vec_out[0:1, : x.shape[1]] += masked_sum(carrier[...], cell, dx_bf)


def last_kernel(
    cell, carry, finish,
    sent, carrier, q, do, dot, k, v, kept, w_all, w_kv, first, dq_in, dw_in, sum_in, vec_in, *refs
):
    if carry:
        dwq_in, refs = refs[0], refs[1:]
    if finish:
        vec_mid, dx_out, keep_out, give_out, low_q, low, pack = refs
    else:
        dx_out, dw_out, sum_out, vec_out, dwq_out, low_q, low = refs

    def put_query(cols, dq):
        low_q[:, cols] = ((dq + dq_in[:, cols]) * HEAD_DIM ** (-0.5)).astype(BF)

    all_heads(q, k, v, do, dot, kept, low, put_query)
    grads = first[...] + nt(low_q[...], w_all[:, :WIDE]) * HEAD_DIM**0.5
    grads += jnp.transpose(nn(w_kv[...], low[...]))
    dx_out[...] = grads
    width = grads.shape[1]
    x = sent[: q.shape[0], :]
    dwq = tn(x, low_q[...])
    dw = nn(low[...], x) + dw_in[...]
    sum_q = jnp.sum(low_q[...].astype(F32), axis=0, keepdims=True) + vec_in[1:2, :]
    sum_v = value_sums(low) + sum_in[...]
    sum_mask = masked_sum(carrier[...], cell, grads.astype(BF)) + vec_in[0:1, :width]
    if carry:
        dwq += dwq_in[...]
    if not finish:
        dwq_out[...] = dwq
        dw_out[...] = dw
        sum_out[...] = sum_v
        vec_out[...] = jnp.zeros_like(vec_out)
        vec_out[0:1, :width] = sum_mask
        vec_out[1:2, :] = sum_q
        return
    pack[:width, :] = joined(dwq).astype(BF)
    pack[width : 3 * width, :] = dw.astype(BF)
    rows = jnp.concatenate(
        [
            vec_mid[:12, :],
            joined(sum_q),
            jnp.transpose(sum_v)[0:1, :],
            sum_mask,
            jnp.zeros((1, width), F32),
        ],
        axis=0,
    )
    high = rows.astype(BF)
    pack[3 * width : 3 * width + 16, :] = high
    pack[3 * width + 16 : 3 * width + 32, :] = (rows - high.astype(F32)).astype(BF)
    used = 3 * width + 32
    if pack.shape[0] > used:
        pack[used:, :] = jnp.zeros((pack.shape[0] - used, width), BF)
    halve(pack, keep_out, give_out)


def unpack_kernel(ring, *refs):
    mine, other, refs = refs[: 2 * ring], refs[2 * ring : 4 * ring], refs[4 * ring :]
    dwo_out, dw1_out, dw2_out, dwq_out, dwk_out, dwv_out = refs[:6]
    outs, pack_one, pack = refs[6:-2], refs[-2], refs[-1]
    place_pieces(ring, mine, other, pack_one, pack)
    width = pack.shape[1]
    dwo_out[...] = jnp.transpose(pack_one[:width, :].astype(F32))
    dw1_out[:, :width] = pack_one[width : 2 * width, :].astype(F32)
    dw1_out[:, width:] = pack_one[2 * width : 3 * width, :].astype(F32)
    for at in range(0, dw2_out.shape[0], width):
        dw2_out[at : at + width, :] = jnp.transpose(
            pack_one[3 * width + at : 4 * width + at, :].astype(F32)
        )
    dwq_out[...] = pack[:width, :].astype(F32)
    dwk_out[...] = jnp.transpose(pack[width : 2 * width, :].astype(F32))
    dwv_out[...] = jnp.transpose(pack[2 * width : 3 * width, :].astype(F32))
    vec = pack[3 * width : 3 * width + 16, :].astype(F32)
    vec += pack[3 * width + 16 : 3 * width + 32, :].astype(F32)
    for out, row in zip(outs, (0, 1, 2, (3, 4), 5, 6, 7, 12, 13, 14)):
        if isinstance(row, tuple):
            out[:, :width] = vec[row[0] : row[0] + 1]
            out[:, width:] = vec[row[1] : row[1] + 1]
        else:
            out[...] = vec[row : row + 1]
    squares = jnp.sum(vec[8:16], axis=1, keepdims=True)
    count = vec[11:12, 0:1]
    means = jnp.sqrt(squares / (count * width))
    lane = lane_of((1, 3))
    outs[10][...] = jnp.where(
        lane == 0, means[0:1], jnp.where(lane == 1, means[1:2], means[2:3])
    )


def finish_kernel(cells, carrier, *refs):
    local, received, out = refs[:cells], refs[cells:-1], refs[-1]
    rows, count = local[0].shape[0], len(received) // cells
    for cell in range(cells):
        grads = local[cell][...]
        for piece in received[cell * count : (cell + 1) * count]:
            grads += piece[...].astype(F32)
        mask = jnp.broadcast_to(mask_of(carrier[...], cell), (8, rows))
        out[cell] = jnp.where(jnp.transpose(mask)[:, :1] == 1.0, 0.0, grads)


def call(kernel, ins, outs, scratch=(), flops=0):
    moved = sum(a.size * a.dtype.itemsize for a in ins) + sum(
        s.size * s.dtype.itemsize for s in outs
    )
    vmem = pl.BlockSpec(memory_space=pltpu.VMEM)
    smem = pl.BlockSpec(memory_space=pltpu.SMEM)
    return pl.pallas_call(
        kernel,
        in_specs=[smem if a.ndim == 1 else vmem for a in ins],
        out_specs=[vmem] * len(outs),
        out_shape=outs,
        scratch_shapes=list(scratch),
        compiler_params=pltpu.CompilerParams(vmem_limit_bytes=VMEM_LIMIT),
        cost_estimate=pl.CostEstimate(
            flops=flops, bytes_accessed=moved if flops != 1 else 1, transcendentals=0
        ),
    )(*ins)


def send(block, distance, ring):
    route = [(i, (i + distance) % ring) for i in range(ring)]
    return lax.ppermute(block, "seq", route)


NEAR = ("x", "core", "seq")
PLANE = ("x", "seq")


def swap(block, axes, step):
    return lax.ppermute(block, axes, [(i, i ^ step) for i in range(lax.axis_size(axes))])


def tree_sum(blocks):
    blocks = [block.astype(F32) for block in blocks]
    while len(blocks) > 1:
        blocks = [a + b for a, b in zip(blocks[::2], blocks[1::2])]
    return blocks[0].astype(BF)


def swaps(blocks, axes):
    return {step: swap(blocks[step], axes, step) for step in sorted(blocks, reverse=True)}


def sum_steps(own, got):
    return tree_sum([own] + [got[step] for step in sorted(got)])


def divide(keep, received, ring):
    half, width = keep.shape
    piece = jax.ShapeDtypeStruct((half // (2 * ring), width), BF)
    own, *pieces = call(
        functools.partial(divide_kernel, ring), [keep, received], [piece] * (2 * ring)
    )
    return own, dict(enumerate(pieces, 1))


def to_all(block, axes):
    return swaps({step: block for step in range(1, lax.axis_size(axes))}, axes)


def padded(rows, pieces):
    piece = -(-rows // pieces)
    return -(-piece // 16) * 16 * pieces


def body(
    tokens, masked, lengths, cotangent, mask_embed, query_weight, query_bias, key_weight,
    value_weight, value_bias, out_weight, out_bias, gain_one, shift_one, expand_weight,
    expand_bias, reduce_weight, reduce_bias, gain_two, shift_two,
):
    cells, rows, width = tokens.shape
    hidden = expand_weight.shape[1]
    ring = lax.axis_size("seq")

    def row(vector):
        return vector.reshape(1, -1)

    shape = jax.ShapeDtypeStruct
    low_wide, full_wide = shape((rows, WIDE), BF), shape((rows, WIDE), F32)
    low_narrow, full_narrow = shape((rows, width), BF), shape((rows, width), F32)
    weights = shape((HEADS * rows, rows), BF)
    score_flops = 2 * rows * rows * HEADS * 256

    stream, x_moved, x_low = [], [], []
    vmem = pl.BlockSpec(memory_space=pltpu.VMEM)
    masks = masked
    for cell in range(cells):
        carry = cell == cells - 1
        outs = [full_narrow, low_narrow] + [shape((rows + MASK_ROWS, width), BF)] * carry
        made = pl.pallas_call(
            functools.partial(select_kernel, cell, carry),
            in_specs=[pl.BlockSpec(memory_space=pltpu.HBM)] * 3,
            out_specs=[vmem] * len(outs),
            out_shape=outs,
            scratch_shapes=[
                pltpu.VMEM((rows, width), F32),
                pltpu.VMEM((cells, rows), jnp.int32),
                pltpu.VMEM((1, width), F32),
                pltpu.SemaphoreType.DMA((3,)),
            ],
            compiler_params=pltpu.CompilerParams(vmem_limit_bytes=VMEM_LIMIT),
        )(
            *[
                pltpu.with_memory_space_constraint(a, pltpu.HBM)
                for a in (tokens, masks, row(mask_embed))
            ]
        )
        stream.append(made[0])
        x_low.append(made[1])
        x_moved.append([made[-1]])
        if cell == 0:
            x_moved[0] += [send(x_moved[0][0], t, ring) for t in range(1, ring)]
        masks, x_low[cell] = lax.optimization_barrier((masks, x_low[cell]))

    made = call(
        functools.partial(first_kernel, cells),
        [lengths]
        + x_low
        + [query_weight, key_weight, value_weight, row(query_bias), row(value_bias)],
        [low_wide, low_wide, low_wide, weights, full_wide, full_wide] * cells
        + [
            shape((width, 3 * WIDE), BF),
            shape((width, 2 * width), BF),
        ],
        flops=2 * cells * score_flops,
    )
    w_all, w_kv = made[-2:]
    wo, w1, w2 = out_weight, expand_weight, reduce_weight
    low_weights = [
        shape((WIDE, width), BF), shape((width, hidden), BF), shape((hidden, width), BF)
    ]
    bias_v = row(value_bias)
    for cell in range(1, cells):
        sent, w_all = lax.optimization_barrier((x_moved[cell][0], w_all))
        x_moved[cell] += [send(sent, t, ring) for t in range(1, ring)]
    carriers = list(x_moved[-1])
    keys, values, kept, queries, states, peaks = [], [], [], [], [], []
    for cell in range(cells):
        q, k, v, p, state, peak = made[6 * cell : 6 * cell + 6]
        queries.append(q)
        keys.append([k])
        values.append([v])
        kept.append([p])
        own_peaks = [peak]
        for t in range(1, ring - 1):
            k, v, p, own, state, peak = call(
                functools.partial(more_kernel, cell, t, ring),
                [lengths, x_moved[cell][t], q, state, peak, w_all, bias_v],
                [low_wide, low_wide, weights, full_wide, full_wide, full_wide],
                flops=2 * score_flops,
            )
            keys[cell].append(k)
            values[cell].append(v)
            kept[cell].append(p)
            own_peaks.append(own)
        states.append([state, peak])
        peaks.append(own_peaks if ring > 2 else [])

    one_rows = padded(3 * width + hidden, lax.axis_size(NEAR))
    results, firsts, grads_out = [], [], []
    carried, carried_back, received = [], [], []
    dq = [None] * cells

    def backward_of_blocks(cell):
        nonlocal carried_back
        partial = []
        for t in range(1, ring):
            ins = [
                x_moved[cell][t], carriers[t], queries[cell], *grads_out[cell][t],
                keys[cell][t], values[cell][t], kept[cell][t], w_kv,
            ]
            ins += ([dq[cell]] if t > 1 else []) + carried_back
            dq[cell], dx, *carried_back = call(
                functools.partial(block_kernel, cell, t > 1, bool(carried_back)),
                ins,
                [
                    full_wide,
                    low_narrow,
                    shape((2 * width, width), F32),
                    shape((width, SLOT), F32),
                    shape((8, WIDE), F32),
                ],
                [pltpu.VMEM((2 * width, rows), BF)],
                flops=5 * score_flops,
            )
            partial.append(dx)
        return partial

    def returned(partial):
        return [send(dx, -t, ring) for t, dx in enumerate(partial, 1)]

    for cell in range(cells):
        finish = cell == cells - 1
        if cell > 0:
            partial = backward_of_blocks(cell - 1)
            states[cell], partial = lax.optimization_barrier((states[cell], partial))
            received.append(returned(partial))
        outs = [low_wide] * ring + [full_wide] * ring
        outs += [full_narrow, low_wide, low_wide, weights, low_narrow, full_narrow]
        outs += [shape((16, width), F32)] + (low_weights if cell == 0 else [])
        if finish:
            outs += [shape((one_rows // 2, width), BF)] * 2
        else:
            outs += [shape((width, WIDE), F32)] + [shape((width, hidden), F32)] * 2
        scratch = [pltpu.VMEM((rows, WIDE), F32)] * ring + [
            pltpu.VMEM((rows, WIDE), F32),
            pltpu.VMEM((rows, WIDE), BF),
            pltpu.VMEM((rows, width), BF),
            pltpu.VMEM((rows, hidden), BF),
            pltpu.VMEM((rows, hidden), BF),
            pltpu.VMEM((rows, width), BF),
            pltpu.VMEM((rows, width), BF),
            pltpu.VMEM((rows, width), F32),
            pltpu.VMEM((rows, SLOT), F32),
            pltpu.VMEM((rows, width), F32),
            pltpu.VMEM((rows, hidden), F32),
            pltpu.VMEM((12, 8, width), F32),
        ]
        if finish:
            scratch.append(pltpu.VMEM((one_rows, width), BF))
        made = call(
            functools.partial(middle_kernel, cell, ring, bool(carried), finish),
            [
                lengths, x_moved[cell][ring - 1], queries[cell], *states[cell], stream[cell],
                cotangent[cell], w_all, bias_v, wo, row(out_bias), row(gain_one), row(shift_one),
                w1, row(expand_bias), w2, row(reduce_bias), row(gain_two), row(shift_two),
            ]
            + peaks[cell]
            + carried,
            outs,
            scratch,
            flops=7 * score_flops,
        )
        grads_out.append(list(zip(made[:ring], made[ring : 2 * ring])))
        made = made[ring:]
        result, k, v, p, x_moved[cell][ring - 1], first, vec_mid = made[ring : ring + 7]
        made = made[ring + 7 :]
        if cell == 0:
            wo, w1, w2 = made[:3]
            made = made[3:]
        results.append(result)
        keys[cell].append(k)
        values[cell].append(v)
        kept[cell].append(p)
        firsts.append(first)
        carried = list(made) + [vec_mid]
    keep, give = made
    received_one = swap(give, "core", 1)
    queries[-1], received = lax.optimization_barrier((queries[-1], received))
    partial = backward_of_blocks(cells - 1)
    own_one, pieces = divide(keep, received_one, ring)
    carried, partial, own_one, pieces = lax.optimization_barrier(
        (carried_back, partial, own_one, pieces)
    )
    got_one = swaps(pieces, PLANE)

    two_rows = padded(3 * width + 32, lax.axis_size(NEAR))
    local = []
    depth_steps = [1 << i for i in range(lax.axis_size("z").bit_length() - 1)]
    for cell in range(cells):
        finish = cell == cells - 1
        if finish:
            carried, got_one = lax.optimization_barrier((carried, got_one))
            own_one = sum_steps(own_one, got_one)
            got_one = swap(own_one, "z", depth_steps[0])
        ins = [
            x_moved[cell][0], carriers[0], queries[cell], *grads_out[cell][0],
            keys[cell][0], values[cell][0], kept[cell][0], w_all, w_kv, firsts[cell], dq[cell],
        ]
        outs = [full_narrow]
        scratch = [pltpu.VMEM((rows, WIDE), BF), pltpu.VMEM((2 * width, rows), BF)]
        if finish:
            outs += [shape((two_rows // 2, width), BF)] * 2
            scratch += [pltpu.VMEM((two_rows, width), BF)]
        else:
            outs += [shape((2 * width, width), F32), shape((width, SLOT), F32)]
            outs += [shape((8, WIDE), F32), shape((width, WIDE), F32)]
        made = call(
            functools.partial(last_kernel, cell, cell > 0, finish),
            ins + carried + ([vec_mid] if finish else []),
            outs,
            scratch,
            flops=1,
        )
        local.append(made[0])
        carried = list(made[1:])
    keep, give = carried
    give, got_one = lax.optimization_barrier((give, got_one))
    other = swap(give, "core", 1)
    for step in depth_steps[1:]:
        own_one = tree_sum([own_one, got_one])
        got_one = swap(own_one, "z", step)
    own, pieces = divide(keep, other, ring)
    got, got_one = lax.optimization_barrier((swaps(pieces, PLANE), got_one))
    own = sum_steps(own, got)
    own, partial = lax.optimization_barrier((own, partial))
    received.append(returned(partial))
    got, received = lax.optimization_barrier((to_all(own, "z"), received))
    own = sum_steps(own, got)
    own_one = tree_sum([own_one, got_one])
    own = jnp.concatenate([own_one, own], axis=0)
    tokens_grad = call(
        functools.partial(finish_kernel, cells),
        [carriers[0]] + local + sum(received, []),
        [shape((cells, rows, width), F32)],
    )[0]
    got = to_all(own, PLANE)
    result = jnp.stack(results)
    got[1], tokens_grad, result = lax.optimization_barrier((got[1], tokens_grad, result))
    mine = [own] + [got[step] for step in sorted(got)]
    other = [swap(piece, "core", 1) for piece in mine]

    vector = shape((1, width), F32)
    made = call(
        functools.partial(unpack_kernel, ring),
        mine + other,
        [shape((width, width), F32), shape((width, hidden), F32), shape((hidden, width), F32)]
        + [shape((width, width), F32)] * 3
        + [vector] * 3
        + [shape((1, hidden), F32)]
        + [vector] * 6
        + [shape((1, 3), F32)],
        [pltpu.VMEM((one_rows, width), BF), pltpu.VMEM((two_rows, width), BF)],
    )
    dwo, dw1, dw2, dwq, dwk, dwv = made[:6]
    (
        gain_two_grad, shift_two_grad, bias_2_grad, bias_1_grad, gain_one_grad, shift_one_grad,
        bias_o_grad, bias_q_grad, bias_v_grad, mask_embed_grad, root_means,
    ) = [a.reshape(-1) for a in made[6:]]

    return (
        result,
        tokens_grad,
        mask_embed_grad,
        dwq,
        bias_q_grad,
        dwk,
        dwv,
        bias_v_grad,
        dwo,
        bias_o_grad,
        gain_one_grad,
        shift_one_grad,
        dw1,
        bias_1_grad,
        dw2,
        bias_2_grad,
        gain_two_grad,
        shift_two_grad,
        root_means,
    )


def solution(mesh):
    dp, seq = mesh.shape["dp"], mesh.shape["seq"]
    cut = jax.sharding.Mesh(mesh.devices.reshape(dp // 4, 2, 2, seq), ("z",) + NEAR)
    dp = ("z", "x", "core")
    split = P(dp, "seq", None)
    return jax.shard_map(
        body,
        mesh=cut,
        in_specs=(split, P(dp, "seq"), P(dp), split) + (P(),) * 16,
        out_specs=(split, split) + (P(),) * 17,
        check_vma=False,
    )
```

```python
import functools

import jax
import jax.numpy as jnp
from jax import lax
from jax.experimental import pallas as pl
from jax.experimental.pallas import tpu as pltpu
from jax.sharding import PartitionSpec as P

HEADS = 4
HEAD_DIM = 64
SLOT = 128
WIDE = HEADS * SLOT

EPSILON = 1e-05
NEGATIVE = -1e30
INV_ROOT_TWO_PI = 0.3989422804014327
LOG2_E = 1.4426950408889634
BF = jnp.bfloat16
F32 = jnp.float32
VMEM_LIMIT = 16 * 1024 * 1024
MASK_ROWS = 16


def nn(left, right):
    return lax.dot_general(left, right, (((1,), (0,)), ((), ())), preferred_element_type=F32)


def nt(left, right):
    return lax.dot_general(left, right, (((1,), (1,)), ((), ())), preferred_element_type=F32)


def tn(left, right):
    return lax.dot_general(left, right, (((0,), (0,)), ((), ())), preferred_element_type=F32)


def lane_of(shape):
    return lax.broadcasted_iota(jnp.int32, shape, len(shape) - 1)


def row_of(shape):
    return lax.broadcasted_iota(jnp.int32, shape, len(shape) - 2)


def spread(matrix):
    pieces = []
    for pair in range(HEADS // 2):
        both = matrix[:, pair * SLOT : (pair + 1) * SLOT]
        first = lane_of(both.shape) < HEAD_DIM
        pieces.append(jnp.where(first, both, 0.0))
        pieces.append(jnp.where(first, pltpu.roll(both, HEAD_DIM, 1), 0.0))
    return jnp.concatenate(pieces, axis=1)


def joined(wide):
    pieces = []
    for pair in range(HEADS // 2):
        even = wide[:, 2 * pair * SLOT : (2 * pair + 1) * SLOT]
        odd = wide[:, (2 * pair + 1) * SLOT : (2 * pair + 2) * SLOT]
        pieces.append(jnp.where(lane_of(even.shape) < HEAD_DIM, even, pltpu.roll(odd, HEAD_DIM, 1)))
    return jnp.concatenate(pieces, axis=1)


def spread_rows(matrix):
    gap = jnp.zeros((SLOT - HEAD_DIM, matrix.shape[1]), matrix.dtype)
    pieces = []
    for head in range(HEADS):
        pieces += [matrix[head * HEAD_DIM : (head + 1) * HEAD_DIM], gap]
    return jnp.concatenate(pieces, axis=0)


def head_cols(head):
    return slice(head * SLOT, (head + 1) * SLOT)


def project_keys(x, w_all, bias_v, first_place, length, k_out, v_out):
    raw = nn(x, w_all[:, WIDE : 2 * WIDE])
    one_head = (raw.shape[0], SLOT)
    shut = jnp.where(row_of(one_head) + first_place >= length, NEGATIVE, 0.0)
    here = lane_of(one_head) == HEAD_DIM + 2
    for head in range(HEADS):
        cols = head_cols(head)
        k_out[:, cols] = jnp.where(here, shut, raw[:, cols]).astype(BF)
    ones_row = jnp.where(lane_of((1, WIDE)) % SLOT == HEAD_DIM, 1.0, 0.0)
    v_out[...] = (nn(x, w_all[:, 2 * WIDE :]) + (spread(bias_v) + ones_row)).astype(BF)


def attend(queries, keys, values, kept):
    scores = nt(queries, keys)
    peak = jnp.max(scores, axis=1, keepdims=True)
    kept[...] = jnp.exp(scores - peak).astype(BF)
    return nn(kept[...], values), jnp.broadcast_to(peak, (peak.shape[0], SLOT))


def kept_rows(head, rows):
    return slice(head * rows, (head + 1) * rows)


def owner_of(distance, ring):
    return lax.rem(lax.axis_index("seq") - distance + ring, ring)


def select_kernel(
    cell, carry, tokens, masks, embed, stream_out, low_out, *refs
):
    held, mask_held, embed_held, arrived = refs[-4:]
    copies = [
        pltpu.make_async_copy(source, target, arrived.at[which])
        for which, (source, target) in enumerate(
            ((tokens.at[cell], held), (masks, mask_held), (embed, embed_held))
        )
    ]
    for copy in copies:
        copy.start()
    for copy in copies[1:]:
        copy.wait()
    rows, width = held.shape
    mask = mask_held[cell : cell + 1, :].astype(F32)
    column = jnp.transpose(jnp.broadcast_to(mask, (8, rows)))[:, :1]
    copies[0].wait()
    stream = jnp.where(column == 1.0, embed_held[...], held[...])
    stream_out[...] = stream
    low_out[...] = stream.astype(BF)
    if not carry:
        return
    carrier_out = refs[0]
    pieces = [
        mask_held[which : which + 1, at : at + width]
        for which in range(masks.shape[0])
        for at in range(0, rows, width)
    ]
    pieces.append(jnp.zeros((MASK_ROWS - len(pieces), width), masks.dtype))
    carrier_out[:rows, :] = stream.astype(BF)
    carrier_out[rows:, :] = jnp.concatenate(pieces, axis=0).astype(F32).astype(BF)


def mask_of(carrier, cell):
    rows = carrier.shape[0] - MASK_ROWS
    count = rows // carrier.shape[1]
    under = carrier[rows:, :].astype(F32)
    first = cell * count
    return jnp.concatenate([under[first + at : first + at + 1] for at in range(count)], axis=1)


def first_kernel(cells, lengths, *refs):
    xs, refs = refs[:cells], refs[cells:]
    wq, wk, wv, bias_q, bias_v = refs[:5]
    outs, (w_all, w_kv) = refs[5:-2], refs[-2:]
    w_all[:, :WIDE] = spread(wq[...] * HEAD_DIM ** (-0.5)).astype(BF)
    w_all[:, WIDE : 2 * WIDE] = spread(wk[...]).astype(BF)
    w_all[:, 2 * WIDE :] = spread(wv[...]).astype(BF)
    rows = outs[0].shape[0]
    first_place = lax.axis_index("seq") * rows
    one_row = lane_of((1, WIDE)) % SLOT
    bias = spread(bias_q[...]) * HEAD_DIM ** (-0.5) + jnp.where(one_row == HEAD_DIM + 2, 1.0, 0.0)
    for cell in range(cells):
        x = xs[cell].at[:rows]
        q_out, k_out, v_out, kept_out, state_out, peak_out = outs[6 * cell : 6 * cell + 6]
        q_out[...] = (nn(x[...], w_all[:, :WIDE]) + bias).astype(BF)
        project_keys(x[...], w_all, bias_v[...], first_place, lengths[cell], k_out, v_out)
        for head in range(HEADS):
            cols = head_cols(head)
            state_out[:, cols], peak_out[:, cols] = attend(
                q_out[:, cols], k_out[:, cols], v_out[:, cols], kept_out.at[kept_rows(head, rows)]
            )
    width = wk.shape[1]
    w_kv[:, :width] = wk[...].astype(BF)
    w_kv[:, width:] = wv[...].astype(BF)


def more_kernel(
    cell, distance, ring,
    lengths, x, q, state, peak, w_all, bias_v,
    k_out, v_out, kept_out, own_out, state_out, peak_out,
):
    rows = q.shape[0]
    first_place = owner_of(distance, ring) * rows
    project_keys(x[:rows, :], w_all, bias_v[...], first_place, lengths[cell], k_out, v_out)
    for head in range(HEADS):
        cols = head_cols(head)
        total, own = attend(
            q[:, cols], k_out[:, cols], v_out[:, cols], kept_out.at[kept_rows(head, rows)]
        )
        top = jnp.maximum(peak[:, cols], own)
        own_out[:, cols] = own
        peak_out[:, cols] = top
        state_out[:, cols] = state[:, cols] * jnp.exp(peak[:, cols] - top)
        state_out[:, cols] += total * jnp.exp(own - top)


def norm_parts(matrix):
    row_mean = jnp.mean(matrix, axis=1, keepdims=True)
    centred = matrix - row_mean
    row_var = jnp.mean(centred * centred, axis=1, keepdims=True)
    inverse = lax.rsqrt(row_var + EPSILON)
    return centred * inverse, inverse


def norm_back(grad, gain, unit, inverse):
    product = grad * unit
    scaled = grad * gain
    shift = jnp.mean(scaled, axis=1, keepdims=True)
    scale = jnp.mean(product * gain, axis=1, keepdims=True)
    return (scaled - shift - unit * scale) * inverse, product


def eight_sum(matrix):
    return jnp.sum(matrix.reshape(-1, 8, matrix.shape[1]), axis=0)


def inverse_of(value):
    guess = pl.reciprocal(value, approx=True)
    return guess * (2.0 - value * guess)


def gelu_parts(pre):
    bell = jnp.exp2(pre * pre * (-0.5 * LOG2_E))
    t = inverse_of(1.0 + (0.3275911 * 0.7071067811865476) * jnp.abs(pre))
    poly = 0.5 * 1.061405429
    for factor in (-1.453152027, 1.421413741, -0.284496736, 0.254829592):
        poly = poly * t + 0.5 * factor
    tail = poly * t * bell
    half = jnp.where(pre >= 0.0, 1.0 - tail, tail)
    return pre * half, half + pre * bell * INV_ROOT_TWO_PI


def halve(pack, keep_out, give_out):
    half = keep_out.shape[0]
    core = lax.axis_index("core")
    keep_out[...] = pack[pl.ds(pl.multiple_of(core * half, half), half), :]
    give_out[...] = pack[pl.ds(pl.multiple_of((1 - core) * half, half), half), :]


def my_plane(ring):
    return lax.axis_index("x") * ring + lax.axis_index("seq")


def halve(pack, keep_out, give_out):
    half = keep_out.shape[0]
    core = lax.axis_index("core")
    keep_out[...] = pack[pl.ds(pl.multiple_of(core * half, half), half), :]
    give_out[...] = pack[pl.ds(pl.multiple_of((1 - core) * half, half), half), :]


def near_bits(ring, core):
    bits = [("seq", 1 << i) for i in range(ring.bit_length() - 1)]
    return bits + [("x", 1)] if core else [("x", 1)] + bits


def my_side(ring, step):
    sides = []
    for core in range(2):
        axis, bit = near_bits(ring, core)[step]
        sides.append(lax.rem(lax.axis_index(axis) // bit, 2))
    return jnp.where(lax.axis_index("core") == 0, sides[0], sides[1])


def halve_kernel(ring, step, keep, received, keep_out, give_out):
    half = keep_out.shape[0]
    side = my_side(ring, step)
    for out, place in ((keep_out, side), (give_out, 1 - side)):
        at = pl.ds(pl.multiple_of(place * half, half), half)
        out[...] = (keep[at, :].astype(F32) + received[at, :].astype(F32)).astype(BF)


def join_kernel(ring, step, mine, other, out):
    rows = mine.shape[0]
    side = my_side(ring, step)
    out[pl.ds(pl.multiple_of(side * rows, rows), rows), :] = mine[...]
    out[pl.ds(pl.multiple_of((1 - side) * rows, rows), rows), :] = other[...]


def divide_kernel(ring, keep, received, own_out, *give_outs):
    piece = own_out.shape[0]
    plane = my_plane(ring)
    for step, out in enumerate((own_out,) + give_outs):
        at = pl.ds(pl.multiple_of((plane ^ step) * piece, piece), piece)
        out[...] = (keep[at, :].astype(F32) + received[at, :].astype(F32)).astype(BF)


def place_pieces(ring, mine, other, pack_one, pack_two):
    plane, core = my_plane(ring), lax.axis_index("core")
    for step in range(2 * ring):
        start = 0
        for pack in (pack_one, pack_two):
            piece = pack.shape[0] // (4 * ring)
            for half, sources in ((core, mine), (1 - core, other)):
                at = pl.multiple_of((half * 2 * ring + (plane ^ step)) * piece, piece)
                pack[pl.ds(at, piece), :] = sources[step][start : start + piece, :]
            start += piece


def middle_kernel(
    cell, ring, carry, finish,
    lengths, x, q, state, peak, stream, cotangent, w_all, bias_v, wo_in, bias_o, gain_one,
    shift_one, w1_in, bias_1, w2_in, bias_2, gain_two, shift_two, *refs,
):
    count = ring - 1 if ring > 2 else 0
    before, refs = refs[:count], refs[count:]
    if carry:
        dwo_in, dw1_in, dw2_in, vec_in = refs[:4]
        refs = refs[4:]
    do_outs, dot_outs, refs = refs[:ring], refs[ring : 2 * ring], refs[2 * ring :]
    result_out, k_out, v_out, kept_out, x_out, first_out, vec_out = refs[:7]
    refs = refs[7:]
    if carry:
        wo, w1, w2 = wo_in, w1_in, w2_in
    else:
        wo, w1, w2 = refs[:3]
        refs = refs[3:]
        wo[...] = spread_rows(wo_in[...].astype(BF))
        w1[...] = w1_in[...].astype(BF)
        w2[...] = w2_in[...].astype(BF)
    if finish:
        keep_out, give_out = refs[:2]
        refs = refs[2:]
    else:
        dwo_out, dw1_out, dw2_out = refs[:3]
        refs = refs[3:]
    scales, refs = refs[:ring], refs[ring:]
    (
        attended_wide, attended_low, normed_low, active_low, hidden_low, branch_low, attn_low,
        unit_one, inverse_one, narrow_b, wide_b, acc, *pack_ref,
    ) = refs
    rows, width = stream.shape
    x_out[...] = x[:rows, :]
    hidden = w1.shape[1]
    length = lengths[cell]
    first_place = owner_of(ring - 1, ring) * rows
    project_keys(x[:rows, :], w_all, bias_v[...], first_place, length, k_out, v_out)
    for head in range(HEADS):
        cols = head_cols(head)
        total, own = attend(
            q[:, cols], k_out[:, cols], v_out[:, cols], kept_out.at[kept_rows(head, rows)]
        )
        top = jnp.maximum(peak[:, cols], own)
        old_scale, own_scale = jnp.exp(peak[:, cols] - top), jnp.exp(own - top)
        both = state[:, cols] * old_scale + total * own_scale
        inverse = inverse_of(both[:, HEAD_DIM : HEAD_DIM + 1])
        attended = both * inverse
        attended_wide[:, cols] = attended
        attended_low[:, cols] = attended.astype(BF)
        scales[ring - 1][:, cols] = own_scale * inverse
        if ring == 2:
            scales[0][:, cols] = old_scale * inverse
        else:
            for block in range(ring - 1):
                scales[block][:, cols] = jnp.exp(before[block][:, cols] - top) * inverse

    my_place = lax.axis_index("seq") * rows

    valid = jnp.where(row_of((rows, SLOT)) + my_place < length, 1.0, 0.0)
    valid = jnp.concatenate([valid] * (width // SLOT), axis=1)

    def add(slot, matrix):
        acc[slot] = eight_sum(matrix)

    attn_out = nn(attended_low[...], wo[...]) + bias_o[...]
    unit, inverse = norm_parts(stream[...] + attn_out)
    unit_one[...] = unit
    inverse_one[...] = jnp.broadcast_to(inverse, (rows, SLOT))
    normed = unit * gain_one[...] + shift_one[...]
    narrow_b[...] = normed
    normed_low[...] = normed.astype(BF)
    add(8, stream[...] * stream[...] * valid)
    add(9, attn_out * attn_out * valid)

    active, slope = gelu_parts(nn(normed_low[...], w1[...]) + bias_1[...])
    active_low[...] = active.astype(BF)
    wide_b[...] = slope

    branch = nn(active_low[...], w2[...]) + bias_2[...]
    unit, inverse = norm_parts(narrow_b[...] + branch)
    result_out[...] = unit * gain_two[...] + shift_two[...]
    grad_result = cotangent[...] * valid
    grad_second, product = norm_back(grad_result, gain_two[...], unit, inverse)
    narrow_b[...] = grad_second
    branch_bf = grad_second.astype(BF)
    branch_low[...] = branch_bf
    add(0, product)
    add(1, grad_result)
    add(10, branch * branch * valid)

    hidden_bf = (nt(branch_low[...], w2[...]) * wide_b[...]).astype(BF)
    hidden_low[...] = hidden_bf

    grad_normed = narrow_b[...] + nt(hidden_low[...], w1[...])
    unit = unit_one[...]
    grad_first, product = norm_back(grad_normed, gain_one[...], unit, inverse_one[:, :1])
    first_out[...] = grad_first
    attn_bf = grad_first.astype(BF)
    attn_low[...] = attn_bf
    add(5, product)
    add(6, grad_normed)

    do_wide = nt(attn_low[...], wo[...]).astype(BF).astype(F32)
    for head in range(HEADS):
        cols = head_cols(head)
        do_head = do_wide[:, cols]
        row_dot = jnp.sum(do_head * attended_wide[:, cols], axis=1, keepdims=True)
        for scale, do_out, dot_out in zip(scales, do_outs, dot_outs):
            factor = scale[:, cols]
            do_out[:, cols] = (do_head * factor).astype(BF)
            dot_out[:, cols] = row_dot * factor

    ones = jnp.ones((8, rows), BF)
    hidden_sum = nn(ones, hidden_low[...])[0:1]
    known = {
        2: nn(ones, branch_low[...])[0:1],
        3: hidden_sum[:, :width],
        4: hidden_sum[:, width:],
        7: nn(ones, attn_low[...])[0:1],
        11: jnp.full((1, width), jnp.clip(length - my_place, 0, rows).astype(F32)),
    }
    sums = [
        known[slot] if slot in known else jnp.sum(acc[slot], axis=0, keepdims=True)
        for slot in range(12)
    ]
    vec = jnp.concatenate(sums + [jnp.zeros((4, width), F32)], axis=0)
    vec_out[...] = vec + vec_in[...] if carry else vec

    dwo = tn(attn_low[...], attended_low[...])
    dw1 = tn(normed_low[...], hidden_low[...])
    dw2 = tn(branch_low[...], active_low[...])
    if carry:
        dwo += dwo_in[...]
        dw1 += dw1_in[...]
        dw2 += dw2_in[...]
    if not finish:
        dwo_out[...] = dwo
        dw1_out[...] = dw1
        dw2_out[...] = dw2
        return
    (pack,) = pack_ref
    pack[:width, :] = joined(dwo).astype(BF)
    pack[width : 2 * width, :] = dw1[:, :width].astype(BF)
    pack[2 * width : 3 * width, :] = dw1[:, width:].astype(BF)
    for at in range(0, hidden, width):
        pack[3 * width + at : 4 * width + at, :] = dw2[:, at : at + width].astype(BF)
    used = 3 * width + hidden
    if pack.shape[0] > used:
        pack[used:, :] = jnp.zeros((pack.shape[0] - used, width), BF)
    halve(pack, keep_out, give_out)


def head_grads(q, k, v, do, dot, kept):
    dots = jnp.concatenate([dot] * (kept.shape[1] // SLOT), axis=1)
    score_grad = (kept.astype(F32) * (nt(do, v) - dots)).astype(BF)
    return (
        nn(score_grad, k),
        tn(q[:, :HEAD_DIM], score_grad),
        tn(do[:, :HEAD_DIM], kept),
    )


def all_heads(q, k, v, do, dot, kept, low, put_query):
    rows = q.shape[0]
    for head in range(HEADS):
        cols = head_cols(head)
        dq, dk, dv = head_grads(
            q[:, cols], k[:, cols], v[:, cols], do[:, cols], dot[:, cols],
            kept[kept_rows(head, rows), :],
        )
        put_query(cols, dq)
        low[head * HEAD_DIM : (head + 1) * HEAD_DIM, :] = dk.astype(BF)
        at = (HEADS + head) * HEAD_DIM
        low[at : at + HEAD_DIM, :] = dv.astype(BF)


def masked_sum(carrier, cell, grad_bf):
    mask = mask_of(carrier, cell)
    picked = jnp.broadcast_to(mask, (8, mask.shape[1])).astype(BF)
    return nn(picked, grad_bf)[0:1]


def value_sums(low):
    half = low.shape[0] // 2
    sums = jnp.sum(low[half:, :].astype(F32), axis=1, keepdims=True)
    return jnp.broadcast_to(sums, (half, SLOT))


def block_kernel(cell, carry_dq, carry, sent, carrier, q, do, dot, k, v, kept, w_kv, *refs):
    if carry_dq:
        dq_in, refs = refs[0], refs[1:]
    if carry:
        (dw_in, sum_in, vec_in), refs = refs[:3], refs[3:]
    dq_out, dx_out, dw_out, sum_out, vec_out, low = refs

    def put_query(cols, dq):
        dq_out[:, cols] = dq + dq_in[:, cols] if carry_dq else dq

    all_heads(q, k, v, do, dot, kept, low, put_query)
    x = sent[: q.shape[0], :]
    dx_bf = jnp.transpose(nn(w_kv[...], low[...]).astype(BF))
    dx_out[...] = dx_bf
    dw = nn(low[...], x)
    dw_out[...] = dw + dw_in[...] if carry else dw
    sums = value_sums(low)
    sum_out[...] = sums + sum_in[...] if carry else sums
    vec_out[...] = vec_in[...] if carry else jnp.zeros_like(vec_out)
    vec_out[0:1, : x.shape[1]] += masked_sum(carrier[...], cell, dx_bf)


def last_kernel(
    cell, carry, finish,
    sent, carrier, q, do, dot, k, v, kept, w_all, w_kv, first, dq_in, dw_in, sum_in, vec_in, *refs
):
    if carry:
        dwq_in, refs = refs[0], refs[1:]
    if finish:
        vec_mid, dx_out, keep_out, give_out, low_q, low, pack = refs
    else:
        dx_out, dw_out, sum_out, vec_out, dwq_out, low_q, low = refs

    def put_query(cols, dq):
        low_q[:, cols] = ((dq + dq_in[:, cols]) * HEAD_DIM ** (-0.5)).astype(BF)

    all_heads(q, k, v, do, dot, kept, low, put_query)
    grads = first[...] + nt(low_q[...], w_all[:, :WIDE]) * HEAD_DIM**0.5
    grads += jnp.transpose(nn(w_kv[...], low[...]))
    dx_out[...] = grads
    width = grads.shape[1]
    x = sent[: q.shape[0], :]
    dwq = tn(x, low_q[...])
    dw = nn(low[...], x) + dw_in[...]
    sum_q = jnp.sum(low_q[...].astype(F32), axis=0, keepdims=True) + vec_in[1:2, :]
    sum_v = value_sums(low) + sum_in[...]
    sum_mask = masked_sum(carrier[...], cell, grads.astype(BF)) + vec_in[0:1, :width]
    if carry:
        dwq += dwq_in[...]
    if not finish:
        dwq_out[...] = dwq
        dw_out[...] = dw
        sum_out[...] = sum_v
        vec_out[...] = jnp.zeros_like(vec_out)
        vec_out[0:1, :width] = sum_mask
        vec_out[1:2, :] = sum_q
        return
    pack[:width, :] = joined(dwq).astype(BF)
    pack[width : 3 * width, :] = dw.astype(BF)
    rows = jnp.concatenate(
        [
            vec_mid[:12, :],
            joined(sum_q),
            jnp.transpose(sum_v)[0:1, :],
            sum_mask,
            jnp.zeros((1, width), F32),
        ],
        axis=0,
    )
    high = rows.astype(BF)
    pack[3 * width : 3 * width + 16, :] = high
    pack[3 * width + 16 : 3 * width + 32, :] = (rows - high.astype(F32)).astype(BF)
    used = 3 * width + 32
    if pack.shape[0] > used:
        pack[used:, :] = jnp.zeros((pack.shape[0] - used, width), BF)
    halve(pack, keep_out, give_out)


def unpack_kernel(ring, *refs):
    mine, other, refs = refs[: 2 * ring], refs[2 * ring : 4 * ring], refs[4 * ring :]
    dwo_out, dw1_out, dw2_out, dwq_out, dwk_out, dwv_out = refs[:6]
    outs, pack_one, pack = refs[6:-2], refs[-2], refs[-1]
    place_pieces(ring, mine, other, pack_one, pack)
    width = pack.shape[1]
    dwo_out[...] = jnp.transpose(pack_one[:width, :]).astype(F32)
    dw1_out[:, :width] = pack_one[width : 2 * width, :].astype(F32)
    dw1_out[:, width:] = pack_one[2 * width : 3 * width, :].astype(F32)
    for at in range(0, dw2_out.shape[0], width):
        dw2_out[at : at + width, :] = jnp.transpose(
            pack_one[3 * width + at : 4 * width + at, :]
        ).astype(F32)
    dwq_out[...] = pack[:width, :].astype(F32)
    dwk_out[...] = jnp.transpose(pack[width : 2 * width, :]).astype(F32)
    dwv_out[...] = jnp.transpose(pack[2 * width : 3 * width, :]).astype(F32)
    vec = pack[3 * width : 3 * width + 16, :].astype(F32)
    vec += pack[3 * width + 16 : 3 * width + 32, :].astype(F32)
    for out, row in zip(outs, (0, 1, 2, (3, 4), 5, 6, 7, 12, 13, 14)):
        if isinstance(row, tuple):
            out[:, :width] = vec[row[0] : row[0] + 1]
            out[:, width:] = vec[row[1] : row[1] + 1]
        else:
            out[...] = vec[row : row + 1]
    squares = jnp.sum(vec[8:16], axis=1, keepdims=True)
    count = vec[11:12, 0:1]
    means = jnp.sqrt(squares / (count * width))
    lane = lane_of((1, 3))
    outs[10][...] = jnp.where(
        lane == 0, means[0:1], jnp.where(lane == 1, means[1:2], means[2:3])
    )


def finish_kernel(cells, carrier, *refs):
    local, received, out = refs[:cells], refs[cells:-1], refs[-1]
    rows, count = local[0].shape[0], len(received) // cells
    for cell in range(cells):
        grads = local[cell][...]
        for piece in received[cell * count : (cell + 1) * count]:
            grads += piece[...].astype(F32)
        mask = jnp.broadcast_to(mask_of(carrier[...], cell), (8, rows))
        out[cell] = jnp.where(jnp.transpose(mask)[:, :1] == 1.0, 0.0, grads)


def call(kernel, ins, outs, scratch=(), flops=0):
    moved = sum(a.size * a.dtype.itemsize for a in ins) + sum(
        s.size * s.dtype.itemsize for s in outs
    )
    vmem = pl.BlockSpec(memory_space=pltpu.VMEM)
    smem = pl.BlockSpec(memory_space=pltpu.SMEM)
    return pl.pallas_call(
        kernel,
        in_specs=[smem if a.ndim == 1 else vmem for a in ins],
        out_specs=[vmem] * len(outs),
        out_shape=outs,
        scratch_shapes=list(scratch),
        compiler_params=pltpu.CompilerParams(vmem_limit_bytes=VMEM_LIMIT),
        cost_estimate=pl.CostEstimate(
            flops=flops, bytes_accessed=moved if flops != 1 else 1, transcendentals=0
        ),
    )(*ins)


def send(block, distance, ring):
    route = [(i, (i + distance) % ring) for i in range(ring)]
    return lax.ppermute(block, "seq", route)


NEAR = ("x", "core", "seq")
PLANE = ("x", "seq")


def swap(block, axes, step):
    return lax.ppermute(block, axes, [(i, i ^ step) for i in range(lax.axis_size(axes))])


def tree_sum(blocks):
    blocks = [block.astype(F32) for block in blocks]
    while len(blocks) > 1:
        blocks = [a + b for a, b in zip(blocks[::2], blocks[1::2])]
    return blocks[0].astype(BF)


def swaps(blocks, axes):
    return {step: swap(blocks[step], axes, step) for step in sorted(blocks, reverse=True)}


def sum_steps(own, got):
    return tree_sum([own] + [got[step] for step in sorted(got)])


def divide(keep, received, ring):
    half, width = keep.shape
    piece = jax.ShapeDtypeStruct((half // (2 * ring), width), BF)
    own, *pieces = call(
        functools.partial(divide_kernel, ring), [keep, received], [piece] * (2 * ring)
    )
    return own, dict(enumerate(pieces, 1))


def to_all(block, axes):
    return swaps({step: block for step in range(1, lax.axis_size(axes))}, axes)


def padded(rows, pieces):
    piece = -(-rows // pieces)
    return -(-piece // 16) * 16 * pieces


def body(
    tokens, masked, lengths, cotangent, mask_embed, query_weight, query_bias, key_weight,
    value_weight, value_bias, out_weight, out_bias, gain_one, shift_one, expand_weight,
    expand_bias, reduce_weight, reduce_bias, gain_two, shift_two,
):
    cells, rows, width = tokens.shape
    hidden = expand_weight.shape[1]
    ring = lax.axis_size("seq")

    def row(vector):
        return vector.reshape(1, -1)

    shape = jax.ShapeDtypeStruct
    low_wide, full_wide = shape((rows, WIDE), BF), shape((rows, WIDE), F32)
    low_narrow, full_narrow = shape((rows, width), BF), shape((rows, width), F32)
    weights = shape((HEADS * rows, rows), BF)
    score_flops = 2 * rows * rows * HEADS * 256

    stream, x_moved, x_low = [], [], []
    vmem = pl.BlockSpec(memory_space=pltpu.VMEM)
    masks = masked
    for cell in range(cells):
        carry = cell == cells - 1
        outs = [full_narrow, low_narrow] + [shape((rows + MASK_ROWS, width), BF)] * carry
        made = pl.pallas_call(
            functools.partial(select_kernel, cell, carry),
            in_specs=[pl.BlockSpec(memory_space=pltpu.HBM)] * 3,
            out_specs=[vmem] * len(outs),
            out_shape=outs,
            scratch_shapes=[
                pltpu.VMEM((rows, width), F32),
                pltpu.VMEM((cells, rows), jnp.int32),
                pltpu.VMEM((1, width), F32),
                pltpu.SemaphoreType.DMA((3,)),
            ],
            compiler_params=pltpu.CompilerParams(vmem_limit_bytes=VMEM_LIMIT),
        )(
            *[
                pltpu.with_memory_space_constraint(a, pltpu.HBM)
                for a in (tokens, masks, row(mask_embed))
            ]
        )
        stream.append(made[0])
        x_low.append(made[1])
        x_moved.append([made[-1]])
        if cell == 0:
            x_moved[0] += [send(x_moved[0][0], t, ring) for t in range(1, ring)]
        masks, x_low[cell] = lax.optimization_barrier((masks, x_low[cell]))

    made = call(
        functools.partial(first_kernel, cells),
        [lengths]
        + x_low
        + [query_weight, key_weight, value_weight, row(query_bias), row(value_bias)],
        [low_wide, low_wide, low_wide, weights, full_wide, full_wide] * cells
        + [
            shape((width, 3 * WIDE), BF),
            shape((width, 2 * width), BF),
        ],
        flops=2 * cells * score_flops,
    )
    w_all, w_kv = made[-2:]
    wo, w1, w2 = out_weight, expand_weight, reduce_weight
    low_weights = [
        shape((WIDE, width), BF), shape((width, hidden), BF), shape((hidden, width), BF)
    ]
    bias_v = row(value_bias)
    for cell in range(1, cells):
        sent, w_all = lax.optimization_barrier((x_moved[cell][0], w_all))
        x_moved[cell] += [send(sent, t, ring) for t in range(1, ring)]
    carriers = list(x_moved[-1])
    keys, values, kept, queries, states, peaks = [], [], [], [], [], []
    for cell in range(cells):
        q, k, v, p, state, peak = made[6 * cell : 6 * cell + 6]
        queries.append(q)
        keys.append([k])
        values.append([v])
        kept.append([p])
        own_peaks = [peak]
        for t in range(1, ring - 1):
            k, v, p, own, state, peak = call(
                functools.partial(more_kernel, cell, t, ring),
                [lengths, x_moved[cell][t], q, state, peak, w_all, bias_v],
                [low_wide, low_wide, weights, full_wide, full_wide, full_wide],
                flops=2 * score_flops,
            )
            keys[cell].append(k)
            values[cell].append(v)
            kept[cell].append(p)
            own_peaks.append(own)
        states.append([state, peak])
        peaks.append(own_peaks if ring > 2 else [])

    one_rows = padded(3 * width + hidden, lax.axis_size(NEAR))
    results, firsts, grads_out = [], [], []
    carried, carried_back, received = [], [], []
    dq = [None] * cells

    def backward_of_blocks(cell):
        nonlocal carried_back
        partial = []
        for t in range(1, ring):
            ins = [
                x_moved[cell][t], carriers[t], queries[cell], *grads_out[cell][t],
                keys[cell][t], values[cell][t], kept[cell][t], w_kv,
            ]
            ins += ([dq[cell]] if t > 1 else []) + carried_back
            dq[cell], dx, *carried_back = call(
                functools.partial(block_kernel, cell, t > 1, bool(carried_back)),
                ins,
                [
                    full_wide,
                    low_narrow,
                    shape((2 * width, width), F32),
                    shape((width, SLOT), F32),
                    shape((8, WIDE), F32),
                ],
                [pltpu.VMEM((2 * width, rows), BF)],
                flops=5 * score_flops,
            )
            partial.append(dx)
        return partial

    def returned(partial):
        return [send(dx, -t, ring) for t, dx in enumerate(partial, 1)]

    for cell in range(cells):
        finish = cell == cells - 1
        if cell > 0:
            partial = backward_of_blocks(cell - 1)
            states[cell], partial = lax.optimization_barrier((states[cell], partial))
            received.append(returned(partial))
        outs = [low_wide] * ring + [full_wide] * ring
        outs += [full_narrow, low_wide, low_wide, weights, low_narrow, full_narrow]
        outs += [shape((16, width), F32)] + (low_weights if cell == 0 else [])
        if finish:
            outs += [shape((one_rows // 2, width), BF)] * 2
        else:
            outs += [shape((width, WIDE), F32)] + [shape((width, hidden), F32)] * 2
        scratch = [pltpu.VMEM((rows, WIDE), F32)] * ring + [
            pltpu.VMEM((rows, WIDE), F32),
            pltpu.VMEM((rows, WIDE), BF),
            pltpu.VMEM((rows, width), BF),
            pltpu.VMEM((rows, hidden), BF),
            pltpu.VMEM((rows, hidden), BF),
            pltpu.VMEM((rows, width), BF),
            pltpu.VMEM((rows, width), BF),
            pltpu.VMEM((rows, width), F32),
            pltpu.VMEM((rows, SLOT), F32),
            pltpu.VMEM((rows, width), F32),
            pltpu.VMEM((rows, hidden), F32),
            pltpu.VMEM((12, 8, width), F32),
        ]
        if finish:
            scratch.append(pltpu.VMEM((one_rows, width), BF))
        made = call(
            functools.partial(middle_kernel, cell, ring, bool(carried), finish),
            [
                lengths, x_moved[cell][ring - 1], queries[cell], *states[cell], stream[cell],
                cotangent[cell], w_all, bias_v, wo, row(out_bias), row(gain_one), row(shift_one),
                w1, row(expand_bias), w2, row(reduce_bias), row(gain_two), row(shift_two),
            ]
            + peaks[cell]
            + carried,
            outs,
            scratch,
            flops=7 * score_flops,
        )
        grads_out.append(list(zip(made[:ring], made[ring : 2 * ring])))
        made = made[ring:]
        result, k, v, p, x_moved[cell][ring - 1], first, vec_mid = made[ring : ring + 7]
        made = made[ring + 7 :]
        if cell == 0:
            wo, w1, w2 = made[:3]
            made = made[3:]
        results.append(result)
        keys[cell].append(k)
        values[cell].append(v)
        kept[cell].append(p)
        firsts.append(first)
        carried = list(made) + [vec_mid]
    keep, give = made
    received_one = swap(give, "core", 1)
    queries[-1], received = lax.optimization_barrier((queries[-1], received))
    partial = backward_of_blocks(cells - 1)
    own_one, pieces = divide(keep, received_one, ring)
    carried, partial, own_one, pieces = lax.optimization_barrier(
        (carried_back, partial, own_one, pieces)
    )
    got_one = swaps(pieces, PLANE)

    two_rows = padded(3 * width + 32, lax.axis_size(NEAR))
    local = []
    depth_steps = [1 << i for i in range(lax.axis_size("z").bit_length() - 1)]
    for cell in range(cells):
        finish = cell == cells - 1
        if finish:
            carried, got_one = lax.optimization_barrier((carried, got_one))
            own_one = sum_steps(own_one, got_one)
            got_one = swap(own_one, "z", depth_steps[0])
        ins = [
            x_moved[cell][0], carriers[0], queries[cell], *grads_out[cell][0],
            keys[cell][0], values[cell][0], kept[cell][0], w_all, w_kv, firsts[cell], dq[cell],
        ]
        outs = [full_narrow]
        scratch = [pltpu.VMEM((rows, WIDE), BF), pltpu.VMEM((2 * width, rows), BF)]
        if finish:
            outs += [shape((two_rows // 2, width), BF)] * 2
            scratch += [pltpu.VMEM((two_rows, width), BF)]
        else:
            outs += [shape((2 * width, width), F32), shape((width, SLOT), F32)]
            outs += [shape((8, WIDE), F32), shape((width, WIDE), F32)]
        made = call(
            functools.partial(last_kernel, cell, cell > 0, finish),
            ins + carried + ([vec_mid] if finish else []),
            outs,
            scratch,
            flops=1,
        )
        local.append(made[0])
        carried = list(made[1:])
    keep, give = carried
    give, got_one = lax.optimization_barrier((give, got_one))
    other = swap(give, "core", 1)
    for step in depth_steps[1:]:
        own_one = tree_sum([own_one, got_one])
        got_one = swap(own_one, "z", step)
    own, pieces = divide(keep, other, ring)
    got, got_one = lax.optimization_barrier((swaps(pieces, PLANE), got_one))
    own = sum_steps(own, got)
    own, partial = lax.optimization_barrier((own, partial))
    received.append(returned(partial))
    got, received = lax.optimization_barrier((to_all(own, "z"), received))
    own = sum_steps(own, got)
    own_one = tree_sum([own_one, got_one])
    own = jnp.concatenate([own_one, own], axis=0)
    tokens_grad = call(
        functools.partial(finish_kernel, cells),
        [carriers[0]] + local + sum(received, []),
        [shape((cells, rows, width), F32)],
    )[0]
    got = to_all(own, PLANE)
    result = jnp.stack(results)
    got[1], tokens_grad, result = lax.optimization_barrier((got[1], tokens_grad, result))
    mine = [own] + [got[step] for step in sorted(got)]
    other = [swap(piece, "core", 1) for piece in mine]

    vector = shape((1, width), F32)
    made = call(
        functools.partial(unpack_kernel, ring),
        mine + other,
        [shape((width, width), F32), shape((width, hidden), F32), shape((hidden, width), F32)]
        + [shape((width, width), F32)] * 3
        + [vector] * 3
        + [shape((1, hidden), F32)]
        + [vector] * 6
        + [shape((1, 3), F32)],
        [pltpu.VMEM((one_rows, width), BF), pltpu.VMEM((two_rows, width), BF)],
    )
    dwo, dw1, dw2, dwq, dwk, dwv = made[:6]
    (
        gain_two_grad, shift_two_grad, bias_2_grad, bias_1_grad, gain_one_grad, shift_one_grad,
        bias_o_grad, bias_q_grad, bias_v_grad, mask_embed_grad, root_means,
    ) = [a.reshape(-1) for a in made[6:]]

    return (
        result,
        tokens_grad,
        mask_embed_grad,
        dwq,
        bias_q_grad,
        dwk,
        dwv,
        bias_v_grad,
        dwo,
        bias_o_grad,
        gain_one_grad,
        shift_one_grad,
        dw1,
        bias_1_grad,
        dw2,
        bias_2_grad,
        gain_two_grad,
        shift_two_grad,
        root_means,
    )


def solution(mesh):
    dp, seq = mesh.shape["dp"], mesh.shape["seq"]
    cut = jax.sharding.Mesh(mesh.devices.reshape(dp // 4, 2, 2, seq), ("z",) + NEAR)
    dp = ("z", "x", "core")
    split = P(dp, "seq", None)
    return jax.shard_map(
        body,
        mesh=cut,
        in_specs=(split, P(dp, "seq"), P(dp), split) + (P(),) * 16,
        out_specs=(split, split) + (P(),) * 17,
        check_vma=False,
    )
```
